32 devices in a mesh: ctx: 8 (over y, x, core), fsdp: 4 (over z).
Axes of the slice: x: 2, y: 2, z: 4, core: 2. Of those that a mesh axis runs over, the one named last changes fastest.
Arguments:
- acts: bfloat16 [4, 2048, 1024], P('fsdp', 'ctx'), may hold values from -6 to 6
- cotangent: bfloat16 [4, 2048, 1024], P('fsdp', 'ctx'), may hold values from -6 to 6
- pair_slots: int32 [8], replicated, may hold values from 0 to 7, as said below
- segments: int32 [4, 2048], P('fsdp'), may hold values from 0 to 2, as said below
- attn_gain: bfloat16 [2, 1024], P(None, 'fsdp'), may hold values from 0.099609375 to 1.8984375
- attn_shift: bfloat16 [2, 1024], P(None, 'fsdp'), may hold values from -3 to 3
- qkv_weight: bfloat16 [2, 1024, 3072], P(None, 'fsdp'), may hold values from -0.1875 to 0.1875
- qkv_bias: bfloat16 [2, 3072], P(None, 'fsdp'), may hold values from -2 to 2
- proj_weight: bfloat16 [2, 1024, 1024], P(None, 'fsdp'), may hold values from -3 to 3
- proj_bias: bfloat16 [2, 1024], P(None, 'fsdp'), may hold values from -2 to 2
- mlp_gain: bfloat16 [2, 1024], P(None, 'fsdp'), may hold values from 0.099609375 to 1.8984375
- mlp_shift: bfloat16 [2, 1024], P(None, 'fsdp'), may hold values from -3 to 3
- fc_weight: bfloat16 [2, 1024, 4096], P(None, 'fsdp'), may hold values from -0.1875 to 0.1875
- fc_bias: bfloat16 [2, 4096], P(None, 'fsdp'), may hold values from -2 to 2
- out_weight: bfloat16 [2, 4096, 1024], P(None, 'fsdp'), may hold values from -0.09375 to 0.09375
- out_bias: bfloat16 [2, 1024], P(None, 'fsdp'), may hold values from -2 to 2
- final_gain: bfloat16 [1024], P('fsdp'), may hold values from 0.099609375 to 1.8984375
- final_shift: bfloat16 [1024], P('fsdp'), may hold values from -3 to 3
Outputs:
- activations: bfloat16 [4, 2048, 1024], P('fsdp', 'ctx')
- input_grad: bfloat16 [4, 2048, 1024], P('fsdp', 'ctx')
- attn_gain_grad: float32 [2, 1024], P(None, 'fsdp')
- attn_shift_grad: float32 [2, 1024], P(None, 'fsdp')
- qkv_weight_grad: float32 [2, 1024, 3072], P(None, 'fsdp')
- qkv_bias_grad: float32 [2, 3072], P(None, 'fsdp')
- proj_weight_grad: float32 [2, 1024, 1024], P(None, 'fsdp')
- proj_bias_grad: float32 [2, 1024], P(None, 'fsdp')
- mlp_gain_grad: float32 [2, 1024], P(None, 'fsdp')
- mlp_shift_grad: float32 [2, 1024], P(None, 'fsdp')
- fc_weight_grad: float32 [2, 1024, 4096], P(None, 'fsdp')
- fc_bias_grad: float32 [2, 4096], P(None, 'fsdp')
- out_weight_grad: float32 [2, 4096, 1024], P(None, 'fsdp')
- out_bias_grad: float32 [2, 1024], P(None, 'fsdp')
- final_gain_grad: float32 [1024], P('fsdp')
- final_shift_grad: float32 [1024], P('fsdp')
The draws below stay inside these ranges and needn't reach their ends.
Inputs may be any that keep to these rules, and one draw needn't show every extreme that they name: Each number once; index i of ctx holds the pieces pair_slots[i] and 15 - pair_slots[i] of its pack's sequence, each of 128 tokens, the lower piece in the first half of its rows. `segments`: three documents a pack; taken in the order of positions the numbers never fall; document 0 starts at position 0 and takes at least half of the pack.
All inputs are finite; a program needn't handle non-finite values.
Results may differ from the reference program's by a relative error of at most 0.018.
Values may be sent and summed in bfloat16 or wider, within the bound.
A program may use at most 320 MiB of HBM per device.

```python
import jax
import jax.numpy as jnp
from jax import lax

D = 1024
HEADS = 16
HEAD_DIM = 64
FF = 4096
LAYERS = 2
TOK_DEV = 256
CTX_LEN = 2048
GROUPS = 4
N_CTX = 8


def pair_order(key):
    return jax.random.permutation(key, N_CTX).astype(jnp.int32)


def draw_pair_slots(key, part):
    shared = pair_order(key)
    return shared


def draw_segments(key, part):
    shared = pair_order(key)
    key = jax.random.fold_in(key, 7)
    first_key, second_key = jax.random.split(key)
    seq_len = TOK_DEV * N_CTX
    cut_one = jax.random.randint(first_key, (GROUPS, 1), seq_len // 2, seq_len - seq_len // 8 + 1).astype(jnp.int32)
    cut_two = jax.random.randint(second_key, (GROUPS, 1), cut_one + 1, seq_len).astype(jnp.int32)
    indices = jnp.arange(seq_len, dtype=jnp.int32)
    owner = indices // TOK_DEV
    within = indices % TOK_DEV
    half_len = TOK_DEV // 2
    partner = shared[owner]
    piece = jnp.where(within < half_len, partner, 2 * N_CTX - 1 - partner)
    position = (piece * half_len + within % half_len)[None, :]
    return ((position >= cut_one).astype(jnp.int32) + (position >= cut_two).astype(jnp.int32)).astype(jnp.int32)


def block_levels(rng, extent, cuts, low, largest):
    loudness = 1.0
    for axis_at, parts in cuts:
        draws = jax.random.uniform(jax.random.fold_in(jax.random.fold_in(rng, 6), axis_at), (parts,), jnp.float32, low / len(cuts), largest / len(cuts))
        loudness = loudness * jnp.repeat(jnp.exp(draws), extent[axis_at] // parts).reshape((-1,) + (1,) * (len(extent) - 1 - axis_at))
    return loudness


def noise(rng, extent, scale, reach, shards=(), held_as=jnp.bfloat16):
    loudness = block_levels(rng, extent, shards, -0.22, 0.18) if shards else 1.0
    entries = jax.random.normal(rng, extent, jnp.float32) * scale * loudness
    return jnp.minimum(jnp.maximum(entries, -reach), reach).astype(held_as)


def setup_inputs(seed: int = 0) -> dict:
    seeds = jax.random.split(jax.random.key(seed), 19)
    acts = noise(seeds[0], (GROUPS, CTX_LEN, D), 1.0, 6.0, ((0, 4), (1, 8)))
    cotangent = noise(seeds[1], (GROUPS, CTX_LEN, D), 1.0, 6.0, ((0, 4), (1, 8)))
    pair_slots = draw_pair_slots(jax.random.fold_in(seeds[18], 71), 0)
    segments = draw_segments(jax.random.fold_in(seeds[18], 71), 0)
    attn_gain = jnp.clip(1.0 + 0.18 * jax.random.normal(seeds[4], (LAYERS, D), jnp.float32), 0.099609375, 1.8984375).astype(jnp.bfloat16)
    attn_shift = noise(seeds[5], (LAYERS, D), 0.5, 3.0, ((1, 4),))
    qkv_weight = noise(seeds[6], (LAYERS, D, 3 * D), D ** -0.5, 0.1875, ((1, 4),))
    qkv_bias = noise(seeds[7], (LAYERS, 3 * D), 0.3, 2.0, ((1, 4),))
    proj_weight = noise(seeds[8], (LAYERS, D, D), (max(D // 256, 2)) ** -0.5, 3.0, ((1, 4),))
    proj_bias = noise(seeds[9], (LAYERS, D), 0.3, 2.0, ((1, 4),))
    mlp_gain = jnp.clip(1.0 + 0.18 * jax.random.normal(seeds[10], (LAYERS, D), jnp.float32), 0.099609375, 1.8984375).astype(jnp.bfloat16)
    mlp_shift = noise(seeds[11], (LAYERS, D), 0.5, 3.0, ((1, 4),))
    fc_weight = noise(seeds[12], (LAYERS, D, FF), D ** -0.5, 0.1875, ((1, 4),))
    fc_bias = noise(seeds[13], (LAYERS, FF), 0.3, 2.0, ((1, 4),))
    out_weight = noise(seeds[14], (LAYERS, FF, D), FF ** -0.5, 0.09375, ((1, 4),))
    out_bias = noise(seeds[15], (LAYERS, D), 0.3, 2.0, ((1, 4),))
    final_gain = jnp.clip(1.0 + 0.18 * jax.random.normal(seeds[16], (D,), jnp.float32), 0.099609375, 1.8984375).astype(jnp.bfloat16)
    final_shift = noise(seeds[17], (D,), 0.5, 3.0, ((0, 4),))
    return dict(acts=acts, cotangent=cotangent, pair_slots=pair_slots, segments=segments, attn_gain=attn_gain, attn_shift=attn_shift, qkv_weight=qkv_weight, qkv_bias=qkv_bias, proj_weight=proj_weight, proj_bias=proj_bias, mlp_gain=mlp_gain, mlp_shift=mlp_shift, fc_weight=fc_weight, fc_bias=fc_bias, out_weight=out_weight, out_bias=out_bias, final_gain=final_gain, final_shift=final_shift)


EPS = 1e-05
NEG = -1e+30
HIGH = lax.Precision.HIGHEST

@jax.custom_vjp
def low(v):
    return lax.optimization_barrier(v.astype(jnp.bfloat16)).astype(jnp.float32)

@jax.custom_vjp
def low_back(v):
    return v

def low_keep(v):
    return (low(v), None)

def low_pass(kept, grad):
    return (grad,)

def back_keep(v):
    return (v, None)

def back_low(kept, grad):
    return (low(grad),)
low.defvjp(low_keep, low_pass)
low_back.defvjp(back_keep, back_low)

def layer_norm(values, gain, shift):
    center = values - lax.optimization_barrier(jnp.mean(values, axis=-1, keepdims=True))
    spread = lax.optimization_barrier(jnp.mean(center * center, axis=-1, keepdims=True))
    return center * lax.rsqrt(spread + EPS) * gain + shift

def matmul(left, right):
    return jnp.dot(left, right, precision=HIGH, preferred_element_type=jnp.float32)

def seq_positions(pair_slots):
    indices = jnp.arange(TOK_DEV * N_CTX, dtype=jnp.int32)
    owner = indices // TOK_DEV
    within = indices % TOK_DEV
    half_len = TOK_DEV // 2
    partner = pair_slots[owner].astype(jnp.int32)
    piece = jnp.where(within < half_len, partner, 2 * N_CTX - 1 - partner)
    return (piece * half_len + within % half_len).astype(jnp.int32)

def attention(queries, key_rows, values, positions, seg_ids):
    all_rows = positions.shape[0]
    block_rows = min(512, all_rows)
    num_blocks = all_rows // block_rows
    score_scale = HEAD_DIM ** (-0.5)

    def one_block(entry):
        query_blk, query_pos, query_seg = entry
        scores = jnp.einsum('qhd,khd->hqk', query_blk, key_rows, precision=HIGH) * score_scale
        visible = (query_seg[:, None] == seg_ids[None, :]) & (positions[None, :] <= query_pos[:, None])
        scores = low_back(jnp.where(visible[None], scores, NEG))
        weights = jax.nn.softmax(scores, axis=-1)
        return jnp.einsum('hqk,khd->qhd', low(weights), values, precision=HIGH)
    outputs = lax.map(jax.checkpoint(one_block), (queries.reshape(num_blocks, block_rows, HEADS, HEAD_DIM), positions.reshape(num_blocks, block_rows), seg_ids.reshape(num_blocks, block_rows)))
    return outputs.reshape(all_rows, HEADS * HEAD_DIM)

def block_forward(hidden, params, positions, seg_ids):
    gain_one, shift_one, w_qkv, b_qkv, w_proj, b_proj, gain_two, shift_two, w_fc, b_fc, w_out, b_out = params
    normed = low(layer_norm(hidden, gain_one, shift_one))
    packed = low(low_back(matmul(normed, w_qkv) + b_qkv))
    queries = packed[:, :D].reshape(-1, HEADS, HEAD_DIM)
    key_rows = packed[:, D:2 * D].reshape(-1, HEADS, HEAD_DIM)
    values = packed[:, 2 * D:].reshape(-1, HEADS, HEAD_DIM)
    mixed = low(low_back(attention(queries, key_rows, values, positions, seg_ids)))
    middle = hidden + low_back(matmul(mixed, w_proj) + b_proj)
    normed_two = low(layer_norm(middle, gain_two, shift_two))
    pre_act = low_back(matmul(normed_two, w_fc) + b_fc)
    activated = low(jax.nn.gelu(pre_act, approximate=True))
    return middle + low_back(matmul(activated, w_out) + b_out)

def reference(acts, cotangent, pair_slots, segments, attn_gain, attn_shift, qkv_weight, qkv_bias, proj_weight, proj_bias, mlp_gain, mlp_shift, fc_weight, fc_bias, out_weight, out_bias, final_gain, final_shift):
    params = tuple((tensor.astype(jnp.float32) for tensor in (attn_gain, attn_shift, qkv_weight, qkv_bias, proj_weight, proj_bias, mlp_gain, mlp_shift, fc_weight, fc_bias, out_weight, out_bias, final_gain, final_shift)))
    positions = seq_positions(pair_slots)

    def one_group(running, group_data):
        group_acts, group_cot, group_seg = group_data

        def forward(weights, hidden):
            for layer_index in range(LAYERS):
                layer_params = tuple((tensor[layer_index] for tensor in weights[:12]))
                hidden = block_forward(hidden, layer_params, positions, group_seg)
            return layer_norm(hidden, weights[12], weights[13])
        result, pullback = jax.vjp(forward, params, group_acts.astype(jnp.float32))
        weight_grads, group_grad = pullback(group_cot.astype(jnp.float32))
        running = tuple((summed + update for summed, update in zip(running, weight_grads)))
        return (running, (result.astype(jnp.bfloat16), group_grad.astype(jnp.bfloat16)))
    initial = tuple((jnp.zeros(tensor.shape, jnp.float32) for tensor in params))
    gradients, (activations, input_grads) = lax.scan(one_group, initial, (acts, cotangent, segments))
    return (activations, input_grads, gradients[0], gradients[1], gradients[2], gradients[3], gradients[4], gradients[5], gradients[6], gradients[7], gradients[8], gradients[9], gradients[10], gradients[11], gradients[12], gradients[13])
```

```python
import collections
import functools
import itertools

import jax
import jax.numpy as jnp
from jax import lax
from jax.experimental import pallas as pl
from jax.experimental.pallas import tpu as pltpu
from jax.sharding import PartitionSpec as P

HEADS = 16
HEAD_DIM = 64
LAYERS = 2
EPS = 1e-05
NEG = -1e30
LOW = -1e29
F32 = jnp.float32
BF16 = jnp.bfloat16
VMEM_BYTES = 56 * 1024 * 1024

FIELDS = ("t", "d", "ff", "nf", "nc", "pr", "pc", "nq", "ncs", "ffn", "w", "hl", "rows", "half")
Dims = collections.namedtuple("Dims", FIELDS)


def dims_of(acts, fc_weight, nf, nc):
    t, d = acts.shape[1], acts.shape[2]
    ff = fc_weight.shape[2]
    pr, pc = d // nf, ff // nc
    return Dims(
        t=t, d=d, ff=ff, nf=nf, nc=nc, pr=pr, pc=pc, nq=3 * d // pc, ncs=d // pc, ffn=ff // nf,
        w=d // nc, hl=HEADS // nc, rows=t * nc, half=t // 2,
    )


SMALL = (("g1", 1), ("s1", 1), ("bq", 3), ("bp", 1), ("g2", 1), ("s2", 1), ("bf", 4), ("bo", 1))


def small_offsets(dm):
    table, at = {}, 0
    for layer in range(LAYERS):
        for name, _ in SMALL:
            size = {"bq": 3 * dm.pr, "bf": dm.ffn}.get(name, dm.pr)
            table[name + str(layer)] = (at, size)
            at += size
    for name in ("gf", "sf"):
        table[name] = (at, dm.pr)
        at += dm.pr
    return table, at


def send_blocks(dm, at, shape):
    return Move(
        shape, BF16,
        [([(None, Local(at), (j,))], ("ctx", j) if j else None, (j,)) for j in range(dm.nc)],
    )


def mult(value, by):
    return pl.multiple_of(value, by)


def nn(a, b):
    return lax.dot_general(a, b, (((1,), (0,)), ((), ())), preferred_element_type=F32)


def nt(a, b):
    return lax.dot_general(a, b, (((1,), (1,)), ((), ())), preferred_element_type=F32)


def tn(a, b):
    return lax.dot_general(a, b, (((0,), (0,)), ((), ())), preferred_element_type=F32)


def col_sum(v):
    return jnp.sum(v.astype(F32), axis=0, keepdims=True)


def small_vec(dm, small_ref, name):
    at, size = small_offsets(dm)[0][name]
    return jnp.concatenate([small_ref[g : g + 1, at : at + size] for g in range(dm.nf)], axis=1)


def norm_parts(v):
    center = v - jnp.mean(v, axis=-1, keepdims=True)
    scale = lax.rsqrt(jnp.mean(center * center, axis=-1, keepdims=True) + EPS)
    return center * scale, scale


def norm(v, gain, shift):
    return norm_parts(v)[0] * gain + shift


def norm_back(v, gain, dy):
    xh, scale = norm_parts(v)
    e = dy * gain
    dv = scale * (
        e - jnp.mean(e, axis=-1, keepdims=True) - xh * jnp.mean(e * xh, axis=-1, keepdims=True)
    )
    return dv, col_sum(dy * xh), col_sum(dy)


K0 = 0.7978845608028654
K1 = 0.044715


def gelu(u):
    return 0.5 * u * (1.0 + jnp.tanh(K0 * (u + K1 * u * u * u)))


def gelu_slope(u):
    th = jnp.tanh(K0 * (u + K1 * u * u * u))
    return 0.5 * (1.0 + th) + 0.5 * u * (1.0 - th * th) * (K0 * (1.0 + 3.0 * K1 * u * u))


class Local:
    def __init__(self, at):
        self.at = at


class Move:
    def __init__(self, shape, dtype, parts):
        self.shape, self.dtype, self.parts = shape, dtype, parts
        self.result = None

    def inside(self):
        return any(
            isinstance(src, Local) or (isinstance(src, Move) and src.result is None)
            for sources, _, _ in self.parts
            for _, src, _ in sources
        )


def whole(array, route):
    return Move(array.shape, array.dtype, [([(None, array, None)], route, None)])


def at_of(ref, index):
    return ref if index is None else ref.at[index() if callable(index) else index]


def run(dm, body, operands, outs, scratch, flops, grid=None, in_specs=None, out_specs=None, alias=None,
        moves=(), ids=None):
    places = {"v": pltpu.VMEM, "s": pltpu.SMEM, "a": pl.ANY}
    specs = list(in_specs or [pl.BlockSpec(memory_space=places[p]) for _, p in operands])
    arrays = [a for a, _ in operands]
    outs = list(outs)
    out_specs = list(out_specs or [pl.BlockSpec(memory_space=pltpu.VMEM)] * len(outs))
    scratch = list(scratch)
    n_in, n_out, n_scratch = len(arrays), len(outs), len(scratch)
    bytes_moved = sum(a.size * a.dtype.itemsize for a in arrays)
    bytes_moved += sum(o.size * o.dtype.itemsize for o in outs)
    kwargs = {"grid": grid} if grid else {}
    params = {}
    kernel = body
    moves = list(moves)
    if moves:
        sent = {}
        for move in moves:
            for sources, _, _ in move.parts:
                for _, src, _ in sources:
                    array = src.result if isinstance(src, Move) else src
                    if array is not None and not isinstance(array, Local) and id(array) not in sent:
                        sent[id(array)] = n_in + len(sent)
                        arrays.append(array)
                        specs.append(pl.BlockSpec(memory_space=pl.ANY))
        total_in = len(arrays)
        outs += [sds(m.shape, m.dtype) for m in moves]
        out_specs += [pl.BlockSpec(memory_space=pl.ANY)] * len(moves)
        count = sum(len(m.parts) for m in moves)
        scratch += [pltpu.SemaphoreType.DMA((count,)), pltpu.SemaphoreType.DMA((count,))]
        pending = {id(m): n for n, m in enumerate(moves)}
        fixed = [m.result is None for m in moves]
        assert all(fixed)
        routes = sorted({route for m in moves for _, route, _ in m.parts if route is not None})

        def kernel(*refs):
            ins, out_refs = refs[:total_in], refs[total_in : total_in + len(outs)]
            rest = refs[total_in + len(outs) :]
            own_refs = ins[:n_in] + out_refs[:n_out] + rest[:n_scratch]
            send_sems, recv_sems = rest[n_scratch], rest[n_scratch + 1]
            c, f = lax.axis_index("ctx"), lax.axis_index("fsdp")

            def device(route, back=False):
                axis, by = route
                if axis == "ctx":
                    return (c ^ by, f)
                by = dm.nf - by if back else by
                return (c, lax.rem(f + by, dm.nf))

            barrier = pltpu.get_barrier_semaphore()
            for route in routes:
                pl.semaphore_signal(
                    barrier, inc=1, device_id=device(route, True), device_id_type=pl.DeviceIdType.MESH
                )
            pl.semaphore_wait(barrier, len(routes))

            def ref_of(src):
                if isinstance(src, Local):
                    return own_refs[src.at]
                if isinstance(src, Move):
                    if id(src) in pending:
                        return out_refs[n_out + pending[id(src)]]
                    src = src.result
                return ins[sent[id(src)]]

            first, copies = 0, []
            for n, move in enumerate(moves):
                row = []
                for sources, route, place in move.parts:
                    choices = []
                    for cond, src, index in sources:
                        if route is None:
                            choices.append((cond, pltpu.make_async_copy(
                                at_of(ref_of(src), index), at_of(out_refs[n_out + n], place),
                                recv_sems.at[first],
                            )))
                            continue
                        copy = pltpu.make_async_remote_copy(
                            src_ref=at_of(ref_of(src), index),
                            dst_ref=at_of(out_refs[n_out + n], place),
                            send_sem=send_sems.at[first],
                            recv_sem=recv_sems.at[first],
                            device_id=device(route),
                            device_id_type=pl.DeviceIdType.MESH,
                        )
                        choices.append((cond, copy))
                    row.append(choices)
                    first += 1
                copies.append(row)
            arrived = set()

            def wait(n):
                if n not in arrived:
                    arrived.add(n)
                    for choices, part in zip(copies[n], moves[n].parts):
                        copy = choices[0][1]
                        copy.wait() if part[1] is None else copy.wait_recv()

            def start(n):
                for sources, _, _ in moves[n].parts:
                    for _, src, _ in sources:
                        if isinstance(src, Move) and id(src) in pending:
                            wait(pending[id(src)])
                for choices in copies[n]:
                    for cond, copy in choices:
                        if cond is None:
                            copy.start()
                        else:
                            pl.when(cond())(copy.start)

            early = 0
            while early < len(moves) and not moves[early].inside():
                start(early)
                early += 1
            if body is not None:
                body(*own_refs)
            for n in range(early, len(moves)):
                start(n)
            for n in range(len(moves)):
                wait(n)
            for row, move in zip(copies, moves):
                for choices, part in zip(row, move.parts):
                    if part[1] is not None:
                        choices[0][1].wait_send()

        params = {"collective_id": next(ids), "has_side_effects": True}
    results = pl.pallas_call(
        kernel,
        out_shape=outs,
        in_specs=specs,
        out_specs=out_specs,
        scratch_shapes=scratch,
        input_output_aliases=alias or {},
        compiler_params=pltpu.CompilerParams(vmem_limit_bytes=VMEM_BYTES, **params),
        cost_estimate=pl.CostEstimate(flops=flops, bytes_accessed=bytes_moved, transcendentals=0),
        **kwargs,
    )(*arrays)
    for move, result in zip(moves, results[n_out:]):
        move.result = result
    return results[:n_out]


def sds(shape, dtype):
    return jax.ShapeDtypeStruct(shape, dtype)


class Pieces:
    def __init__(self, dm, layer, own, pieces, own_buf, piece_buf, sems, wanted):
        self.dm, self.wanted = dm, wanted
        self.own_copy = pltpu.make_async_copy(own.at[layer], own_buf, sems.at[dm.nc])
        self.copies = [
            pltpu.make_async_copy(pieces[j], piece_buf.at[j], sems.at[j]) for j in range(dm.nc)
        ]
        self.own, self.buf = own_buf, piece_buf

    def start(self):
        self.own_copy.start()
        for j in range(self.dm.nc):
            self.each(j, self.copies[j].start)

    def each(self, j, act):
        if self.wanted is None:
            act()
        else:
            pl.when(self.wanted(j))(act)

    def wait_own(self):
        self.own_copy.wait()

    def flat(self, j):
        return self.buf[j].reshape((self.dm.nf - 1) * self.dm.pr, self.dm.pc)


def piece_scratch(dm, own_shape):
    return [
        pltpu.VMEM(own_shape, BF16),
        pltpu.VMEM((dm.nc, dm.nf - 1, dm.pr, dm.pc), BF16),
        pltpu.SemaphoreType.DMA((dm.nc + 1,)),
    ]


def ring(dm, f, s):
    return lax.rem(f + (dm.nf - s), dm.nf)


def relative(dm, f, src, dst):
    for s in range(dm.nf):
        at = mult(ring(dm, f, s) * dm.pr, dm.pr)
        dst[:, s * dm.pr : (s + 1) * dm.pr] = src[:, pl.ds(at, dm.pr)]


def take_heads(dm, ref, base, i):
    if dm.w % 128 == 0:
        return ref[:, pl.ds(mult(base + i * dm.w, 128), dm.w)]
    per = 128 // dm.w
    wide = ref[:, pl.ds(mult(base + (i // per) * 128, 128), 128)]
    part = wide[:, : dm.w]
    for at in range(1, per):
        part = jnp.where(lax.rem(i, per) == at, wide[:, at * dm.w : (at + 1) * dm.w], part)
    return part


def put_heads(dm, ref, base, blocks, at, c):
    if dm.w % 128 == 0:
        for j in range(dm.nc):
            ref[:, pl.ds(mult(base + (c ^ j) * dm.w, 128), dm.w)] = blocks[j][:, at : at + dm.w]
        return
    for j in range(0, dm.nc, 2):
        one, two = blocks[j][:, at : at + dm.w], blocks[j + 1][:, at : at + dm.w]
        even = lax.rem(c, 2) == 0
        pair = jnp.concatenate([jnp.where(even, one, two), jnp.where(even, two, one)], axis=1)
        ref[:, pl.ds(mult(base + ((c ^ j) // 2) * 128, 128), 128)] = pair


def qkv_body(dm, layer, *refs):
    nc = dm.nc
    meta, h, small, own = refs[:4]
    pieces = refs[4 : 4 + nc]
    n1, xr, y, bias, blocks, own_buf, piece_buf, sems = refs[4 + nc :]
    c, f = lax.axis_index("ctx"), lax.axis_index("fsdp")
    weight = Pieces(dm, layer, own, pieces, own_buf, piece_buf, sems, lambda j: (c ^ j) < dm.nq)
    weight.start()
    tag = str(layer)
    n1[...] = norm(
        h[...].astype(F32), small_vec(dm, small, "g1" + tag), small_vec(dm, small, "s1" + tag)
    ).astype(BF16)
    bias[...] = small_vec(dm, small, "bq" + tag)
    relative(dm, f, n1, xr)
    weight.wait_own()
    for j in range(nc):
        i = c ^ j

        @pl.when(i < dm.nq)
        def _():
            weight.copies[j].wait()
            at = pl.ds(mult(i * dm.pc, dm.pc), dm.pc)
            acc = nn(xr[:, dm.pr :], weight.flat(j)) + nn(xr[:, : dm.pr], own_buf[:, at])
            y[:, at] = (acc + bias[:, at]).astype(BF16)

    for j in range(nc):
        for third in range(3):
            blocks[j, :, third * dm.w : (third + 1) * dm.w] = take_heads(
                dm, y, third * dm.d, c ^ j
            )


def qkv_call(dm, layer, meta, h, small, own, pieces, moves, ids):
    shape = (dm.nc, dm.t, 3 * dm.w)
    blocks = send_blocks(dm, 8 + dm.nc, shape)
    n1 = run(
        dm,
        functools.partial(qkv_body, dm, layer),
        [(meta, "s"), (h, "v"), (small, "v"), (own, "a")] + [(p, "a") for p in pieces],
        [sds((dm.t, dm.d), BF16)],
        [
            pltpu.VMEM((dm.t, dm.d), BF16),
            pltpu.VMEM((dm.t, 3 * dm.d), BF16),
            pltpu.VMEM((1, 3 * dm.d), F32),
            pltpu.VMEM(shape, BF16),
        ]
        + piece_scratch(dm, (dm.pr, 3 * dm.d)),
        flops=2 * dm.t * dm.d * 3 * dm.d,
        moves=moves + [blocks],
        ids=ids,
    )
    return n1[0], blocks.result


def proj_body(dm, layer, *refs):
    nc = dm.nc
    meta, h, small, own, heads = refs[:5]
    pieces = refs[5 : 5 + nc]
    ob, mid, n2 = refs[5 + nc : 8 + nc]
    xr, bias, own_buf, piece_buf, sems = refs[8 + nc :]
    c, f = lax.axis_index("ctx"), lax.axis_index("fsdp")
    weight = Pieces(dm, layer, own, pieces, own_buf, piece_buf, sems, lambda j: (c ^ j) >= dm.nq)
    weight.start()
    tag = str(layer)
    bias[...] = small_vec(dm, small, "bp" + tag)
    put_heads(dm, ob, 0, [heads.at[j] for j in range(nc)], 0, c)
    relative(dm, f, ob, xr)
    weight.wait_own()
    for j in range(nc):
        i = c ^ j

        @pl.when(i >= dm.nq)
        def _():
            weight.copies[j].wait()
            at = pl.ds(mult((i - dm.nq) * dm.pc, dm.pc), dm.pc)
            acc = nn(xr[:, dm.pr :], weight.flat(j)) + nn(xr[:, : dm.pr], own_buf[:, at])
            mid[:, at] = h[:, at].astype(F32) + acc + bias[:, at]

    n2[...] = norm(
        mid[...], small_vec(dm, small, "g2" + tag), small_vec(dm, small, "s2" + tag)
    ).astype(BF16)


def proj_call(dm, layer, meta, h, small, own, heads, pieces, moves, ids):
    td = (dm.t, dm.d)
    return run(
        dm,
        functools.partial(proj_body, dm, layer),
        [(meta, "s"), (h, "v"), (small, "v"), (own, "a"), (heads, "v")] + [(p, "a") for p in pieces],
        [sds(td, BF16), sds(td, F32), sds(td, BF16)],
        [pltpu.VMEM(td, BF16), pltpu.VMEM((1, dm.d), F32)] + piece_scratch(dm, (dm.pr, dm.d)),
        flops=2 * dm.t * dm.d * dm.d,
        moves=moves,
        ids=ids,
    )


def fc_body(dm, layer, *refs):
    nc = dm.nc
    meta, n2, small, own = refs[:4]
    pieces = refs[4 : 4 + nc]
    u, act = refs[4 + nc : 6 + nc]
    xr, bias, own_buf, piece_buf, sems = refs[6 + nc :]
    c, f = lax.axis_index("ctx"), lax.axis_index("fsdp")
    weight = Pieces(dm, layer, own, pieces, own_buf, piece_buf, sems, None)
    weight.start()
    bias[...] = small_vec(dm, small, "bf" + str(layer))
    relative(dm, f, n2, xr)
    weight.wait_own()
    for j in range(nc):
        i = c ^ j
        weight.copies[j].wait()
        at = pl.ds(mult(i * dm.pc, dm.pc), dm.pc)
        acc = nn(xr[:, dm.pr :], weight.flat(j)) + nn(xr[:, : dm.pr], own_buf[:, at])
        acc = acc + bias[:, at]
        u[:, at] = acc
        act[:, at] = gelu(acc).astype(BF16)


def fc_call(dm, layer, meta, n2, small, own, pieces, moves, ids):
    return run(
        dm,
        functools.partial(fc_body, dm, layer),
        [(meta, "s"), (n2, "v"), (small, "v"), (own, "a")] + [(p, "a") for p in pieces],
        [sds((dm.t, dm.ff), F32), sds((dm.t, dm.ff), BF16)],
        [pltpu.VMEM((dm.t, dm.d), BF16), pltpu.VMEM((1, dm.ff), F32)] + piece_scratch(dm, (dm.pr, dm.ff)),
        flops=2 * dm.t * dm.d * dm.ff,
        moves=moves,
        ids=ids,
    )


def out_body(dm, layer, *refs):
    nc = dm.nc
    meta, mid, act, small, own = refs[:5]
    pieces = refs[5 : 5 + nc]
    h = refs[5 + nc]
    own_buf, piece_buf, sems = refs[6 + nc :]
    c, f = lax.axis_index("ctx"), lax.axis_index("fsdp")
    weight = Pieces(dm, layer, own, pieces, own_buf, piece_buf, sems, None)
    weight.start()
    weight.wait_own()
    mine = act[:, pl.ds(mult(f * dm.ffn, dm.ffn), dm.ffn)]
    h[...] = mid[...] + nn(mine, own_buf[...]) + small_vec(dm, small, "bo" + str(layer))
    for col in range(dm.ncs):
        acc = None
        for j in range(col, nc, dm.ncs):
            i = c ^ j
            weight.copies[j].wait()
            for s in range(1, dm.nf):
                at = mult(ring(dm, f, s) * dm.ffn + (i // dm.ncs) * dm.pr, dm.pr)
                part = nn(act[:, pl.ds(at, dm.pr)], piece_buf[j, s - 1])
                acc = part if acc is None else acc + part
        at = pl.ds(mult((lax.rem(c, dm.ncs) ^ col) * dm.pc, dm.pc), dm.pc)
        h[:, at] = h[:, at] + acc


def out_call(dm, layer, meta, mid, act, small, own, pieces, moves, ids):
    return run(
        dm,
        functools.partial(out_body, dm, layer),
        [(meta, "s"), (mid, "v"), (act, "v"), (small, "v"), (own, "a")] + [(p, "a") for p in pieces],
        [sds((dm.t, dm.d), F32)],
        piece_scratch(dm, (dm.ffn, dm.d)),
        flops=2 * dm.t * dm.d * dm.ff,
        moves=moves,
        ids=ids,
    )[0]


def chosen(dm, which, take):
    out = take(0).astype(F32)
    pick = jnp.full(out.shape, which, jnp.int32)
    for k in range(1, dm.nc):
        out = jnp.where(pick == k, take(k).astype(F32), out)
    return out.astype(BF16)


def sort_rows(dm, meta, blocks, dst):
    for piece in range(2 * dm.nc):
        slot = meta[4 + dm.nc + min(piece, 2 * dm.nc - 1 - piece)]
        half = 0 if piece < dm.nc else dm.half
        dst[piece * dm.half : (piece + 1) * dm.half, :] = chosen(
            dm, slot, lambda j: blocks[j, half : half + dm.half, :]
        )


def unsort_rows(dm, meta, src, blocks, at):
    cols = slice(at, at + src.shape[1])

    def rows(piece):
        return src[piece * dm.half : (piece + 1) * dm.half, :]

    for j in range(dm.nc):
        low = meta[4 + j]
        blocks[j, : dm.half, cols] = chosen(dm, low, rows)
        blocks[j, dm.half :, cols] = chosen(dm, low, lambda k: rows(2 * dm.nc - 1 - k))


def stack_heads(dm, v, scale=None):
    if scale is not None:
        v = v * scale
    if dm.hl == 1:
        return v
    lane = lax.broadcasted_iota(jnp.int32, v.shape, 1) // HEAD_DIM
    return jnp.concatenate([jnp.where(lane == k, v, 0.0).astype(v.dtype) for k in range(dm.hl)], axis=0)


def pick_heads(dm, v):
    if dm.hl == 1:
        return v
    rows = v.shape[0] // dm.hl
    lane = lax.broadcasted_iota(jnp.int32, (rows, v.shape[1]), 1) // HEAD_DIM
    out = v[:rows]
    for k in range(1, dm.hl):
        out = jnp.where(lane == k, v[k * rows : (k + 1) * rows], out)
    return out


def doc_start(first_cut, second_cut, row):
    return jnp.where(row < first_cut, 0, jnp.where(row < second_cut, first_cut, second_cut))


def tile_rows(dm, t, tq, cuts):
    row = t * tq + lax.rem(lax.broadcasted_iota(jnp.int32, (dm.hl * tq, 1), 0), tq)
    return row, doc_start(cuts[0], cuts[1], row)


TQ = 256
TK = 256


def attend_body(dm, *refs):
    nc, w = dm.nc, dm.w
    meta, blocks, packed, lse, mixed, heads = refs
    cuts = (meta[2], meta[3])
    tq, tk = min(TQ, dm.rows), min(TK, dm.rows)
    sort_rows(dm, meta, blocks, packed)

    def tile(t, carry):
        here = pl.ds(mult(t * tq, tq), tq)
        q = stack_heads(dm, packed[here, :w], HEAD_DIM**-0.5)
        row, start = tile_rows(dm, t, tq, cuts)

        def chunk(kb, state):
            top, mass, acc = state
            there = pl.ds(mult(kb * tk, tk), tk)
            col = kb * tk + lax.broadcasted_iota(jnp.int32, (1, tk), 1)
            s = jnp.where((col <= row) & (col >= start), nt(q, packed[there, w : 2 * w]), NEG)
            new_top = jnp.maximum(top, jnp.max(s, axis=1, keepdims=True))
            p = jnp.exp(s - new_top)
            fade = jnp.exp(top - new_top)
            mass = mass * fade + jnp.sum(p, axis=1, keepdims=True)
            acc = acc * fade + nn(p.astype(BF16), packed[there, 2 * w :])
            return new_top, mass, acc

        initial = (
            jnp.full((dm.hl * tq, 1), LOW, F32),
            jnp.zeros((dm.hl * tq, 1), F32),
            jnp.zeros((dm.hl * tq, w), F32),
        )
        top, mass, acc = lax.fori_loop(0, ((t + 1) * tq + tk - 1) // tk, chunk, initial)
        mixed[here, :] = pick_heads(dm, acc * (1.0 / mass))
        norms = top + jnp.log(mass)
        for k in range(dm.hl):
            lse[k, here, :] = norms[k * tq : (k + 1) * tq]
        return carry

    lax.fori_loop(0, dm.rows // tq, tile, 0)
    unsort_rows(dm, meta, mixed, heads, 0)


def attend_call(dm, meta, blocks, moves, ids):
    shape = (dm.nc, dm.t, dm.w)
    heads = send_blocks(dm, 5, shape)
    saved = run(
        dm,
        functools.partial(attend_body, dm),
        [(meta, "s"), (blocks, "v")],
        [sds((dm.rows, 3 * dm.w), BF16), sds((dm.hl, dm.rows, 1), F32), sds((dm.rows, dm.w), F32)],
        [pltpu.VMEM(shape, BF16)],
        flops=8 * dm.rows * dm.rows * dm.w,
        moves=moves + [heads],
        ids=ids,
    )
    return saved, heads.result


def attend_back_body(dm, *refs):
    nc, w = dm.nc, dm.w
    meta, packed, lse, mixed, grads, blocks, dmix, dq, dk, dv = refs
    cuts = (meta[2], meta[3])
    tq, tk = min(TQ, dm.rows), min(TK, dm.rows)
    scale = HEAD_DIM**-0.5
    sort_rows(dm, meta, grads, dmix)
    dk[...] = jnp.zeros_like(dk)
    dv[...] = jnp.zeros_like(dv)

    def tile(t, carry):
        here = pl.ds(mult(t * tq, tq), tq)
        q = stack_heads(dm, packed[here, :w], scale)
        do = stack_heads(dm, dmix[here, :])
        o = jnp.concatenate([mixed[here, :]] * dm.hl, axis=0)
        delta = jnp.sum(do.astype(F32) * o, axis=1, keepdims=True)
        norms = jnp.concatenate([lse[k, here, :] for k in range(dm.hl)], axis=0)
        row, start = tile_rows(dm, t, tq, cuts)

        def chunk(kb, acc):
            there = pl.ds(mult(kb * tk, tk), tk)
            col = kb * tk + lax.broadcasted_iota(jnp.int32, (1, tk), 1)
            keys = packed[there, w : 2 * w]
            s = jnp.where((col <= row) & (col >= start), nt(q, keys), NEG)
            p = jnp.exp(s - norms)
            dp = nt(do, packed[there, 2 * w :])
            ds = (p * (dp - delta)).astype(BF16)
            dv[there, :] += tn(p.astype(BF16), do)
            dk[there, :] += tn(ds, q)
            return acc + nn(ds, keys)

        acc = lax.fori_loop(
            0, ((t + 1) * tq + tk - 1) // tk, chunk, jnp.zeros((dm.hl * tq, w), F32)
        )
        dq[here, :] = pick_heads(dm, acc) * scale
        return carry

    lax.fori_loop(0, dm.rows // tq, tile, 0)
    for at, src in enumerate((dq, dk, dv)):
        unsort_rows(dm, meta, src, blocks, at * w)


def attend_back_call(dm, meta, saved, grads, moves, ids):
    shape = (dm.nc, dm.t, 3 * dm.w)
    blocks = send_blocks(dm, 5, shape)
    run(
        dm,
        functools.partial(attend_back_body, dm),
        [(meta, "s")] + [(a, "v") for a in saved] + [(grads, "v")],
        [],
        [pltpu.VMEM(shape, BF16), pltpu.VMEM((dm.rows, dm.w), BF16)]
        + [pltpu.VMEM((dm.rows, dm.w), F32)] * 3,
        flops=16 * dm.rows * dm.rows * dm.w,
        moves=moves + [blocks],
        ids=ids,
    )
    return blocks.result


def top_body(dm, h, cot, small, result, dh, low, g_gain, g_shift):
    gain = small_vec(dm, small, "gf")
    v = h[...]
    result[...] = norm(v, gain, small_vec(dm, small, "sf")).astype(BF16)
    dv, g_gain[...], g_shift[...] = norm_back(v, gain, cot[...].astype(F32))
    dh[...] = dv
    low[...] = dv.astype(BF16)


def top_call(dm, h, cot, small):
    td, vec = (dm.t, dm.d), sds((1, dm.d), F32)
    return run(
        dm,
        functools.partial(top_body, dm),
        [(h, "v"), (cot, "v"), (small, "v")],
        [sds(td, BF16), sds(td, F32), sds(td, BF16), vec, vec],
        [],
        flops=20 * dm.t * dm.d,
    )


def out_back_body(dm, layer, *refs):
    nc = dm.nc
    meta, gm, u, own = refs[:4]
    pieces = refs[4 : 4 + nc]
    du, sum_gm, sum_du = refs[4 + nc : 7 + nc]
    gr, own_buf, piece_buf, sems = refs[7 + nc :]
    c, f = lax.axis_index("ctx"), lax.axis_index("fsdp")
    weight = Pieces(dm, layer, own, pieces, own_buf, piece_buf, sems, None)
    weight.start()
    sum_gm[...] = col_sum(gm[...])
    for col in range(dm.ncs):
        at = mult((lax.rem(c, dm.ncs) ^ col) * dm.pc, dm.pc)
        gr[:, col * dm.pc : (col + 1) * dm.pc] = gm[:, pl.ds(at, dm.pc)]

    def finish(dact, at):
        at = pl.ds(mult(at, dm.pr), dm.pr)
        low = (dact * gelu_slope(u[:, at])).astype(BF16)
        du[:, at] = low
        sum_du[:, at] = col_sum(low)

    weight.wait_own()
    for g in range(nc // dm.ncs):
        finish(nt(gm[...], own_buf[g * dm.pr : (g + 1) * dm.pr, :]), f * dm.ffn + g * dm.pr)
    for g in range(nc // dm.ncs):
        for col in range(dm.ncs):
            weight.copies[g * dm.ncs + col].wait()
        for s in range(1, dm.nf):
            dact = None
            for col in range(dm.ncs):
                part = nt(gr[:, col * dm.pc : (col + 1) * dm.pc], piece_buf[g * dm.ncs + col, s - 1])
                dact = part if dact is None else dact + part
            finish(dact, ring(dm, f, s) * dm.ffn + ((c // dm.ncs) ^ g) * dm.pr)


def out_back_call(dm, layer, meta, gm, u, own, pieces, moves, ids):
    return run(
        dm,
        functools.partial(out_back_body, dm, layer),
        [(meta, "s"), (gm, "v"), (u, "v"), (own, "a")] + [(p, "a") for p in pieces],
        [sds((dm.t, dm.ff), BF16), sds((1, dm.d), F32), sds((1, dm.ff), F32)],
        [pltpu.VMEM((dm.t, dm.d), BF16)] + piece_scratch(dm, (dm.ffn, dm.d)),
        flops=2 * dm.t * dm.d * dm.ff,
        moves=moves,
        ids=ids,
    )


def cols_back(dm, f, c, weight, dy, first, last, acc, out):
    weight.wait_own()
    acc[:, : dm.pr] = nt(dy[...], weight.own[...])
    acc[:, dm.pr :] = jnp.zeros((dm.t, dm.d - dm.pr), F32)
    for j in range(dm.nc):
        i = c ^ j

        def step():
            weight.copies[j].wait()
            at = pl.ds(mult((i - first) * dm.pc, dm.pc), dm.pc)
            acc[:, dm.pr :] += nt(dy[:, at], weight.flat(j))

        weight.each(j, step)
    for s in range(dm.nf):
        at = mult(ring(dm, f, s) * dm.pr, dm.pr)
        out[:, pl.ds(at, dm.pr)] = acc[:, s * dm.pr : (s + 1) * dm.pr].astype(out.dtype)


def fc_back_body(dm, layer, *refs):
    nc = dm.nc
    meta, du, dh, mid, small, own = refs[:6]
    pieces = refs[6 : 6 + nc]
    dmid, ga, sum_ga, g_gain, g_shift = refs[6 + nc : 11 + nc]
    acc, dn, own_buf, piece_buf, sems = refs[11 + nc :]
    c, f = lax.axis_index("ctx"), lax.axis_index("fsdp")
    weight = Pieces(dm, layer, own, pieces, own_buf, piece_buf, sems, None)
    weight.start()
    cols_back(dm, f, c, weight, du, 0, nc, acc, dn)
    dv, g_gain[...], g_shift[...] = norm_back(
        mid[...], small_vec(dm, small, "g2" + str(layer)), dn[...]
    )
    total = dh[...] + dv
    dmid[...] = total
    low = total.astype(BF16)
    ga[...] = low
    sum_ga[...] = col_sum(low)


def fc_back_call(dm, layer, meta, du, dh, mid, small, own, pieces, moves, ids):
    td, vec = (dm.t, dm.d), sds((1, dm.d), F32)
    return run(
        dm,
        functools.partial(fc_back_body, dm, layer),
        [(meta, "s"), (du, "v"), (dh, "v"), (mid, "v"), (small, "v"), (own, "a")]
        + [(p, "a") for p in pieces],
        [sds(td, F32), sds(td, BF16), vec, vec, vec],
        [pltpu.VMEM(td, F32), pltpu.VMEM(td, F32)] + piece_scratch(dm, (dm.pr, dm.ff)),
        flops=2 * dm.t * dm.d * dm.ff,
        moves=moves,
        ids=ids,
    )


def proj_back_body(dm, layer, *refs):
    nc = dm.nc
    meta, ga, own = refs[:3]
    pieces = refs[3 : 3 + nc]
    acc, dob, blocks, own_buf, piece_buf, sems = refs[3 + nc :]
    c, f = lax.axis_index("ctx"), lax.axis_index("fsdp")
    weight = Pieces(dm, layer, own, pieces, own_buf, piece_buf, sems, lambda j: (c ^ j) >= dm.nq)
    weight.start()
    cols_back(dm, f, c, weight, ga, dm.nq, nc, acc, dob)
    for j in range(nc):
        blocks[j] = take_heads(dm, dob, 0, c ^ j)


def proj_back_call(dm, layer, meta, ga, own, pieces, moves, ids):
    td, shape = (dm.t, dm.d), (dm.nc, dm.t, dm.w)
    blocks = send_blocks(dm, 5 + dm.nc, shape)
    run(
        dm,
        functools.partial(proj_back_body, dm, layer),
        [(meta, "s"), (ga, "v"), (own, "a")] + [(p, "a") for p in pieces],
        [],
        [pltpu.VMEM(td, F32), pltpu.VMEM(td, BF16), pltpu.VMEM(shape, BF16)]
        + piece_scratch(dm, (dm.pr, dm.d)),
        flops=2 * dm.t * dm.d * dm.d,
        moves=moves + [blocks],
        ids=ids,
    )
    return blocks.result


def qkv_back_body(dm, layer, *refs):
    nc = dm.nc
    meta, dmid, h, small, own, blocks = refs[:6]
    pieces = refs[6 : 6 + nc]
    dh, low, dqkv, sum_dqkv, g_gain, g_shift = refs[6 + nc : 12 + nc]
    acc, dn, own_buf, piece_buf, sems = refs[12 + nc :]
    blocks = [blocks.at[j] for j in range(nc)]
    c, f = lax.axis_index("ctx"), lax.axis_index("fsdp")
    weight = Pieces(dm, layer, own, pieces, own_buf, piece_buf, sems, lambda j: (c ^ j) < dm.nq)
    weight.start()
    for third in range(3):
        put_heads(dm, dqkv, third * dm.d, blocks, third * dm.w, c)
    sum_dqkv[...] = col_sum(dqkv[...])
    cols_back(dm, f, c, weight, dqkv, 0, dm.nq, acc, dn)
    dv, g_gain[...], g_shift[...] = norm_back(
        h[...].astype(F32), small_vec(dm, small, "g1" + str(layer)), dn[...]
    )
    total = dmid[...] + dv
    dh[...] = total
    low[...] = total.astype(BF16)


def qkv_back_call(dm, layer, meta, dmid, h, small, own, blocks, pieces, moves, ids):
    td, vec = (dm.t, dm.d), sds((1, dm.d), F32)
    return run(
        dm,
        functools.partial(qkv_back_body, dm, layer),
        [(meta, "s"), (dmid, "v"), (h, "v"), (small, "v"), (own, "a"), (blocks, "v")]
        + [(p, "a") for p in pieces],
        [sds(td, F32), sds(td, BF16), sds((dm.t, 3 * dm.d), BF16), sds((1, 3 * dm.d), F32), vec, vec],
        [pltpu.VMEM(td, F32), pltpu.VMEM(td, F32)] + piece_scratch(dm, (dm.pr, 3 * dm.d)),
        flops=2 * dm.t * dm.d * 3 * dm.d,
        moves=moves,
        ids=ids,
    )


def grad_body(dm, kind, meta, *refs):
    c, f = lax.axis_index("ctx"), lax.axis_index("fsdp")
    step = pl.program_id(0)
    if kind == "attn":
        n1, ob, dqkv, ga, keep, send, xt = refs
    else:
        x, y, keep, send, xt = refs

    @pl.when(step == 0)
    def _():
        if kind == "attn":
            xt[: dm.d, :] = n1[...].T
            xt[dm.d :, :] = ob[...].T
        else:
            xt[...] = x[...].T

    for odd, dst in enumerate((keep, send)):
        i = c ^ (2 * step + odd)

        def fill(row_base, row_step, dy):
            for s in range(dm.nf):
                at = mult(row_base + ring(dm, f, s) * row_step, dm.pr)
                dst[0, s] = nn(xt[pl.ds(at, dm.pr), :], dy).astype(BF16)

        if kind == "attn":

            @pl.when(i < dm.nq)
            def _():
                fill(0, dm.pr, dqkv[:, pl.ds(mult(i * dm.pc, dm.pc), dm.pc)])

            @pl.when(i >= dm.nq)
            def _():
                fill(dm.d, dm.pr, ga[:, pl.ds(mult((i - dm.nq) * dm.pc, dm.pc), dm.pc)])

        elif kind == "fc":
            fill(0, dm.pr, y[:, pl.ds(mult(i * dm.pc, dm.pc), dm.pc)])
        else:
            dy = y[:, pl.ds(mult(lax.rem(i, dm.ncs) * dm.pc, dm.pc), dm.pc)]
            fill((i // dm.ncs) * dm.pr, dm.ffn, dy)


def grad_call(dm, kind, meta, *arrays):
    depth = {"attn": 2 * dm.d, "fc": dm.d, "out": dm.ff}[kind]
    steps = dm.nc // 2
    block = (1, dm.nf, dm.pr, dm.pc)
    out = sds((steps,) + block[1:], BF16)
    return run(
        dm,
        functools.partial(grad_body, dm, kind),
        [(meta, "s")] + [(a, "v") for a in arrays],
        [out, out],
        [pltpu.VMEM((depth, dm.t), BF16)],
        flops=2 * dm.t * dm.d * dm.ff,
        grid=(steps,),
        in_specs=[pl.BlockSpec(memory_space=pltpu.SMEM)]
        + [pl.BlockSpec(a.shape, lambda k: (0, 0)) for a in arrays],
        out_specs=[pl.BlockSpec(block, lambda k: (k, 0, 0, 0))] * 2,
    )


def place_body(dm, kind, layer, old, *refs):
    nc = dm.nc
    meta = refs[0]
    pieces = refs[1 : 1 + nc]
    rest = refs[1 + nc + old :]
    count = 2 if kind == "attn" else 1
    outs, buf, sems = rest[:count], rest[count], rest[count + 1]
    c = lax.axis_index("ctx")
    for j in range(nc):
        i = c ^ j
        if kind == "out":
            rows = pl.ds(mult((i // dm.ncs) * dm.pr, dm.pr), dm.pr)
            cols = pl.ds(mult(lax.rem(i, dm.ncs) * dm.pc, dm.pc), dm.pc)
            buf[rows, cols] = pieces[j][...].astype(F32)
        else:
            buf[:, pl.ds(mult(i * dm.pc, dm.pc), dm.pc)] = pieces[j][...].astype(F32)
    if kind == "attn":
        copies = [
            pltpu.make_async_copy(buf.at[:, pl.ds(0, 3 * dm.d)], outs[0].at[layer], sems.at[0]),
            pltpu.make_async_copy(buf.at[:, pl.ds(3 * dm.d, dm.d)], outs[1].at[layer], sems.at[1]),
        ]
    else:
        copies = [pltpu.make_async_copy(buf, outs[0].at[layer], sems.at[0])]
    for copy in copies:
        copy.start()
    for copy in copies:
        copy.wait()


def place_call(dm, kind, layer, meta, pieces, old):
    shapes = {
        "attn": [(LAYERS, dm.pr, 3 * dm.d), (LAYERS, dm.pr, dm.d)],
        "fc": [(LAYERS, dm.pr, dm.ff)],
        "out": [(LAYERS, dm.ffn, dm.d)],
    }[kind]
    buf = {"attn": (dm.pr, dm.ff), "fc": (dm.pr, dm.ff), "out": (dm.ffn, dm.d)}[kind]
    return run(
        dm,
        functools.partial(place_body, dm, kind, layer, len(old)),
        [(meta, "s")] + [(p, "v") for p in pieces] + [(o, "a") for o in old],
        [sds(s, F32) for s in shapes],
        [pltpu.VMEM(buf, F32), pltpu.SemaphoreType.DMA((2,))],
        flops=0,
        out_specs=[pl.BlockSpec(memory_space=pl.ANY)] * len(shapes),
        alias={1 + dm.nc + k: k for k in range(len(old))},
    )


def plane_bits(nc):
    bits = []
    bit = 2
    while bit < nc:
        bits.append(bit)
        bit *= 2
    return bits


def value(v):
    return v.result if isinstance(v, Move) else v


def spread(dm, first):
    bits = plane_bits(dm.nc)
    held = {0: first}
    if len(bits) == 2:
        one, two = bits
        held.update({bit: whole(first, ("ctx", bit)) for bit in (one, two, 1)})
        yield [held[one], held[two], held[1]]
        lead = (slice(None),) * (len(first.shape) - 2)
        cut = first.shape[-2] // 2
        low, high = lead + (pl.ds(0, cut),), lead + (pl.ds(cut, cut),)
        far = Move(
            first.shape, first.dtype,
            [([(None, held[two], low)], ("ctx", one), low), ([(None, held[one], high)], ("ctx", two), high)],
        )
        held[one ^ two] = far
        held.update({bit ^ 1: whole(held[bit], ("ctx", 1)) for bit in bits})
        yield [far, held[one ^ 1], held[two ^ 1]]
        held[one ^ two ^ 1] = whole(far, ("ctx", 1))
        yield [held[one ^ two ^ 1]]
    else:
        for bit in bits + [1]:
            new = {j ^ bit: whole(v, ("ctx", bit)) for j, v in held.items()}
            yield list(new.values())
            held.update(new)
    return [held[j] for j in range(dm.nc)]


def gather(dm, source):
    others = Move(
        (dm.nf - 1, dm.pr, dm.pc), BF16,
        [(source, ("fsdp", s), (s - 1,)) for s in range(1, dm.nf)],
    )
    yield [others]
    return (yield from spread(dm, others))


def plane_sum(dm, keep, send):
    bits = plane_bits(dm.nc)
    other = whole(send, ("ctx", 1))
    yield [other]
    other = value(other)
    if len(bits) == 2:
        one, two = bits
        cut = dm.pr // 2
        low, high = slice(0, cut), slice(cut, dm.pr)

        def part(t, rows, *more):
            v = keep[t, :, rows].astype(F32) + other[t, :, rows].astype(F32)
            for m in more:
                v = v + value(m).astype(F32)
            return v

        def moved(v, bit):
            return whole(v.astype(BF16), ("ctx", bit))

        far_x, own_x = moved(part(3, low), one), moved(part(1, low), one)
        far_y, own_y = moved(part(3, high), two), moved(part(2, high), two)
        yield [far_x, own_x, far_y, own_y]
        x, y = moved(part(1, high, far_y), one), moved(part(2, low, far_x), two)
        yield [x, y]
        return jnp.concatenate([part(0, low, own_x, y), part(0, high, x, own_y)], axis=1)
    total = (keep.astype(F32) + other.astype(F32)).reshape((2,) * len(bits) + keep.shape[1:])
    for bit in reversed(bits):
        away = whole(total[1].astype(BF16), ("ctx", bit))
        yield [away]
        total = total[0] + value(away).astype(F32)
    return total


def reduce(dm, keep, send):
    total = (yield from plane_sum(dm, keep, send)).astype(BF16)
    others = Move(
        (dm.nf - 1,) + total.shape[1:], BF16,
        [([(None, total, (s,))], ("fsdp", dm.nf - s), (s - 1,)) for s in range(1, dm.nf)],
    )
    yield [others]
    mine = total[0].astype(F32)
    for s in range(1, dm.nf):
        mine = mine + value(others)[s - 1].astype(F32)
    return (yield from spread(dm, mine.astype(BF16)))


def reduce_small(dm, rows, f):
    n = rows.shape[1]
    total = rows.reshape(dm.nf, n // 128, 128)
    bit = 1
    while bit < dm.nc:
        other = whole(total, ("ctx", bit))
        yield [other]
        total = total + value(other)
        bit *= 2
    double = jnp.concatenate([total, total])
    turned = lax.dynamic_slice_in_dim(double, f, dm.nf)
    others = Move(
        (dm.nf - 1,) + total.shape[1:], F32,
        [([(None, turned, (dm.nf - s,))], ("fsdp", dm.nf - s), (s - 1,)) for s in range(1, dm.nf)],
    )
    yield [others]
    return (turned[0] + jnp.sum(value(others), axis=0)).reshape(n)


class Flow:
    def __init__(self, dm):
        self.dm, self.live, self.done = dm, {}, {}
        self.ids = itertools.count()

    def add(self, name, transfer):
        self.live[name] = transfer

    def take(self, *names):
        moves = []
        for name in names:
            if name in self.live:
                try:
                    moves += next(self.live[name])
                except StopIteration as stop:
                    self.done[name] = [value(v) for v in stop.value]
                    del self.live[name]
        return moves

    def move(self, *names):
        moves = self.take(*names)
        if moves:
            run(self.dm, None, [], [], [], 0, moves=moves, ids=self.ids)

    def finish(self, name):
        while name in self.live:
            self.move(name)
        return self.done[name]


def local(acts, cotangent, pair_slots, segments, *tensors):
    (
        attn_gain, attn_shift, qkv_weight, qkv_bias, proj_weight, proj_bias, mlp_gain, mlp_shift,
        fc_weight, fc_bias, out_weight, out_bias, final_gain, final_shift,
    ) = tensors
    nf, nc = lax.axis_size("fsdp"), lax.axis_size("ctx")
    dm = dims_of(acts, fc_weight, nf, nc)
    c, f = lax.axis_index("ctx"), lax.axis_index("fsdp")
    offsets, small_size = small_offsets(dm)

    seg = segments[0]
    cut_one = jnp.sum((seg == 0).astype(jnp.int32))
    cut_two = cut_one + jnp.sum((seg == 1).astype(jnp.int32))
    index = jnp.arange(nc, dtype=jnp.int32)
    others = jnp.bitwise_xor(c, index)
    lows = jnp.sum(jnp.where(others[:, None] == index[None, :], pair_slots[None, :], 0), axis=1)
    slots = jnp.sum(jnp.where(lows[None, :] == index[:, None], index[None, :], 0), axis=1)
    meta = jnp.concatenate([jnp.stack([c, f, cut_one, cut_two]).astype(jnp.int32), lows, slots])

    def source(kind, layer):
        def cols(first, last):
            at = jnp.clip(lax.axis_index("ctx"), first, last - 1) - first
            return (layer, pl.ds(0, dm.pr), pl.ds(mult(at * dm.pc, dm.pc), dm.pc))

        def place():
            at = lax.axis_index("ctx")
            row, col = (at // dm.ncs) * dm.pr, lax.rem(at, dm.ncs) * dm.pc
            return (layer, pl.ds(mult(row, dm.pr), dm.pr), pl.ds(mult(col, dm.pc), dm.pc))

        if kind == "attn":
            return [
                (lambda: lax.axis_index("ctx") < dm.nq, qkv_weight, lambda: cols(0, dm.nq)),
                (lambda: lax.axis_index("ctx") >= dm.nq, proj_weight, lambda: cols(dm.nq, nc)),
            ]
        if kind == "fc":
            return [(None, fc_weight, lambda: cols(0, nc))]
        return [(None, out_weight, place)]

    per_layer = (attn_gain, attn_shift, qkv_bias, proj_bias, mlp_gain, mlp_shift, fc_bias, out_bias)
    parts = [p[layer] for layer in range(LAYERS) for p in per_layer] + [final_gain, final_shift]
    packed = jnp.concatenate(parts).reshape(small_size // 128, 128)
    small_move = Move(
        (nf - 1,) + packed.shape, BF16,
        [([(None, packed, None)], ("fsdp", s), (s - 1,)) for s in range(1, nf)],
    )

    flow = Flow(dm)
    ids = flow.ids
    for layer in range(LAYERS):
        for kind, name in (("attn", "A"), ("fc", "C"), ("out", "O")):
            flow.add(name + str(layer), gather(dm, source(kind, layer)))
    moves = [small_move] + flow.take("A0") + flow.take("A0", "C0") + flow.take("A0", "C0", "O0")
    while "A0" in flow.live:
        extra = []
        try:
            extra = next(flow.live["A0"])
        except StopIteration as stop:
            flow.done["A0"] = stop.value
            del flow.live["A0"]
        moves += extra
    run(dm, None, [], [], [], 0, moves=moves, ids=ids)
    flow.done["A0"] = [value(v) for v in flow.done["A0"]]
    backwards = jnp.concatenate([packed[None], value(small_move)])[::-1]
    small = lax.dynamic_slice_in_dim(jnp.concatenate([backwards, backwards]), nf - 1 - f, nf)
    small = small.reshape(nf, small_size).astype(F32)

    h = acts[0]
    kept = []
    plan = (
        (("O0",), ("C0", "O0", "A1"), ("C0", "O0", "A1", "C1"), ("A1",), ("A1", "C1", "O1")),
        (("C1",), ("O1",), ("C1", "O1"), ("O1",), ()),
    )
    for layer in range(LAYERS):
        tag = str(layer)
        beside = plan[layer]
        attn = flow.finish("A" + tag)
        n1, blocks = qkv_call(dm, layer, meta, h, small, qkv_weight, attn, flow.take(*beside[0]), ids)
        saved, heads = attend_call(dm, meta, blocks, flow.take(*beside[1]), ids)
        ob, mid, n2 = proj_call(
            dm, layer, meta, h, small, proj_weight, heads, attn, flow.take(*beside[2]), ids
        )
        fc = flow.finish("C" + tag)
        u, act = fc_call(dm, layer, meta, n2, small, fc_weight, fc, flow.take(*beside[3]), ids)
        kept.append((h, n1, saved, ob, mid, n2, u, act))
        out = flow.finish("O" + tag)
        h = out_call(dm, layer, meta, mid, act, small, out_weight, out, flow.take(*beside[4]), ids)

    weights = flow.done
    vectors = {}
    result, dh, gm, vectors["gf"], vectors["sf"] = top_call(dm, h, cotangent[0], small)
    placed = {"attn": [], "fc": [], "out": []}

    def start(name, kind, *arrays):
        keep, send = grad_call(dm, kind, meta, *arrays)
        flow.add(name, reduce(dm, keep, send))

    def place(name, kind, layer):
        placed[kind] = place_call(dm, kind, layer, meta, flow.finish(name), placed[kind])

    for layer in reversed(range(LAYERS)):
        tag, nxt = str(layer), str(layer + 1)
        o_, a_, k_ = "o" + nxt, "a" + nxt, "c" + nxt
        o, a, k = "o" + tag, "a" + tag, "c" + tag
        h, n1, saved, ob, mid, n2, u, act = kept[layer]
        du, vectors["bo" + tag], vectors["bf" + tag] = out_back_call(
            dm, layer, meta, gm, u, out_weight, weights["O" + tag], flow.take(a_, k_, o_), ids
        )
        start(o, "out", act, gm)
        dmid, ga, vectors["bp" + tag], vectors["g2" + tag], vectors["s2" + tag] = fc_back_call(
            dm, layer, meta, du, dh, mid, small, fc_weight, weights["C" + tag], flow.take(o, a_, k_, o_), ids
        )
        start(k, "fc", n2, du)
        grads = proj_back_call(
            dm, layer, meta, ga, proj_weight, weights["A" + tag], flow.take(k, o, a_, k_, o_), ids
        )
        blocks = attend_back_call(dm, meta, saved, grads, flow.take(k, o, a_, k_), ids)
        dh, gm, dqkv, vectors["bq" + tag], vectors["g1" + tag], vectors["s1" + tag] = qkv_back_call(
            dm, layer, meta, dmid, h, small, qkv_weight, blocks, weights["A" + tag],
            flow.take(o, k, a_), ids,
        )
        start(a, "attn", n1, ob, dqkv, ga)

    names = [name + str(layer) for layer in range(LAYERS) for name, _ in SMALL] + ["gf", "sf"]
    rows = jnp.concatenate([vectors[name].reshape(nf, -1) for name in names], axis=1)
    small_sum = reduce_small(dm, rows, f)

    def listed(transfer):
        return [(yield from transfer)]

    flow.add("small", listed(small_sum))
    while flow.live:
        flow.move(*list(flow.live))
    for layer in reversed(range(LAYERS)):
        tag = str(layer)
        place("o" + tag, "out", layer)
        place("c" + tag, "fc", layer)
        place("a" + tag, "attn", layer)
    mine = flow.finish("small")[0]

    def vec(name):
        at, size = offsets[name]
        return mine[at : at + size]

    def both(name):
        return jnp.stack([vec(name + str(layer)) for layer in range(LAYERS)])

    return (
        result[None], gm[None], both("g1"), both("s1"), placed["attn"][0], both("bq"),
        placed["attn"][1], both("bp"), both("g2"), both("s2"), placed["fc"][0], both("bf"),
        placed["out"][0], both("bo"), vec("gf"), vec("sf"),
    )


def solution(mesh):
    row = P("fsdp", "ctx", None)
    vec, mat = P(None, "fsdp"), P(None, "fsdp", None)
    tensors = (vec, vec, mat, vec, mat, vec, vec, vec, mat, vec, mat, vec, P("fsdp"), P("fsdp"))
    return jax.shard_map(
        local,
        mesh=mesh,
        in_specs=(row, row, P(), P("fsdp", None)) + tensors,
        out_specs=(row, row) + tensors,
        check_vma=False,
    )
```

```python
import collections
import functools
import itertools

import jax
import jax.numpy as jnp
from jax import lax
from jax.experimental import pallas as pl
from jax.experimental.pallas import tpu as pltpu
from jax.sharding import PartitionSpec as P

HEADS = 16
HEAD_DIM = 64
LAYERS = 2
EPS = 1e-05
NEG = -1e30
LOW = -1e29
F32 = jnp.float32
BF16 = jnp.bfloat16
VMEM_BYTES = 56 * 1024 * 1024

FIELDS = ("t", "d", "ff", "nf", "nc", "pr", "pc", "nq", "ncs", "ffn", "w", "hl", "rows", "half")
Dims = collections.namedtuple("Dims", FIELDS)


def dims_of(acts, fc_weight, nf, nc):
    t, d = acts.shape[1], acts.shape[2]
    ff = fc_weight.shape[2]
    pr, pc = d // nf, ff // nc
    return Dims(
        t=t, d=d, ff=ff, nf=nf, nc=nc, pr=pr, pc=pc, nq=3 * d // pc, ncs=d // pc, ffn=ff // nf,
        w=d // nc, hl=HEADS // nc, rows=t * nc, half=t // 2,
    )


SMALL = (("g1", 1), ("s1", 1), ("bq", 3), ("bp", 1), ("g2", 1), ("s2", 1), ("bf", 4), ("bo", 1))


def small_offsets(dm):
    table, at = {}, 0
    for layer in range(LAYERS):
        for name, _ in SMALL:
            size = {"bq": 3 * dm.pr, "bf": dm.ffn}.get(name, dm.pr)
            table[name + str(layer)] = (at, size)
            at += size
    for name in ("gf", "sf"):
        table[name] = (at, dm.pr)
        at += dm.pr
    return table, at


def send_blocks(dm, slot, shape):
    return Move(
        shape, BF16,
        [([(None, slot, (j,))], ("ctx", j) if j else None, (j,)) for j in range(dm.nc)],
    )


def vector_names():
    return [name + str(layer) for layer in range(LAYERS) for name, _ in SMALL] + ["gf", "sf"]


def mult(v, by):
    return pl.multiple_of(v, by)


def nn(a, b):
    return lax.dot_general(a, b, (((1,), (0,)), ((), ())), preferred_element_type=F32)


def nt(a, b):
    return lax.dot_general(a, b, (((1,), (1,)), ((), ())), preferred_element_type=F32)


def tn(a, b):
    return lax.dot_general(a, b, (((0,), (0,)), ((), ())), preferred_element_type=F32)


def col_sum(v):
    return jnp.sum(v.astype(F32), axis=0, keepdims=True)


def small_vec(dm, small_ref, name):
    at, size = small_offsets(dm)[0][name]
    return jnp.concatenate([small_ref[g : g + 1, at : at + size] for g in range(dm.nf)], axis=1)


def norm_parts(v):
    center = v - jnp.mean(v, axis=-1, keepdims=True)
    scale = lax.rsqrt(jnp.mean(center * center, axis=-1, keepdims=True) + EPS)
    return center * scale, scale


def norm(v, gain, shift):
    return norm_parts(v)[0] * gain + shift


def norm_back(v, gain, dy):
    xh, scale = norm_parts(v)
    e = dy * gain
    dv = scale * (
        e - jnp.mean(e, axis=-1, keepdims=True) - xh * jnp.mean(e * xh, axis=-1, keepdims=True)
    )
    return dv, col_sum(dy * xh), col_sum(dy)


K0 = 0.7978845608028654
K1 = 0.044715


def gelu(u):
    return 0.5 * u * (1.0 + jnp.tanh(K0 * (u + K1 * u * u * u)))


def gelu_slope(u):
    th = jnp.tanh(K0 * (u + K1 * u * u * u))
    return 0.5 * (1.0 + th) + 0.5 * u * (1.0 - th * th) * (K0 * (1.0 + 3.0 * K1 * u * u))


class Slot:
    def __init__(self, kind, at, like=None):
        self.kind, self.at, self.result = kind, at, None
        if like is not None:
            self.shape, self.dtype = like.shape, like.dtype


class Move:
    def __init__(self, shape, dtype, parts):
        self.shape, self.dtype, self.parts = shape, dtype, parts
        self.result = None


def whole(array, route):
    return Move(array.shape, array.dtype, [([(None, array, None)], route, None)])


def value(v):
    return v.result if isinstance(v, (Move, Slot)) else v


def at_of(ref, index):
    return ref if index is None else ref.at[index() if callable(index) else index]


class Kernel:
    def __init__(self, dm, ids=None):
        self.dm, self.ids = dm, ids
        self.arrays, self.in_specs, self.slots = [], [], {}
        self.outs, self.out_specs, self.out_slots = [], [], []
        self.scratch, self.keys, self.steps = [], {}, []
        self.moves, self.flops = [], 0

    def operand(self, a, place):
        if isinstance(a, (Slot, Move)) and a.result is None:
            return a
        a = value(a)
        key = (id(a), place)
        if key not in self.slots:
            spaces = {"v": pltpu.VMEM, "s": pltpu.SMEM, "a": pl.ANY}
            self.slots[key] = Slot("in", len(self.arrays))
            self.arrays.append(a)
            self.in_specs.append(pl.BlockSpec(memory_space=spaces[place]))
        return self.slots[key]

    def output(self, out, space):
        slot = Slot("out", len(self.outs), out)
        self.outs.append(out)
        self.out_specs.append(pl.BlockSpec(memory_space=space))
        self.out_slots.append(slot)
        return slot

    def buffer(self, spec):
        key, spec = spec if isinstance(spec, tuple) else (None, spec)
        if key is None or key not in self.keys:
            slot = Slot("scratch", len(self.scratch))
            self.scratch.append(spec)
            if key is None:
                return slot
            self.keys[key] = slot
        return self.keys[key]

    def section(self, body, operands, outs, scratch, flops):
        refs = [self.operand(a, place) for a, place in operands]
        made = [self.output(o, pltpu.VMEM) for o in outs]
        bufs = [self.buffer(spec) for spec in scratch]
        self.steps.append(("body", body, refs + made + bufs))
        self.flops += flops
        return made, bufs

    def start(self, moves):
        for move in moves:
            parts = [
                ([(cond, self.operand(src, "a"), index) for cond, src, index in sources], route, place)
                for sources, route, place in move.parts
            ]
            slot = self.output(sds(move.shape, move.dtype), pl.ANY)
            self.moves.append((move, parts, slot))
            self.steps.append(("start", len(self.moves) - 1, None))

    def run(self, local=None):
        dm, moves, steps = self.dm, self.moves, self.steps
        order = {id(m): n for n, (m, _, _) in enumerate(moves)}
        count = sum(len(parts) for _, parts, _ in moves)
        routes = sorted({route for _, parts, _ in moves for _, route, _ in parts if route is not None})
        n_in, n_out, n_scratch = len(self.arrays), len(self.outs), len(self.scratch)
        sems = [pltpu.SemaphoreType.DMA((count,))] * 2 if count else []

        def kernel(*refs):
            groups = {"in": refs[:n_in], "out": refs[n_in : n_in + n_out], "scratch": refs[n_in + n_out :]}
            if count:
                send_sems, recv_sems = refs[-2:]
            c, f = lax.axis_index("ctx"), lax.axis_index("fsdp")

            def device(route, back=False):
                axis, by = route
                if axis == "ctx":
                    return (c ^ by, f)
                return (c, lax.rem(f + (dm.nf - by if back else by), dm.nf))

            if routes:
                barrier = pltpu.get_barrier_semaphore()
                for route in routes:
                    pl.semaphore_signal(
                        barrier, inc=1, device_id=device(route, True), device_id_type=pl.DeviceIdType.MESH
                    )
                pl.semaphore_wait(barrier, len(routes))

            def ref_of(src):
                if isinstance(src, Move):
                    src = moves[order[id(src)]][2]
                return groups[src.kind][src.at]

            at, copies = 0, []
            for _, parts, slot in moves:
                rows = []
                for sources, route, place in parts:
                    choices = []
                    for cond, src, index in sources:
                        ends = at_of(ref_of(src), index), at_of(ref_of(slot), place)
                        if route is None:
                            copy = pltpu.make_async_copy(*ends, recv_sems.at[at])
                        else:
                            copy = pltpu.make_async_remote_copy(
                                *ends, send_sems.at[at], recv_sems.at[at],
                                device_id=device(route), device_id_type=pl.DeviceIdType.MESH,
                            )
                        choices.append((cond, copy))
                    rows.append((route, choices))
                    at += 1
                copies.append(rows)
            arrived = set()

            def wait(n):
                if n in arrived:
                    return
                arrived.add(n)
                for route, choices in copies[n]:
                    copy = choices[0][1]
                    copy.wait() if route is None else copy.wait_recv()

            def ready(src):
                if isinstance(src, Move):
                    wait(order[id(src)])

            for kind, what, used in steps:
                if kind == "body":
                    for slot in used:
                        ready(slot)
                    what(*[ref_of(slot) for slot in used])
                    continue
                for sources, _, _ in moves[what][1]:
                    for _, src, _ in sources:
                        ready(src)
                for _, choices in copies[what]:
                    for cond, copy in choices:
                        if cond is None:
                            copy.start()
                        else:
                            pl.when(cond())(copy.start)
            for n in range(len(moves)):
                wait(n)
            for rows in copies:
                for route, choices in rows:
                    if route is not None:
                        choices[0][1].wait_send()

        params = {"collective_id": next(self.ids), "has_side_effects": True} if routes else {}
        moved = sum(a.size * a.dtype.itemsize for a in self.arrays + self.outs)
        results = pl.pallas_call(
            kernel,
            out_shape=self.outs,
            in_specs=self.in_specs,
            out_specs=self.out_specs,
            scratch_shapes=self.scratch + sems,
            compiler_params=pltpu.CompilerParams(vmem_limit_bytes=VMEM_BYTES, **params),
            cost_estimate=pl.CostEstimate(flops=self.flops, bytes_accessed=moved, transcendentals=0),
        )(*self.arrays)
        for slot, result in zip(self.out_slots, results):
            slot.result = result
        for move, _, slot in moves:
            move.result = slot.result


def sds(shape, dtype):
    return jax.ShapeDtypeStruct(shape, dtype)


class Pieces:
    def __init__(self, dm, layer, own, pieces, own_buf, piece_buf, sems, wanted):
        self.dm, self.wanted = dm, wanted
        self.own_copy = pltpu.make_async_copy(own.at[layer], own_buf, sems.at[dm.nc])
        self.copies = [
            pltpu.make_async_copy(pieces[j], piece_buf.at[j], sems.at[j]) for j in range(dm.nc)
        ]
        self.own, self.buf = own_buf, piece_buf

    def start(self):
        self.own_copy.start()
        for j in range(self.dm.nc):
            self.each(j, self.copies[j].start)

    def each(self, j, act):
        if self.wanted is None:
            act()
        else:
            pl.when(self.wanted(j))(act)

    def wait_own(self):
        self.own_copy.wait()

    def flat(self, j):
        return self.buf[j].reshape((self.dm.nf - 1) * self.dm.pr, self.dm.pc)


def piece_scratch(dm, own_shape):
    return [
        ("own" + str(own_shape), pltpu.VMEM(own_shape, BF16)),
        ("pieces", pltpu.VMEM((dm.nc, dm.nf - 1, dm.pr, dm.pc), BF16)),
        ("loads", pltpu.SemaphoreType.DMA((dm.nc + 1,))),
    ]


def ring(dm, f, s):
    return lax.rem(f + (dm.nf - s), dm.nf)


def relative(dm, f, src, dst):
    for s in range(dm.nf):
        at = mult(ring(dm, f, s) * dm.pr, dm.pr)
        dst[:, s * dm.pr : (s + 1) * dm.pr] = src[:, pl.ds(at, dm.pr)]


def take_heads(dm, ref, base, i):
    if dm.w % 128 == 0:
        return ref[:, pl.ds(mult(base + i * dm.w, 128), dm.w)]
    per = 128 // dm.w
    wide = ref[:, pl.ds(mult(base + (i // per) * 128, 128), 128)]
    part = wide[:, : dm.w]
    for at in range(1, per):
        part = jnp.where(lax.rem(i, per) == at, wide[:, at * dm.w : (at + 1) * dm.w], part)
    return part


def put_heads(dm, ref, base, blocks, at, c):
    if dm.w % 128 == 0:
        for j in range(dm.nc):
            ref[:, pl.ds(mult(base + (c ^ j) * dm.w, 128), dm.w)] = blocks[j][:, at : at + dm.w]
        return
    for j in range(0, dm.nc, 2):
        one, two = blocks[j][:, at : at + dm.w], blocks[j + 1][:, at : at + dm.w]
        even = lax.rem(c, 2) == 0
        pair = jnp.concatenate([jnp.where(even, one, two), jnp.where(even, two, one)], axis=1)
        ref[:, pl.ds(mult(base + ((c ^ j) // 2) * 128, 128), 128)] = pair


def qkv_body(dm, layer, *refs):
    nc = dm.nc
    meta, h, small, own = refs[:4]
    pieces = refs[4 : 4 + nc]
    n1, xr, y, bias, blocks, own_buf, piece_buf, sems = refs[4 + nc :]
    c, f = lax.axis_index("ctx"), lax.axis_index("fsdp")
    weight = Pieces(dm, layer, own, pieces, own_buf, piece_buf, sems, lambda j: (c ^ j) < dm.nq)
    weight.start()
    tag = str(layer)
    n1[...] = norm(
        h[...].astype(F32), small_vec(dm, small, "g1" + tag), small_vec(dm, small, "s1" + tag)
    ).astype(BF16)
    bias[...] = small_vec(dm, small, "bq" + tag)
    relative(dm, f, n1, xr)
    weight.wait_own()
    for j in range(nc):
        i = c ^ j

        @pl.when(i < dm.nq)
        def _():
            weight.copies[j].wait()
            at = pl.ds(mult(i * dm.pc, dm.pc), dm.pc)
            acc = nn(xr[:, dm.pr :], weight.flat(j)) + nn(xr[:, : dm.pr], own_buf[:, at])
            y[:, at] = (acc + bias[:, at]).astype(BF16)

    for j in range(nc):
        for third in range(3):
            blocks[j, :, third * dm.w : (third + 1) * dm.w] = take_heads(
                dm, y, third * dm.d, c ^ j
            )


def qkv_section(k, layer, h, small, own, pieces, meta):
    dm = k.dm
    shape = (dm.nc, dm.t, 3 * dm.w)
    (n1,), bufs = k.section(
        functools.partial(qkv_body, dm, layer),
        [(meta, "s"), (h, "v"), (small, "v"), (own, "a")] + [(p, "a") for p in pieces],
        [sds((dm.t, dm.d), BF16)],
        [
            ("xr", pltpu.VMEM((dm.t, dm.d), BF16)),
            pltpu.VMEM((dm.t, 3 * dm.d), BF16),
            pltpu.VMEM((1, 3 * dm.d), F32),
            pltpu.VMEM(shape, BF16),
        ]
        + piece_scratch(dm, (dm.pr, 3 * dm.d)),
        2 * dm.t * dm.d * 3 * dm.d,
    )
    blocks = send_blocks(dm, bufs[3], shape)
    k.start([blocks])
    return n1, blocks


def proj_body(dm, layer, *refs):
    nc = dm.nc
    meta, h, small, own, heads = refs[:5]
    pieces = refs[5 : 5 + nc]
    ob, mid, n2 = refs[5 + nc : 8 + nc]
    xr, bias, own_buf, piece_buf, sems = refs[8 + nc :]
    c, f = lax.axis_index("ctx"), lax.axis_index("fsdp")
    weight = Pieces(dm, layer, own, pieces, own_buf, piece_buf, sems, lambda j: (c ^ j) >= dm.nq)
    weight.start()
    tag = str(layer)
    bias[...] = small_vec(dm, small, "bp" + tag)
    put_heads(dm, ob, 0, [heads.at[j] for j in range(nc)], 0, c)
    relative(dm, f, ob, xr)
    weight.wait_own()
    for j in range(nc):
        i = c ^ j

        @pl.when(i >= dm.nq)
        def _():
            weight.copies[j].wait()
            at = pl.ds(mult((i - dm.nq) * dm.pc, dm.pc), dm.pc)
            acc = nn(xr[:, dm.pr :], weight.flat(j)) + nn(xr[:, : dm.pr], own_buf[:, at])
            mid[:, at] = h[:, at].astype(F32) + acc + bias[:, at]

    n2[...] = norm(
        mid[...], small_vec(dm, small, "g2" + tag), small_vec(dm, small, "s2" + tag)
    ).astype(BF16)


def proj_section(k, layer, h, small, own, heads, pieces, meta):
    dm = k.dm
    td = (dm.t, dm.d)
    return k.section(
        functools.partial(proj_body, dm, layer),
        [(meta, "s"), (h, "v"), (small, "v"), (own, "a"), (heads, "v")] + [(p, "a") for p in pieces],
        [sds(td, BF16), sds(td, F32), sds(td, BF16)],
        [("xr", pltpu.VMEM(td, BF16)), pltpu.VMEM((1, dm.d), F32)] + piece_scratch(dm, (dm.pr, dm.d)),
        2 * dm.t * dm.d * dm.d,
    )[0]


def fc_body(dm, layer, *refs):
    nc = dm.nc
    meta, n2, small, own = refs[:4]
    pieces = refs[4 : 4 + nc]
    u, act = refs[4 + nc : 6 + nc]
    xr, bias, own_buf, piece_buf, sems = refs[6 + nc :]
    c, f = lax.axis_index("ctx"), lax.axis_index("fsdp")
    weight = Pieces(dm, layer, own, pieces, own_buf, piece_buf, sems, None)
    weight.start()
    bias[...] = small_vec(dm, small, "bf" + str(layer))
    relative(dm, f, n2, xr)
    weight.wait_own()
    for j in range(nc):
        i = c ^ j
        weight.copies[j].wait()
        at = pl.ds(mult(i * dm.pc, dm.pc), dm.pc)
        acc = nn(xr[:, dm.pr :], weight.flat(j)) + nn(xr[:, : dm.pr], own_buf[:, at])
        acc = acc + bias[:, at]
        u[:, at] = acc
        act[:, at] = gelu(acc).astype(BF16)


def fc_section(k, layer, n2, small, own, pieces, meta):
    dm = k.dm
    return k.section(
        functools.partial(fc_body, dm, layer),
        [(meta, "s"), (n2, "v"), (small, "v"), (own, "a")] + [(p, "a") for p in pieces],
        [sds((dm.t, dm.ff), F32), sds((dm.t, dm.ff), BF16)],
        [("xr", pltpu.VMEM((dm.t, dm.d), BF16)), pltpu.VMEM((1, dm.ff), F32)]
        + piece_scratch(dm, (dm.pr, dm.ff)),
        2 * dm.t * dm.d * dm.ff,
    )[0]


def out_body(dm, layer, *refs):
    nc = dm.nc
    meta, mid, act, small, own = refs[:5]
    pieces = refs[5 : 5 + nc]
    h = refs[5 + nc]
    own_buf, piece_buf, sems = refs[6 + nc :]
    c, f = lax.axis_index("ctx"), lax.axis_index("fsdp")
    weight = Pieces(dm, layer, own, pieces, own_buf, piece_buf, sems, None)
    weight.start()
    weight.wait_own()
    mine = act[:, pl.ds(mult(f * dm.ffn, dm.ffn), dm.ffn)]
    h[...] = mid[...] + nn(mine, own_buf[...]) + small_vec(dm, small, "bo" + str(layer))
    for col in range(dm.ncs):
        acc = None
        for j in range(col, nc, dm.ncs):
            i = c ^ j
            weight.copies[j].wait()
            for s in range(1, dm.nf):
                at = mult(ring(dm, f, s) * dm.ffn + (i // dm.ncs) * dm.pr, dm.pr)
                part = nn(act[:, pl.ds(at, dm.pr)], piece_buf[j, s - 1])
                acc = part if acc is None else acc + part
        at = pl.ds(mult((lax.rem(c, dm.ncs) ^ col) * dm.pc, dm.pc), dm.pc)
        h[:, at] = h[:, at] + acc


def out_section(k, layer, mid, act, small, own, pieces, meta):
    dm = k.dm
    return k.section(
        functools.partial(out_body, dm, layer),
        [(meta, "s"), (mid, "v"), (act, "v"), (small, "v"), (own, "a")] + [(p, "a") for p in pieces],
        [sds((dm.t, dm.d), F32)],
        piece_scratch(dm, (dm.ffn, dm.d)),
        2 * dm.t * dm.d * dm.ff,
    )[0][0]


def chosen(dm, which, take):
    out = take(0).astype(F32)
    pick = jnp.full(out.shape, which, jnp.int32)
    for k in range(1, dm.nc):
        out = jnp.where(pick == k, take(k).astype(F32), out)
    return out.astype(BF16)


def sort_rows(dm, meta, blocks, dst):
    for piece in range(2 * dm.nc):
        slot = meta[4 + dm.nc + min(piece, 2 * dm.nc - 1 - piece)]
        half = 0 if piece < dm.nc else dm.half
        dst[piece * dm.half : (piece + 1) * dm.half, :] = chosen(
            dm, slot, lambda j: blocks[j, half : half + dm.half, :]
        )


def unsort_rows(dm, meta, src, blocks, at):
    cols = slice(at, at + src.shape[1])

    def rows(piece):
        return src[piece * dm.half : (piece + 1) * dm.half, :]

    for j in range(dm.nc):
        low = meta[4 + j]
        blocks[j, : dm.half, cols] = chosen(dm, low, rows)
        blocks[j, dm.half :, cols] = chosen(dm, low, lambda k: rows(2 * dm.nc - 1 - k))


def stack_heads(dm, v, scale=None):
    if scale is not None:
        v = v * scale
    if dm.hl == 1:
        return v
    lane = lax.broadcasted_iota(jnp.int32, v.shape, 1) // HEAD_DIM
    return jnp.concatenate([jnp.where(lane == k, v, 0.0).astype(v.dtype) for k in range(dm.hl)], axis=0)


def pick_heads(dm, v):
    if dm.hl == 1:
        return v
    rows = v.shape[0] // dm.hl
    lane = lax.broadcasted_iota(jnp.int32, (rows, v.shape[1]), 1) // HEAD_DIM
    out = v[:rows]
    for k in range(1, dm.hl):
        out = jnp.where(lane == k, v[k * rows : (k + 1) * rows], out)
    return out


def doc_start(first_cut, second_cut, row):
    return jnp.where(row < first_cut, 0, jnp.where(row < second_cut, first_cut, second_cut))


def tile_rows(dm, t, tq, cuts):
    row = t * tq + lax.rem(lax.broadcasted_iota(jnp.int32, (dm.hl * tq, 1), 0), tq)
    return row, doc_start(cuts[0], cuts[1], row)


TQ = 256
TK = 256


def attend_body(dm, *refs):
    nc, w = dm.nc, dm.w
    meta, blocks, packed, lse, mixed, heads = refs
    cuts = (meta[2], meta[3])
    tq, tk = min(TQ, dm.rows), min(TK, dm.rows)
    sort_rows(dm, meta, blocks, packed)

    def tile(t, carry):
        here = pl.ds(mult(t * tq, tq), tq)
        q = stack_heads(dm, packed[here, :w], HEAD_DIM**-0.5)
        row, start = tile_rows(dm, t, tq, cuts)

        def chunk(kb, state):
            top, mass, acc = state
            there = pl.ds(mult(kb * tk, tk), tk)
            col = kb * tk + lax.broadcasted_iota(jnp.int32, (1, tk), 1)
            s = jnp.where((col <= row) & (col >= start), nt(q, packed[there, w : 2 * w]), NEG)
            new_top = jnp.maximum(top, jnp.max(s, axis=1, keepdims=True))
            p = jnp.exp(s - new_top)
            fade = jnp.exp(top - new_top)
            mass = mass * fade + jnp.sum(p, axis=1, keepdims=True)
            acc = acc * fade + nn(p.astype(BF16), packed[there, 2 * w :])
            return new_top, mass, acc

        initial = (
            jnp.full((dm.hl * tq, 1), LOW, F32),
            jnp.zeros((dm.hl * tq, 1), F32),
            jnp.zeros((dm.hl * tq, w), F32),
        )
        top, mass, acc = lax.fori_loop(0, ((t + 1) * tq + tk - 1) // tk, chunk, initial)
        mixed[here, :] = pick_heads(dm, acc * (1.0 / mass))
        norms = top + jnp.log(mass)
        for k in range(dm.hl):
            lse[k, here, :] = norms[k * tq : (k + 1) * tq]
        return carry

    lax.fori_loop(0, dm.rows // tq, tile, 0)
    unsort_rows(dm, meta, mixed, heads, 0)


def attend_section(k, blocks, meta):
    dm = k.dm
    shape = (dm.nc, dm.t, dm.w)
    saved, bufs = k.section(
        functools.partial(attend_body, dm),
        [(meta, "s"), (blocks, "v")],
        [sds((dm.rows, 3 * dm.w), BF16), sds((dm.hl, dm.rows, 1), F32), sds((dm.rows, dm.w), F32)],
        [pltpu.VMEM(shape, BF16)],
        8 * dm.rows * dm.rows * dm.w,
    )
    heads = send_blocks(dm, bufs[0], shape)
    k.start([heads])
    return saved, heads


def attend_back_body(dm, *refs):
    nc, w = dm.nc, dm.w
    meta, packed, lse, mixed, grads, blocks, dmix, dq, dk, dv = refs
    cuts = (meta[2], meta[3])
    tq, tk = min(TQ, dm.rows), min(TK, dm.rows)
    scale = HEAD_DIM**-0.5
    sort_rows(dm, meta, grads, dmix)
    dk[...] = jnp.zeros_like(dk)
    dv[...] = jnp.zeros_like(dv)

    def tile(t, carry):
        here = pl.ds(mult(t * tq, tq), tq)
        q = stack_heads(dm, packed[here, :w], scale)
        do = stack_heads(dm, dmix[here, :])
        o = jnp.concatenate([mixed[here, :]] * dm.hl, axis=0)
        delta = jnp.sum(do.astype(F32) * o, axis=1, keepdims=True)
        norms = jnp.concatenate([lse[k, here, :] for k in range(dm.hl)], axis=0)
        row, start = tile_rows(dm, t, tq, cuts)

        def chunk(kb, acc):
            there = pl.ds(mult(kb * tk, tk), tk)
            col = kb * tk + lax.broadcasted_iota(jnp.int32, (1, tk), 1)
            keys = packed[there, w : 2 * w]
            s = jnp.where((col <= row) & (col >= start), nt(q, keys), NEG)
            p = jnp.exp(s - norms)
            dp = nt(do, packed[there, 2 * w :])
            ds = (p * (dp - delta)).astype(BF16)
            dv[there, :] += tn(p.astype(BF16), do)
            dk[there, :] += tn(ds, q)
            return acc + nn(ds, keys)

        acc = lax.fori_loop(
            0, ((t + 1) * tq + tk - 1) // tk, chunk, jnp.zeros((dm.hl * tq, w), F32)
        )
        dq[here, :] = pick_heads(dm, acc) * scale
        return carry

    lax.fori_loop(0, dm.rows // tq, tile, 0)
    for at, src in enumerate((dq, dk, dv)):
        unsort_rows(dm, meta, src, blocks, at * w)


def attend_back_section(k, saved, grads, meta):
    dm = k.dm
    shape = (dm.nc, dm.t, 3 * dm.w)
    _, bufs = k.section(
        functools.partial(attend_back_body, dm),
        [(meta, "s")] + [(a, "v") for a in saved] + [(grads, "v")],
        [],
        [pltpu.VMEM(shape, BF16), pltpu.VMEM((dm.rows, dm.w), BF16)]
        + [pltpu.VMEM((dm.rows, dm.w), F32)] * 3,
        16 * dm.rows * dm.rows * dm.w,
    )
    blocks = send_blocks(dm, bufs[0], shape)
    k.start([blocks])
    return blocks


def top_body(dm, h, cot, small, result, dh, low, g_gain, g_shift):
    gain = small_vec(dm, small, "gf")
    v = h[...]
    result[...] = norm(v, gain, small_vec(dm, small, "sf")).astype(BF16)
    dv, g_gain[...], g_shift[...] = norm_back(v, gain, cot[...].astype(F32))
    dh[...] = dv
    low[...] = dv.astype(BF16)


def top_section(k, h, cot, small):
    dm = k.dm
    td, vec = (dm.t, dm.d), sds((1, dm.d), F32)
    return k.section(
        functools.partial(top_body, dm),
        [(h, "v"), (cot, "v"), (small, "v")],
        [sds(td, BF16), sds(td, F32), sds(td, BF16), vec, vec],
        [],
        20 * dm.t * dm.d,
    )[0]


def out_back_body(dm, layer, *refs):
    nc = dm.nc
    meta, gm, u, own = refs[:4]
    pieces = refs[4 : 4 + nc]
    du, sum_gm, sum_du = refs[4 + nc : 7 + nc]
    gr, own_buf, piece_buf, sems = refs[7 + nc :]
    c, f = lax.axis_index("ctx"), lax.axis_index("fsdp")
    weight = Pieces(dm, layer, own, pieces, own_buf, piece_buf, sems, None)
    weight.start()
    sum_gm[...] = col_sum(gm[...])
    for col in range(dm.ncs):
        at = mult((lax.rem(c, dm.ncs) ^ col) * dm.pc, dm.pc)
        gr[:, col * dm.pc : (col + 1) * dm.pc] = gm[:, pl.ds(at, dm.pc)]

    def finish(dact, at):
        at = pl.ds(mult(at, dm.pr), dm.pr)
        low = (dact * gelu_slope(u[:, at])).astype(BF16)
        du[:, at] = low
        sum_du[:, at] = col_sum(low)

    weight.wait_own()
    for g in range(nc // dm.ncs):
        finish(nt(gm[...], own_buf[g * dm.pr : (g + 1) * dm.pr, :]), f * dm.ffn + g * dm.pr)
    for g in range(nc // dm.ncs):
        for col in range(dm.ncs):
            weight.copies[g * dm.ncs + col].wait()
        for s in range(1, dm.nf):
            dact = None
            for col in range(dm.ncs):
                part = nt(gr[:, col * dm.pc : (col + 1) * dm.pc], piece_buf[g * dm.ncs + col, s - 1])
                dact = part if dact is None else dact + part
            finish(dact, ring(dm, f, s) * dm.ffn + ((c // dm.ncs) ^ g) * dm.pr)


def out_back_section(k, layer, gm, u, own, pieces, meta):
    dm = k.dm
    return k.section(
        functools.partial(out_back_body, dm, layer),
        [(meta, "s"), (gm, "v"), (u, "v"), (own, "a")] + [(p, "a") for p in pieces],
        [sds((dm.t, dm.ff), BF16), sds((1, dm.d), F32), sds((1, dm.ff), F32)],
        [("xr", pltpu.VMEM((dm.t, dm.d), BF16))] + piece_scratch(dm, (dm.ffn, dm.d)),
        2 * dm.t * dm.d * dm.ff,
    )[0]


def cols_back(dm, f, c, weight, dy, first, last, acc, out):
    weight.wait_own()
    acc[:, : dm.pr] = nt(dy[...], weight.own[...])
    acc[:, dm.pr :] = jnp.zeros((dm.t, dm.d - dm.pr), F32)
    for j in range(dm.nc):
        i = c ^ j

        def step():
            weight.copies[j].wait()
            at = pl.ds(mult((i - first) * dm.pc, dm.pc), dm.pc)
            acc[:, dm.pr :] += nt(dy[:, at], weight.flat(j))

        weight.each(j, step)
    for s in range(dm.nf):
        at = mult(ring(dm, f, s) * dm.pr, dm.pr)
        out[:, pl.ds(at, dm.pr)] = acc[:, s * dm.pr : (s + 1) * dm.pr].astype(out.dtype)


def fc_back_body(dm, layer, *refs):
    nc = dm.nc
    meta, du, dh, mid, small, own = refs[:6]
    pieces = refs[6 : 6 + nc]
    dmid, ga, sum_ga, g_gain, g_shift = refs[6 + nc : 11 + nc]
    acc, dn, own_buf, piece_buf, sems = refs[11 + nc :]
    c, f = lax.axis_index("ctx"), lax.axis_index("fsdp")
    weight = Pieces(dm, layer, own, pieces, own_buf, piece_buf, sems, None)
    weight.start()
    cols_back(dm, f, c, weight, du, 0, nc, acc, dn)
    dv, g_gain[...], g_shift[...] = norm_back(
        mid[...], small_vec(dm, small, "g2" + str(layer)), dn[...]
    )
    total = dh[...] + dv
    dmid[...] = total
    low = total.astype(BF16)
    ga[...] = low
    sum_ga[...] = col_sum(low)


def fc_back_section(k, layer, du, dh, mid, small, own, pieces, meta):
    dm = k.dm
    td, vec = (dm.t, dm.d), sds((1, dm.d), F32)
    return k.section(
        functools.partial(fc_back_body, dm, layer),
        [(meta, "s"), (du, "v"), (dh, "v"), (mid, "v"), (small, "v"), (own, "a")]
        + [(p, "a") for p in pieces],
        [sds(td, F32), sds(td, BF16), vec, vec, vec],
        [pltpu.VMEM(td, F32), pltpu.VMEM(td, F32)] + piece_scratch(dm, (dm.pr, dm.ff)),
        2 * dm.t * dm.d * dm.ff,
    )[0]


def proj_back_body(dm, layer, *refs):
    nc = dm.nc
    meta, ga, own = refs[:3]
    pieces = refs[3 : 3 + nc]
    acc, dob, blocks, own_buf, piece_buf, sems = refs[3 + nc :]
    c, f = lax.axis_index("ctx"), lax.axis_index("fsdp")
    weight = Pieces(dm, layer, own, pieces, own_buf, piece_buf, sems, lambda j: (c ^ j) >= dm.nq)
    weight.start()
    cols_back(dm, f, c, weight, ga, dm.nq, nc, acc, dob)
    for j in range(nc):
        blocks[j] = take_heads(dm, dob, 0, c ^ j)


def proj_back_section(k, layer, ga, own, pieces, meta):
    dm = k.dm
    td, shape = (dm.t, dm.d), (dm.nc, dm.t, dm.w)
    _, bufs = k.section(
        functools.partial(proj_back_body, dm, layer),
        [(meta, "s"), (ga, "v"), (own, "a")] + [(p, "a") for p in pieces],
        [],
        [pltpu.VMEM(td, F32), pltpu.VMEM(td, BF16), pltpu.VMEM(shape, BF16)]
        + piece_scratch(dm, (dm.pr, dm.d)),
        2 * dm.t * dm.d * dm.d,
    )
    blocks = send_blocks(dm, bufs[2], shape)
    k.start([blocks])
    return blocks


def qkv_back_body(dm, layer, *refs):
    nc = dm.nc
    meta, dmid, h, small, own, blocks = refs[:6]
    pieces = refs[6 : 6 + nc]
    dh, low, dqkv, sum_dqkv, g_gain, g_shift = refs[6 + nc : 12 + nc]
    acc, dn, own_buf, piece_buf, sems = refs[12 + nc :]
    blocks = [blocks.at[j] for j in range(nc)]
    c, f = lax.axis_index("ctx"), lax.axis_index("fsdp")
    weight = Pieces(dm, layer, own, pieces, own_buf, piece_buf, sems, lambda j: (c ^ j) < dm.nq)
    weight.start()
    for third in range(3):
        put_heads(dm, dqkv, third * dm.d, blocks, third * dm.w, c)
    sum_dqkv[...] = col_sum(dqkv[...])
    cols_back(dm, f, c, weight, dqkv, 0, dm.nq, acc, dn)
    dv, g_gain[...], g_shift[...] = norm_back(
        h[...].astype(F32), small_vec(dm, small, "g1" + str(layer)), dn[...]
    )
    total = dmid[...] + dv
    dh[...] = total
    low[...] = total.astype(BF16)


def qkv_back_section(k, layer, dmid, h, small, own, blocks, pieces, meta):
    dm = k.dm
    td, vec = (dm.t, dm.d), sds((1, dm.d), F32)
    return k.section(
        functools.partial(qkv_back_body, dm, layer),
        [(meta, "s"), (dmid, "v"), (h, "v"), (small, "v"), (own, "a"), (blocks, "v")]
        + [(p, "a") for p in pieces],
        [sds(td, F32), sds(td, BF16), sds((dm.t, 3 * dm.d), BF16), sds((1, 3 * dm.d), F32), vec, vec],
        [pltpu.VMEM(td, F32), pltpu.VMEM(td, F32)] + piece_scratch(dm, (dm.pr, 3 * dm.d)),
        2 * dm.t * dm.d * 3 * dm.d,
    )[0]


def sum_body(indices, *refs):
    n = len(indices)
    out, bufs, sems = refs[n], refs[n + 1 : 2 * n + 1], refs[2 * n + 1]
    copies = [
        pltpu.make_async_copy(at_of(ref, index), buf, sems.at[at])
        for at, (ref, index, buf) in enumerate(zip(refs, indices, bufs))
    ]
    for copy in copies:
        copy.start()
    for copy in copies:
        copy.wait()
    total = bufs[0][...].astype(F32)
    for buf in bufs[1:]:
        total = total + buf[...].astype(F32)
    out[...] = total.astype(out.dtype)


def sum_section(k, terms, shape, dtype=BF16, parts=None):
    bufs = [
        ("sum" + str((at, shape, dtype)), pltpu.VMEM(shape, dtype)) for at in range(len(terms))
    ]
    return k.section(
        functools.partial(sum_body, [index for _, index in terms]),
        [(src, "a") for src, _ in terms],
        [sds(shape, dtype)],
        bufs + [("sum" + str(len(terms)), pltpu.SemaphoreType.DMA((len(terms),)))],
        0,
    )[0][0]


def collect_body(dm, *refs):
    names, (table, _) = vector_names(), small_offsets(dm)
    for name, ref in zip(names, refs):
        at, size = table[name]
        for g in range(dm.nf):
            refs[-1][g, :, at : at + size] = ref[:, g * size : (g + 1) * size]


def grad_body(dm, kind, *refs):
    c, f = lax.axis_index("ctx"), lax.axis_index("fsdp")
    out, xt = refs[-2:]
    pairs = [refs[n : n + 2] for n in range(0, len(refs) - 2, 2)]
    lefts = pairs[: len(pairs) // 2]
    for n, pair in enumerate(lefts):
        depth = pair[0].shape[1]
        for half, ref in enumerate(pair):
            xt[n * depth : (n + 1) * depth, half * dm.t : (half + 1) * dm.t] = ref[...].T
    rights = pairs[len(pairs) // 2 :]

    def fill(t, row_base, row_step, pair, col):
        cols = pl.ds(mult(col * dm.pc, dm.pc), dm.pc)
        dy = jnp.concatenate([pair[0][:, cols], pair[1][:, cols]], axis=0)
        for s in range(dm.nf):
            at = mult(row_base + ring(dm, f, s) * row_step, dm.pr)
            out[t, s] = nn(xt[pl.ds(at, dm.pr), :], dy).astype(BF16)

    for t in reversed(range(dm.nc // 2)):
        i = c ^ (2 * t)
        if kind == "attn":
            pl.when(i < dm.nq)(lambda: fill(t, 0, dm.pr, rights[0], i))
            pl.when(i >= dm.nq)(lambda: fill(t, dm.d, dm.pr, rights[1], i - dm.nq))
        elif kind == "fc":
            fill(t, 0, dm.pr, rights[0], i)
        else:
            fill(t, (i // dm.ncs) * dm.pr, dm.ffn, rights[0], lax.rem(i, dm.ncs))


def grad_section(k, kind, lefts, rights):
    dm = k.dm
    depth = {"attn": 2 * dm.d, "fc": dm.d, "out": dm.ff}[kind]
    return k.section(
        functools.partial(grad_body, dm, kind),
        [(a, "v") for pair in lefts + rights for a in pair],
        [sds((dm.nc // 2, dm.nf, dm.pr, dm.pc), BF16)],
        [pltpu.VMEM((depth, 2 * dm.t), BF16)],
        2 * dm.t * dm.d * dm.ff,
    )[0][0]


def place_body(dm, *refs):
    nc = dm.nc
    jobs = [(layer, kind) for kind in ("out", "fc", "attn") for layer in reversed(range(LAYERS))]
    pieces = {job: refs[n * nc : (n + 1) * nc] for n, job in enumerate(jobs)}
    vector = refs[len(jobs) * nc]
    qkv, proj, fc, out = refs[len(jobs) * nc + 1 : len(jobs) * nc + 5]
    small = refs[len(jobs) * nc + 5 : -5]
    loads, wide, tall, load_sems, sems = refs[-5:]
    c = lax.axis_index("ctx")

    def fetch(n):
        return [
            pltpu.make_async_copy(pieces[jobs[n]][j], loads.at[n % 2, j], load_sems.at[n % 2, j])
            for j in range(nc)
        ]

    def store(n):
        layer, kind = jobs[n]
        buf, sem = (tall if kind == "out" else wide).at[n % 2], sems.at[n % 2]
        if kind == "attn":
            return [
                pltpu.make_async_copy(buf.at[:, pl.ds(0, 3 * dm.d)], qkv.at[layer], sem.at[0]),
                pltpu.make_async_copy(buf.at[:, pl.ds(3 * dm.d, dm.d)], proj.at[layer], sem.at[1]),
            ]
        return [pltpu.make_async_copy(buf, (out if kind == "out" else fc).at[layer], sem.at[0])]

    for copy in fetch(0):
        copy.start()
    for n, name in enumerate(vector_names()):
        at, size = small_offsets(dm)[0][name]
        row, ref = (n // len(SMALL), small[n % len(SMALL)])
        if row == LAYERS:
            row, ref = 0, small[len(SMALL) + n % len(SMALL)]
        ref[row : row + 1, :] = vector[:, at : at + size]
    for n in range(len(jobs)):
        if n + 1 < len(jobs):
            for copy in fetch(n + 1):
                copy.start()
        if n >= 2:
            for copy in store(n - 2):
                copy.wait()
        for copy in fetch(n):
            copy.wait()
        for j in range(nc):
            i = c ^ j
            v = loads[n % 2, j].astype(F32)
            if jobs[n][1] == "out":
                rows = pl.ds(mult((i // dm.ncs) * dm.pr, dm.pr), dm.pr)
                tall[n % 2, rows, pl.ds(mult(lax.rem(i, dm.ncs) * dm.pc, dm.pc), dm.pc)] = v
            else:
                wide[n % 2, :, pl.ds(mult(i * dm.pc, dm.pc), dm.pc)] = v
        for copy in store(n):
            copy.start()
    for n in (len(jobs) - 2, len(jobs) - 1):
        for copy in store(n):
            copy.wait()


def place_call(dm, done, vector):
    names = [k + str(layer) for k in ("o", "c", "a") for layer in reversed(range(LAYERS))]
    pieces = [p for name in names for p in done[name]]
    shapes = [(dm.pr, 3 * dm.d), (dm.pr, dm.d), (dm.pr, dm.ff), (dm.ffn, dm.d)]
    table = small_offsets(dm)[0]
    vectors = [(LAYERS, table[name + "0"][1]) for name, _ in SMALL] + [(1, dm.pr)] * 2
    return pl.pallas_call(
        functools.partial(place_body, dm),
        out_shape=[sds((LAYERS,) + shape, F32) for shape in shapes] + [sds(v, F32) for v in vectors],
        in_specs=[pl.BlockSpec(memory_space=pl.ANY)] * len(pieces) + [pl.BlockSpec(memory_space=pltpu.VMEM)],
        out_specs=[pl.BlockSpec(memory_space=pl.ANY)] * len(shapes)
        + [pl.BlockSpec(memory_space=pltpu.VMEM)] * len(vectors),
        scratch_shapes=[
            pltpu.VMEM((2, dm.nc, dm.pr, dm.pc), BF16),
            pltpu.VMEM((2, dm.pr, dm.ff), F32),
            pltpu.VMEM((2, dm.ffn, dm.d), F32),
            pltpu.SemaphoreType.DMA((2, dm.nc)),
            pltpu.SemaphoreType.DMA((2, 2)),
        ],
        compiler_params=pltpu.CompilerParams(vmem_limit_bytes=VMEM_BYTES),
    )(*pieces, vector)


def plane_bits(nc):
    bits = []
    bit = 2
    while bit < nc:
        bits.append(bit)
        bit *= 2
    return bits


def moving(moves):
    return lambda k: k.start(moves)


def spread(dm, first):
    bits = plane_bits(dm.nc)
    held = {0: first}
    if len(bits) == 2:
        one, two = bits
        held.update({bit: whole(first, ("ctx", bit)) for bit in (one, two, 1)})
        yield moving([held[one], held[two], held[1]])
        lead = (slice(None),) * (len(first.shape) - 2)
        cut = first.shape[-2] // 2
        low, high = lead + (pl.ds(0, cut),), lead + (pl.ds(cut, cut),)
        far = Move(
            first.shape, first.dtype,
            [([(None, held[two], low)], ("ctx", one), low), ([(None, held[one], high)], ("ctx", two), high)],
        )
        held[one ^ two] = far
        held.update({bit ^ 1: whole(held[bit], ("ctx", 1)) for bit in bits})
        yield moving([far, held[one ^ 1], held[two ^ 1]])
        held[one ^ two ^ 1] = whole(far, ("ctx", 1))
        yield moving([held[one ^ two ^ 1]])
    else:
        for bit in bits + [1]:
            new = {j ^ bit: whole(v, ("ctx", bit)) for j, v in held.items()}
            yield moving(list(new.values()))
            held.update(new)
    return [held[j] for j in range(dm.nc)]


def gather(dm, source):
    others = Move(
        (dm.nf - 1, dm.pr, dm.pc), BF16,
        [(source, ("fsdp", s), (s - 1,)) for s in range(1, dm.nf)],
    )
    yield moving([others])
    return (yield from spread(dm, others))


def plane_sum(dm, terms):
    bits = plane_bits(dm.nc)
    if len(bits) == 2:
        one, two = bits
        cut = dm.pr // 2
        shape = (dm.nf, cut, dm.pc)

        def part(t, first):
            return (t, slice(None), pl.ds(first, cut))

        def send(t, first, bit):
            return Move(shape, BF16, [([(None, terms, part(t, first))], ("ctx", bit), None)])

        far_x, own_x = send(3, 0, one), send(1, 0, one)
        far_y, own_y = send(3, cut, two), send(2, cut, two)
        yield moving([far_x, far_y, own_x, own_y])
        near = []

        def second(k):
            x = sum_section(k, [(terms, part(1, cut)), (far_y, None)], shape)
            near.append(whole(x, ("ctx", one)))
            k.start(near[:1])
            y = sum_section(k, [(terms, part(2, 0)), (far_x, None)], shape)
            near.append(whole(y, ("ctx", two)))
            k.start(near[1:])

        yield second
        return [
            [(terms, part(0, 0)), (own_x, None), (near[1], None)],
            [(terms, part(0, cut)), (near[0], None), (own_y, None)],
        ]
    at, index = terms, ()
    count = dm.nc // 2
    for n, _ in enumerate(bits):
        count //= 2
        shape = (count, dm.nf, dm.pr, dm.pc)
        away = Move(shape, BF16, [([(None, at, (pl.ds(count, count),))], ("ctx", bits[-1 - n]), None)])
        yield moving([away])
        if count > 1:
            made = []

            def add(k):
                made.append(sum_section(k, [(at, (pl.ds(0, count),)), (away, None)], shape))

            yield add
            at = made[0]
    return [[(at, (0,)), (away, (0,))]]


def reduce(dm, terms):
    parts = yield from plane_sum(dm, terms)
    rows = dm.pr // len(parts)
    totals = []
    others = []

    def along(k):
        for n, part in enumerate(parts):
            totals.append(sum_section(k, part, (dm.nf, rows, dm.pc)))
            others.append(
                Move(
                    (dm.nf - 1, rows, dm.pc), BF16,
                    [
                        ([(None, totals[n], (s,))], ("fsdp", dm.nf - s), (s - 1,))
                        for s in range(1, dm.nf)
                    ],
                )
            )
            k.start(others[n:])

    yield along
    mine = []

    def join(k):
        def body(*refs):
            out = refs[-1]
            for n in range(len(parts)):
                out[n * rows : (n + 1) * rows, :] = refs[n][...]

        sums = [
            sum_section(
                k, [(totals[n], (0,))] + [(others[n], (s,)) for s in range(dm.nf - 1)], (rows, dm.pc)
            )
            for n in range(len(parts))
        ]
        mine.append(k.section(body, [(v, "v") for v in sums], [sds((dm.pr, dm.pc), BF16)], [], 0)[0][0])

    stages = spread_later(dm, mine, join)
    return (yield from stages)


def spread_later(dm, mine, join):
    inner = None

    def first(k):
        nonlocal inner
        join(k)
        inner = spread(dm, mine[0])
        next(inner)(k)

    yield first
    return (yield from inner)


def reduce_small(dm, total):
    n = total.shape[-1]
    row = lambda s: (lambda: (ring(dm, lax.axis_index("fsdp"), s),))
    bit = 1
    state = [total]
    while bit < dm.nc:

        def step(k):
            other = whole(state[-1], ("ctx", bit))
            k.start([other])
            state.append(other)

        def add(k):
            other = state.pop()
            state.append(sum_section(k, [(state[-1], None), (other, None)], total.shape, F32))

        yield step
        yield add
        bit *= 2
    total = state[-1]
    others = Move(
        (dm.nf - 1, 1, n), F32,
        [([(None, total, row(s))], ("fsdp", dm.nf - s), (s - 1,)) for s in range(1, dm.nf)],
    )
    yield moving([others])
    made = []

    def last(k):
        terms = [(total, row(0))] + [(others, (s,)) for s in range(dm.nf - 1)]
        made.append(sum_section(k, terms, (1, n), F32))

    yield last
    return made[0]


class Flow:
    def __init__(self, dm):
        self.dm, self.live, self.done = dm, {}, {}
        self.ids = itertools.count()

    def kernel(self, *names):
        k = Kernel(self.dm, self.ids)
        self.go(k, *names)
        return k

    def add(self, name, transfer):
        self.live[name] = transfer

    def go(self, k, *names):
        for name in names:
            if name in self.live:
                try:
                    next(self.live[name])(k)
                except StopIteration as stop:
                    self.done[name] = stop.value
                    del self.live[name]

    def finish(self, k, name):
        while name in self.live:
            self.go(k, name)
        return self.done[name]


def local(acts, cotangent, pair_slots, segments, *tensors):
    (
        attn_gain, attn_shift, qkv_weight, qkv_bias, proj_weight, proj_bias, mlp_gain, mlp_shift,
        fc_weight, fc_bias, out_weight, out_bias, final_gain, final_shift,
    ) = tensors
    nf, nc = lax.axis_size("fsdp"), lax.axis_size("ctx")
    dm = dims_of(acts, fc_weight, nf, nc)
    c, f = lax.axis_index("ctx"), lax.axis_index("fsdp")
    small_size = small_offsets(dm)[1]

    seg = segments[0]
    cut_one = jnp.sum((seg == 0).astype(jnp.int32))
    cut_two = cut_one + jnp.sum((seg == 1).astype(jnp.int32))
    index = jnp.arange(nc, dtype=jnp.int32)
    others = jnp.bitwise_xor(c, index)
    lows = jnp.sum(jnp.where(others[:, None] == index[None, :], pair_slots[None, :], 0), axis=1)
    slots = jnp.sum(jnp.where(lows[None, :] == index[:, None], index[None, :], 0), axis=1)
    meta = jnp.concatenate([jnp.stack([c, f, cut_one, cut_two]).astype(jnp.int32), lows, slots])

    def source(kind, layer):
        def cols(first, last):
            at = jnp.clip(lax.axis_index("ctx"), first, last - 1) - first
            return (layer, pl.ds(0, dm.pr), pl.ds(mult(at * dm.pc, dm.pc), dm.pc))

        def place():
            at = lax.axis_index("ctx")
            row, col = (at // dm.ncs) * dm.pr, lax.rem(at, dm.ncs) * dm.pc
            return (layer, pl.ds(mult(row, dm.pr), dm.pr), pl.ds(mult(col, dm.pc), dm.pc))

        if kind == "attn":
            return [
                (lambda: lax.axis_index("ctx") < dm.nq, qkv_weight, lambda: cols(0, dm.nq)),
                (lambda: lax.axis_index("ctx") >= dm.nq, proj_weight, lambda: cols(dm.nq, nc)),
            ]
        if kind == "fc":
            return [(None, fc_weight, lambda: cols(0, nc))]
        return [(None, out_weight, place)]

    per_layer = (attn_gain, attn_shift, qkv_bias, proj_bias, mlp_gain, mlp_shift, fc_bias, out_bias)
    parts = [p[layer] for layer in range(LAYERS) for p in per_layer] + [final_gain, final_shift]
    packed = jnp.concatenate(parts).reshape(small_size // 128, 128)
    small_move = Move(
        (nf - 1,) + packed.shape, BF16,
        [([(None, packed, None)], ("fsdp", s), (s - 1,)) for s in range(1, nf)],
    )

    def other_core(v):
        return whole(v, ("ctx", 1))

    flow = Flow(dm)
    for layer in range(LAYERS):
        for kind, name in (("attn", "A"), ("fc", "C"), ("out", "O")):
            flow.add(name + str(layer), gather(dm, source(kind, layer)))

    k = flow.kernel()
    k.start([small_move])
    flow.go(k, "A0", "A0", "C0", "A0", "C0", "O0")
    flow.finish(k, "A0")
    k.run()
    backwards = jnp.concatenate([packed[None], value(small_move)])[::-1]
    small = lax.dynamic_slice_in_dim(jnp.concatenate([backwards, backwards]), nf - 1 - f, nf)
    small = small.reshape(nf, small_size).astype(F32)

    h = acts[0]
    kept = []
    k = flow.kernel("C0", "O0", "A1")
    n1, blocks = qkv_section(k, 0, h, small, qkv_weight, flow.done["A0"], meta)
    flow.go(k, "C0")
    k.run()
    vectors = {}
    for layer in range(LAYERS):
        tag, nxt = str(layer), str(layer + 1)
        last = layer + 1 == LAYERS
        twin = [other_core(n1)]
        k = flow.kernel("O" + tag, "A" + nxt, "C" + nxt) if not last else flow.kernel("C" + tag, "O" + tag)
        k.start(twin)
        saved, heads = attend_section(k, blocks, meta)
        flow.go(k, "C" + tag if last else "O" + tag)
        k.run()
        k = flow.kernel("A" + nxt, "O" + nxt, "C" + nxt) if not last else flow.kernel("O" + tag)
        attn = flow.done["A" + tag]
        ob, mid, n2 = proj_section(k, layer, h, small, proj_weight, heads, attn, meta)
        twin += [other_core(ob), other_core(n2)]
        k.start(twin[1:])
        u, act = fc_section(k, layer, n2, small, fc_weight, flow.finish(k, "C" + tag), meta)
        twin.append(other_core(act))
        k.start(twin[3:])
        nxt_h = out_section(k, layer, mid, act, small, out_weight, flow.finish(k, "O" + tag), meta)
        kept.append((h, n1, saved, ob, mid, n2, u, act, twin))
        h = nxt_h
        if not last:
            n1, blocks = qkv_section(k, layer + 1, h, small, qkv_weight, flow.finish(k, "A" + nxt), meta)
            k.run()

    weights = flow.done
    result, dh, gm, vectors["gf"], vectors["sf"] = top_section(k, h, cotangent[0], small)

    for layer in reversed(range(LAYERS)):
        tag, nxt = str(layer), str(layer + 1)
        o_, a_, k_ = "o" + nxt, "a" + nxt, "c" + nxt
        o, a, ck = "o" + tag, "a" + tag, "c" + tag
        h, n1, saved, ob, mid, n2, u, act, (n1_, ob_, n2_, act_) = kept[layer]
        gm_ = other_core(gm)
        k.start([gm_])
        du, vectors["bo" + tag], vectors["bf" + tag] = out_back_section(
            k, layer, gm, u, out_weight, weights["O" + tag], meta
        )
        flow.go(k, k_, k_)
        k.run()
        du_ = other_core(du)
        k = flow.kernel()
        k.start([du_])
        flow.go(k, a_)
        flow.add(o, reduce(dm, grad_section(k, "out", [(act, act_)], [(gm, gm_)])))
        flow.go(k, o)
        dmid, ga, vectors["bp" + tag], vectors["g2" + tag], vectors["s2" + tag] = fc_back_section(
            k, layer, du, dh, mid, small, fc_weight, weights["C" + tag], meta
        )
        k.run()
        k = flow.kernel(a_, o)
        ga_ = other_core(ga)
        k.start([ga_])
        grads = proj_back_section(k, layer, ga, proj_weight, weights["A" + tag], meta)
        flow.add(ck, reduce(dm, grad_section(k, "fc", [(n2, n2_)], [(du, du_)])))
        flow.go(k, ck)
        k.run()
        k = flow.kernel(o, ck, a_)
        blocks = attend_back_section(k, saved, grads, meta)
        flow.go(k, a_)
        k.run()
        k = flow.kernel(o, ck, a_)
        dh, gm, dqkv, vectors["bq" + tag], vectors["g1" + tag], vectors["s1" + tag] = qkv_back_section(
            k, layer, dmid, h, small, qkv_weight, blocks, weights["A" + tag], meta
        )
        dqkv_ = other_core(dqkv)
        k.start([dqkv_])
        flow.go(k, o, o)
        k.run()
        k = flow.kernel(ck)
        if layer == 0:
            shape = (nf, 1, small_size)
            rows = k.section(
                functools.partial(collect_body, dm),
                [(vectors[name], "v") for name in vector_names()],
                [sds(shape, F32)],
                [],
                0,
            )[0][0]
            flow.add("small", reduce_small(dm, rows))
            flow.go(k, "small")
        flow.add(
            a,
            reduce(dm, grad_section(k, "attn", [(n1, n1_), (ob, ob_)], [(dqkv, dqkv_), (ga, ga_)])),
        )
        flow.go(k, a)

    flow.go(k, "c0", "small", "small", "c0", "a0", "small", "small", "a0", "small", "small")
    for name in ("a1", "c1", "o1", "c0", "o0", "a0"):
        flow.finish(k, name)
    mine = flow.finish(k, "small")
    k.run()
    done = {name: [value(v) for v in flow.done[name]] for name in ("o0", "c0", "a0", "o1", "c1", "a1")}
    grads = place_call(dm, done, value(mine))
    qkv_grad, proj_grad, fc_grad, out_grad, g1, s1, bq, bp, g2, s2, bf, bo, gf, sf = grads
    return (
        value(result)[None], value(gm)[None], g1, s1, qkv_grad, bq, proj_grad, bp, g2, s2, fc_grad, bf,
        out_grad, bo, gf.reshape(-1), sf.reshape(-1),
    )


def solution(mesh):
    row = P("fsdp", "ctx", None)
    vec, mat = P(None, "fsdp"), P(None, "fsdp", None)
    tensors = (vec, vec, mat, vec, mat, vec, vec, vec, mat, vec, mat, vec, P("fsdp"), P("fsdp"))
    return jax.shard_map(
        local,
        mesh=mesh,
        in_specs=(row, row, P(), P("fsdp", None)) + tensors,
        out_specs=(row, row) + tensors,
        check_vma=False,
    )
```

```python
import collections
import functools
import itertools

import jax
import jax.numpy as jnp
from jax import lax
from jax.experimental import pallas as pl
from jax.experimental.pallas import tpu as pltpu
from jax.sharding import PartitionSpec as P

HEADS = 16
HEAD_DIM = 64
LAYERS = 2
EPS = 1e-05
NEG = -1e30
LOW = -1e29
F32 = jnp.float32
BF16 = jnp.bfloat16
VMEM_BYTES = 60 * 1024 * 1024

FIELDS = ("t", "d", "ff", "nf", "nc", "pr", "pc", "nq", "ncs", "ffn", "w", "hl", "rows", "half")
Dims = collections.namedtuple("Dims", FIELDS)


def dims_of(acts, fc_weight, nf, nc):
    t, d = acts.shape[1], acts.shape[2]
    ff = fc_weight.shape[2]
    pr, pc = d // nf, ff // nc
    return Dims(
        t=t, d=d, ff=ff, nf=nf, nc=nc, pr=pr, pc=pc, nq=3 * d // pc, ncs=d // pc, ffn=ff // nf,
        w=d // nc, hl=HEADS // nc, rows=t * nc, half=t // 2,
    )


SMALL = (("g1", 1), ("s1", 1), ("bq", 3), ("bp", 1), ("g2", 1), ("s2", 1), ("bf", 4), ("bo", 1))


def small_offsets(dm):
    table, at = {}, 0
    for layer in range(LAYERS):
        for name, _ in SMALL:
            size = {"bq": 3 * dm.pr, "bf": dm.ffn}.get(name, dm.pr)
            table[name + str(layer)] = (at, size)
            at += size
    for name in ("gf", "sf"):
        table[name] = (at, dm.pr)
        at += dm.pr
    return table, at


def send_blocks(dm, slot, shape):
    return Move(
        shape, BF16,
        [([(None, slot, (j,))], ("ctx", j) if j else None, (j,)) for j in range(dm.nc)],
    )


def vector_names():
    return [name + str(layer) for layer in range(LAYERS) for name, _ in SMALL] + ["gf", "sf"]


def mult(v, by):
    return pl.multiple_of(v, by)


def nn(a, b):
    return lax.dot_general(a, b, (((1,), (0,)), ((), ())), preferred_element_type=F32)


def nt(a, b):
    return lax.dot_general(a, b, (((1,), (1,)), ((), ())), preferred_element_type=F32)


def tn(a, b):
    return lax.dot_general(a, b, (((0,), (0,)), ((), ())), preferred_element_type=F32)


def col_sum(v):
    return jnp.sum(v.astype(F32), axis=0, keepdims=True)


def small_vec(dm, small_ref, name):
    at, size = small_offsets(dm)[0][name]
    return jnp.concatenate([small_ref[g : g + 1, at : at + size] for g in range(dm.nf)], axis=1)


def norm_parts(v):
    center = v - jnp.mean(v, axis=-1, keepdims=True)
    scale = lax.rsqrt(jnp.mean(center * center, axis=-1, keepdims=True) + EPS)
    return center * scale, scale


def norm(v, gain, shift):
    return norm_parts(v)[0] * gain + shift


def norm_back(v, gain, dy):
    xh, scale = norm_parts(v)
    e = dy * gain
    dv = scale * (
        e - jnp.mean(e, axis=-1, keepdims=True) - xh * jnp.mean(e * xh, axis=-1, keepdims=True)
    )
    return dv, col_sum(dy * xh), col_sum(dy)


K0 = 0.7978845608028654
K1 = 0.044715


def gelu(u):
    return 0.5 * u * (1.0 + jnp.tanh(K0 * (u + K1 * u * u * u)))


def gelu_slope(u):
    th = jnp.tanh(K0 * (u + K1 * u * u * u))
    return 0.5 * (1.0 + th) + 0.5 * u * (1.0 - th * th) * (K0 * (1.0 + 3.0 * K1 * u * u))


class Slot:
    def __init__(self, kind, at, like=None):
        self.kind, self.at, self.result = kind, at, None
        if like is not None:
            self.shape, self.dtype = like.shape, like.dtype


class Move:
    def __init__(self, shape, dtype, parts):
        self.shape, self.dtype, self.parts = shape, dtype, parts
        self.result = None


def whole(array, route):
    return Move(array.shape, array.dtype, [([(None, array, None)], route, None)])


def value(v):
    return v.result if isinstance(v, (Move, Slot)) else v


def at_of(ref, index):
    return ref if index is None else ref.at[index() if callable(index) else index]


class Kernel:
    def __init__(self, dm, ids=None):
        self.dm, self.ids = dm, ids
        self.arrays, self.in_specs, self.slots = [], [], {}
        self.outs, self.out_specs, self.out_slots = [], [], []
        self.scratch, self.keys, self.steps = [], {}, []
        self.moves, self.flops = [], 0

    def operand(self, a, place):
        if isinstance(a, (Slot, Move)) and a.result is None:
            return self.load(a) if isinstance(a, Move) and place == "v" else a
        a = value(a)
        key = (id(a), place)
        if key not in self.slots:
            spaces = {"v": pltpu.VMEM, "s": pltpu.SMEM, "a": pl.ANY}
            self.slots[key] = Slot("in", len(self.arrays))
            self.arrays.append(a)
            self.in_specs.append(pl.BlockSpec(memory_space=spaces[place]))
        return self.slots[key]

    def load(self, move):
        key = ("load", id(move))
        if key not in self.keys:
            self.keys[key] = Slot("scratch", len(self.scratch), move)
            self.scratch.append(pltpu.VMEM(move.shape, move.dtype))
            sem = self.buffer(("load", pltpu.SemaphoreType.DMA))

            def body(src, dst, sem):
                copy = pltpu.make_async_copy(src, dst, sem)
                copy.start()
                copy.wait()

            self.steps.append(("body", body, [move, self.keys[key], sem]))
        return self.keys[key]

    def output(self, out, space):
        slot = Slot("out", len(self.outs), out)
        self.outs.append(out)
        self.out_specs.append(pl.BlockSpec(memory_space=space))
        self.out_slots.append(slot)
        return slot

    def buffer(self, spec):
        key, spec = spec if isinstance(spec, tuple) else (None, spec)
        if key is None or key not in self.keys:
            slot = Slot("scratch", len(self.scratch))
            self.scratch.append(spec)
            if key is None:
                return slot
            self.keys[key] = slot
        return self.keys[key]

    def section(self, body, operands, outs, scratch, flops):
        refs = [self.operand(a, place) for a, place in operands]
        made = [self.output(o, pltpu.VMEM) for o in outs]
        bufs = [self.buffer(spec) for spec in scratch]
        self.steps.append(("body", body, refs + made + bufs))
        self.flops += flops
        return made, bufs

    def start(self, moves):
        for move in moves:
            parts = [
                ([(cond, self.operand(src, "a"), index) for cond, src, index in sources], route, place)
                for sources, route, place in move.parts
            ]
            slot = self.output(sds(move.shape, move.dtype), pl.ANY)
            self.moves.append((move, parts, slot))
            self.steps.append(("start", len(self.moves) - 1, None))

    def run(self, local=None):
        dm, moves, steps = self.dm, self.moves, self.steps
        order = {id(m): n for n, (m, _, _) in enumerate(moves)}
        count = sum(len(parts) for _, parts, _ in moves)
        routes = sorted({route for _, parts, _ in moves for _, route, _ in parts if route is not None})
        n_in, n_out, n_scratch = len(self.arrays), len(self.outs), len(self.scratch)
        sems = [pltpu.SemaphoreType.DMA((count,))] * 2 if count else []

        def kernel(*refs):
            groups = {"in": refs[:n_in], "out": refs[n_in : n_in + n_out], "scratch": refs[n_in + n_out :]}
            if count:
                send_sems, recv_sems = refs[-2:]
            c, f = lax.axis_index("ctx"), lax.axis_index("fsdp")

            def device(route, back=False):
                axis, by = route
                if axis == "ctx":
                    return (c ^ by, f)
                return (c, lax.rem(f + (dm.nf - by if back else by), dm.nf))

            if routes:
                barrier = pltpu.get_barrier_semaphore()
                for route in routes:
                    pl.semaphore_signal(
                        barrier, inc=1, device_id=device(route, True), device_id_type=pl.DeviceIdType.MESH
                    )
                pl.semaphore_wait(barrier, len(routes))

            def ref_of(src):
                if isinstance(src, Move):
                    src = moves[order[id(src)]][2]
                return groups[src.kind][src.at]

            at, copies = 0, []
            for _, parts, slot in moves:
                rows = []
                for sources, route, place in parts:
                    choices = []
                    for cond, src, index in sources:
                        ends = at_of(ref_of(src), index), at_of(ref_of(slot), place)
                        if route is None:
                            copy = pltpu.make_async_copy(*ends, recv_sems.at[at])
                        else:
                            copy = pltpu.make_async_remote_copy(
                                *ends, send_sems.at[at], recv_sems.at[at],
                                device_id=device(route), device_id_type=pl.DeviceIdType.MESH,
                            )
                        choices.append((cond, copy))
                    rows.append((route, choices))
                    at += 1
                copies.append(rows)
            arrived = set()

            def wait(n):
                if n in arrived:
                    return
                arrived.add(n)
                for route, choices in copies[n]:
                    copy = choices[0][1]
                    copy.wait() if route is None else copy.wait_recv()

            def ready(src):
                if isinstance(src, Move):
                    wait(order[id(src)])

            for kind, what, used in steps:
                if kind == "body":
                    for slot in used:
                        ready(slot)
                    what(*[ref_of(slot) for slot in used])
                    continue
                for sources, _, _ in moves[what][1]:
                    for _, src, _ in sources:
                        ready(src)
                for _, choices in copies[what]:
                    for cond, copy in choices:
                        if cond is None:
                            copy.start()
                        else:
                            pl.when(cond())(copy.start)
            for n in range(len(moves)):
                wait(n)
            for rows in copies:
                for route, choices in rows:
                    if route is not None:
                        choices[0][1].wait_send()

        params = {"collective_id": next(self.ids), "has_side_effects": True} if routes else {}
        moved = sum(a.size * a.dtype.itemsize for a in self.arrays + self.outs)
        results = pl.pallas_call(
            kernel,
            out_shape=self.outs,
            in_specs=self.in_specs,
            out_specs=self.out_specs,
            scratch_shapes=self.scratch + sems,
            compiler_params=pltpu.CompilerParams(vmem_limit_bytes=VMEM_BYTES, **params),
            cost_estimate=pl.CostEstimate(flops=self.flops, bytes_accessed=moved, transcendentals=0),
        )(*self.arrays)
        for slot, result in zip(self.out_slots, results):
            slot.result = result
        for move, _, slot in moves:
            move.result = slot.result


def sds(shape, dtype):
    return jax.ShapeDtypeStruct(shape, dtype)


class Pieces:
    def __init__(self, dm, layer, own, pieces, own_buf, piece_buf, sems, wanted):
        self.dm, self.wanted = dm, wanted
        self.own_copy = pltpu.make_async_copy(own.at[layer], own_buf, sems.at[dm.nc])
        self.copies = [
            pltpu.make_async_copy(pieces[j], piece_buf.at[j], sems.at[j]) for j in range(dm.nc)
        ]
        self.own, self.buf = own_buf, piece_buf

    def start(self):
        self.own_copy.start()
        for j in range(self.dm.nc):
            self.each(j, self.copies[j].start)

    def each(self, j, act):
        if self.wanted is None:
            act()
        else:
            pl.when(self.wanted(j))(act)

    def wait_own(self):
        self.own_copy.wait()

    def flat(self, j):
        return self.buf[j].reshape((self.dm.nf - 1) * self.dm.pr, self.dm.pc)


def piece_scratch(dm, own_shape):
    return [
        ("own" + str(own_shape), pltpu.VMEM(own_shape, BF16)),
        ("pieces", pltpu.VMEM((dm.nc, dm.nf - 1, dm.pr, dm.pc), BF16)),
        ("loads", pltpu.SemaphoreType.DMA((dm.nc + 1,))),
    ]


def ring(dm, f, s):
    return lax.rem(f + (dm.nf - s), dm.nf)


def relative(dm, f, src, dst):
    for s in range(dm.nf):
        at = mult(ring(dm, f, s) * dm.pr, dm.pr)
        dst[:, s * dm.pr : (s + 1) * dm.pr] = src[:, pl.ds(at, dm.pr)]


def take_heads(dm, ref, base, i):
    if dm.w % 128 == 0:
        return ref[:, pl.ds(mult(base + i * dm.w, 128), dm.w)]
    per = 128 // dm.w
    wide = ref[:, pl.ds(mult(base + (i // per) * 128, 128), 128)]
    part = wide[:, : dm.w]
    for at in range(1, per):
        part = jnp.where(lax.rem(i, per) == at, wide[:, at * dm.w : (at + 1) * dm.w], part)
    return part


def put_heads(dm, ref, base, blocks, at, c):
    if dm.w % 128 == 0:
        for j in range(dm.nc):
            ref[:, pl.ds(mult(base + (c ^ j) * dm.w, 128), dm.w)] = blocks[j][:, at : at + dm.w]
        return
    for j in range(0, dm.nc, 2):
        one, two = blocks[j][:, at : at + dm.w], blocks[j + 1][:, at : at + dm.w]
        even = lax.rem(c, 2) == 0
        pair = jnp.concatenate([jnp.where(even, one, two), jnp.where(even, two, one)], axis=1)
        ref[:, pl.ds(mult(base + ((c ^ j) // 2) * 128, 128), 128)] = pair


def qkv_body(dm, layer, *refs):
    nc = dm.nc
    meta, h, small, own = refs[:4]
    pieces = refs[4 : 4 + nc]
    n1, xr, y, bias, blocks, own_buf, piece_buf, sems = refs[4 + nc :]
    c, f = lax.axis_index("ctx"), lax.axis_index("fsdp")
    weight = Pieces(dm, layer, own, pieces, own_buf, piece_buf, sems, lambda j: (c ^ j) < dm.nq)
    weight.start()
    tag = str(layer)
    n1[...] = norm(
        h[...].astype(F32), small_vec(dm, small, "g1" + tag), small_vec(dm, small, "s1" + tag)
    ).astype(BF16)
    bias[...] = small_vec(dm, small, "bq" + tag)
    relative(dm, f, n1, xr)
    weight.wait_own()
    for j in range(nc):
        i = c ^ j

        @pl.when(i < dm.nq)
        def _():
            weight.copies[j].wait()
            at = pl.ds(mult(i * dm.pc, dm.pc), dm.pc)
            acc = nn(xr[:, dm.pr :], weight.flat(j)) + nn(xr[:, : dm.pr], own_buf[:, at])
            y[:, at] = (acc + bias[:, at]).astype(BF16)

    for j in range(nc):
        for third in range(3):
            blocks[j, :, third * dm.w : (third + 1) * dm.w] = take_heads(
                dm, y, third * dm.d, c ^ j
            )


def qkv_section(k, layer, h, small, own, pieces, meta):
    dm = k.dm
    shape = (dm.nc, dm.t, 3 * dm.w)
    (n1,), bufs = k.section(
        functools.partial(qkv_body, dm, layer),
        [(meta, "s"), (h, "v"), (small, "v"), (own, "a")] + [(p, "a") for p in pieces],
        [sds((dm.t, dm.d), BF16)],
        [
            ("xr", pltpu.VMEM((dm.t, dm.d), BF16)),
            pltpu.VMEM((dm.t, 3 * dm.d), BF16),
            pltpu.VMEM((1, 3 * dm.d), F32),
            pltpu.VMEM(shape, BF16),
        ]
        + piece_scratch(dm, (dm.pr, 3 * dm.d)),
        2 * dm.t * dm.d * 3 * dm.d,
    )
    blocks = send_blocks(dm, bufs[3], shape)
    k.start([blocks])
    return n1, blocks


def proj_body(dm, layer, *refs):
    nc = dm.nc
    meta, h, small, own, heads = refs[:5]
    pieces = refs[5 : 5 + nc]
    ob, mid, n2 = refs[5 + nc : 8 + nc]
    xr, bias, own_buf, piece_buf, sems = refs[8 + nc :]
    c, f = lax.axis_index("ctx"), lax.axis_index("fsdp")
    weight = Pieces(dm, layer, own, pieces, own_buf, piece_buf, sems, lambda j: (c ^ j) >= dm.nq)
    weight.start()
    tag = str(layer)
    bias[...] = small_vec(dm, small, "bp" + tag)
    put_heads(dm, ob, 0, [heads.at[j] for j in range(nc)], 0, c)
    relative(dm, f, ob, xr)
    weight.wait_own()
    for j in range(nc):
        i = c ^ j

        @pl.when(i >= dm.nq)
        def _():
            weight.copies[j].wait()
            at = pl.ds(mult((i - dm.nq) * dm.pc, dm.pc), dm.pc)
            acc = nn(xr[:, dm.pr :], weight.flat(j)) + nn(xr[:, : dm.pr], own_buf[:, at])
            mid[:, at] = h[:, at].astype(F32) + acc + bias[:, at]

    n2[...] = norm(
        mid[...], small_vec(dm, small, "g2" + tag), small_vec(dm, small, "s2" + tag)
    ).astype(BF16)


def proj_section(k, layer, h, small, own, heads, pieces, meta):
    dm = k.dm
    td = (dm.t, dm.d)
    return k.section(
        functools.partial(proj_body, dm, layer),
        [(meta, "s"), (h, "v"), (small, "v"), (own, "a"), (heads, "v")] + [(p, "a") for p in pieces],
        [sds(td, BF16), sds(td, F32), sds(td, BF16)],
        [("xr", pltpu.VMEM(td, BF16)), pltpu.VMEM((1, dm.d), F32)] + piece_scratch(dm, (dm.pr, dm.d)),
        2 * dm.t * dm.d * dm.d,
    )[0]


def fc_body(dm, layer, *refs):
    nc = dm.nc
    meta, n2, small, own = refs[:4]
    pieces = refs[4 : 4 + nc]
    u, act = refs[4 + nc : 6 + nc]
    xr, bias, own_buf, piece_buf, sems = refs[6 + nc :]
    c, f = lax.axis_index("ctx"), lax.axis_index("fsdp")
    weight = Pieces(dm, layer, own, pieces, own_buf, piece_buf, sems, None)
    weight.start()
    bias[...] = small_vec(dm, small, "bf" + str(layer))
    relative(dm, f, n2, xr)
    weight.wait_own()
    for j in range(nc):
        i = c ^ j
        weight.copies[j].wait()
        at = pl.ds(mult(i * dm.pc, dm.pc), dm.pc)
        acc = nn(xr[:, dm.pr :], weight.flat(j)) + nn(xr[:, : dm.pr], own_buf[:, at])
        acc = acc + bias[:, at]
        u[:, at] = acc
        act[:, at] = gelu(acc).astype(BF16)


def fc_section(k, layer, n2, small, own, pieces, meta):
    dm = k.dm
    return k.section(
        functools.partial(fc_body, dm, layer),
        [(meta, "s"), (n2, "v"), (small, "v"), (own, "a")] + [(p, "a") for p in pieces],
        [sds((dm.t, dm.ff), F32), sds((dm.t, dm.ff), BF16)],
        [("xr", pltpu.VMEM((dm.t, dm.d), BF16)), pltpu.VMEM((1, dm.ff), F32)]
        + piece_scratch(dm, (dm.pr, dm.ff)),
        2 * dm.t * dm.d * dm.ff,
    )[0]


def out_body(dm, layer, *refs):
    nc = dm.nc
    meta, mid, act, small, own = refs[:5]
    pieces = refs[5 : 5 + nc]
    h = refs[5 + nc]
    own_buf, piece_buf, sems = refs[6 + nc :]
    c, f = lax.axis_index("ctx"), lax.axis_index("fsdp")
    weight = Pieces(dm, layer, own, pieces, own_buf, piece_buf, sems, None)
    weight.start()
    weight.wait_own()
    mine = act[:, pl.ds(mult(f * dm.ffn, dm.ffn), dm.ffn)]
    h[...] = mid[...] + nn(mine, own_buf[...]) + small_vec(dm, small, "bo" + str(layer))
    for col in range(dm.ncs):
        acc = None
        for j in range(col, nc, dm.ncs):
            i = c ^ j
            weight.copies[j].wait()
            for s in range(1, dm.nf):
                at = mult(ring(dm, f, s) * dm.ffn + (i // dm.ncs) * dm.pr, dm.pr)
                part = nn(act[:, pl.ds(at, dm.pr)], piece_buf[j, s - 1])
                acc = part if acc is None else acc + part
        at = pl.ds(mult((lax.rem(c, dm.ncs) ^ col) * dm.pc, dm.pc), dm.pc)
        h[:, at] = h[:, at] + acc


def out_section(k, layer, mid, act, small, own, pieces, meta):
    dm = k.dm
    return k.section(
        functools.partial(out_body, dm, layer),
        [(meta, "s"), (mid, "v"), (act, "v"), (small, "v"), (own, "a")] + [(p, "a") for p in pieces],
        [sds((dm.t, dm.d), F32)],
        piece_scratch(dm, (dm.ffn, dm.d)),
        2 * dm.t * dm.d * dm.ff,
    )[0][0]


def chosen(dm, which, take):
    out = take(0).astype(F32)
    pick = jnp.full(out.shape, which, jnp.int32)
    for k in range(1, dm.nc):
        out = jnp.where(pick == k, take(k).astype(F32), out)
    return out.astype(BF16)


def sort_rows(dm, meta, blocks, dst):
    for piece in range(2 * dm.nc):
        slot = meta[4 + dm.nc + min(piece, 2 * dm.nc - 1 - piece)]
        half = 0 if piece < dm.nc else dm.half
        dst[piece * dm.half : (piece + 1) * dm.half, :] = chosen(
            dm, slot, lambda j: blocks[j, half : half + dm.half, :]
        )


def unsort_rows(dm, meta, src, blocks, at):
    cols = slice(at, at + src.shape[1])

    def rows(piece):
        return src[piece * dm.half : (piece + 1) * dm.half, :]

    for j in range(dm.nc):
        low = meta[4 + j]
        blocks[j, : dm.half, cols] = chosen(dm, low, rows)
        blocks[j, dm.half :, cols] = chosen(dm, low, lambda k: rows(2 * dm.nc - 1 - k))


def stack_heads(dm, v, scale=None):
    if scale is not None:
        v = v * scale
    if dm.hl == 1:
        return v
    lane = lax.broadcasted_iota(jnp.int32, v.shape, 1) // HEAD_DIM
    return jnp.concatenate([jnp.where(lane == k, v, 0.0).astype(v.dtype) for k in range(dm.hl)], axis=0)


def pick_heads(dm, v):
    if dm.hl == 1:
        return v
    rows = v.shape[0] // dm.hl
    lane = lax.broadcasted_iota(jnp.int32, (rows, v.shape[1]), 1) // HEAD_DIM
    out = v[:rows]
    for k in range(1, dm.hl):
        out = jnp.where(lane == k, v[k * rows : (k + 1) * rows], out)
    return out


def doc_start(first_cut, second_cut, row):
    return jnp.where(row < first_cut, 0, jnp.where(row < second_cut, first_cut, second_cut))


def tile_rows(dm, t, tq, cuts):
    row = t * tq + lax.rem(lax.broadcasted_iota(jnp.int32, (dm.hl * tq, 1), 0), tq)
    return row, doc_start(cuts[0], cuts[1], row)


TQ = 256
TK = 256


def attend_body(dm, *refs):
    nc, w = dm.nc, dm.w
    meta, blocks, packed, lse, mixed, heads = refs
    cuts = (meta[2], meta[3])
    tq, tk = min(TQ, dm.rows), min(TK, dm.rows)
    sort_rows(dm, meta, blocks, packed)

    def tile(t, carry):
        here = pl.ds(mult(t * tq, tq), tq)
        q = stack_heads(dm, packed[here, :w], HEAD_DIM**-0.5)
        row, start = tile_rows(dm, t, tq, cuts)

        def chunk(kb, state):
            top, mass, acc = state
            there = pl.ds(mult(kb * tk, tk), tk)
            col = kb * tk + lax.broadcasted_iota(jnp.int32, (1, tk), 1)
            s = jnp.where((col <= row) & (col >= start), nt(q, packed[there, w : 2 * w]), NEG)
            new_top = jnp.maximum(top, jnp.max(s, axis=1, keepdims=True))
            p = jnp.exp(s - new_top)
            fade = jnp.exp(top - new_top)
            mass = mass * fade + jnp.sum(p, axis=1, keepdims=True)
            acc = acc * fade + nn(p.astype(BF16), packed[there, 2 * w :])
            return new_top, mass, acc

        initial = (
            jnp.full((dm.hl * tq, 1), LOW, F32),
            jnp.zeros((dm.hl * tq, 1), F32),
            jnp.zeros((dm.hl * tq, w), F32),
        )
        top, mass, acc = lax.fori_loop(0, ((t + 1) * tq + tk - 1) // tk, chunk, initial)
        mixed[here, :] = pick_heads(dm, acc * (1.0 / mass))
        norms = top + jnp.log(mass)
        for k in range(dm.hl):
            lse[k, here, :] = norms[k * tq : (k + 1) * tq]
        return carry

    lax.fori_loop(0, dm.rows // tq, tile, 0)
    unsort_rows(dm, meta, mixed, heads, 0)


def attend_section(k, blocks, meta):
    dm = k.dm
    shape = (dm.nc, dm.t, dm.w)
    saved, bufs = k.section(
        functools.partial(attend_body, dm),
        [(meta, "s"), (blocks, "v")],
        [sds((dm.rows, 3 * dm.w), BF16), sds((dm.hl, dm.rows, 1), F32), sds((dm.rows, dm.w), F32)],
        [pltpu.VMEM(shape, BF16)],
        8 * dm.rows * dm.rows * dm.w,
    )
    heads = send_blocks(dm, bufs[0], shape)
    k.start([heads])
    return saved, heads


def attend_back_body(dm, *refs):
    nc, w = dm.nc, dm.w
    meta, packed, lse, mixed, grads, blocks, dmix, dq, dk, dv = refs
    cuts = (meta[2], meta[3])
    tq, tk = min(TQ, dm.rows), min(TK, dm.rows)
    scale = HEAD_DIM**-0.5
    sort_rows(dm, meta, grads, dmix)
    dk[...] = jnp.zeros_like(dk)
    dv[...] = jnp.zeros_like(dv)

    def tile(t, carry):
        here = pl.ds(mult(t * tq, tq), tq)
        q = stack_heads(dm, packed[here, :w], scale)
        do = stack_heads(dm, dmix[here, :])
        o = jnp.concatenate([mixed[here, :]] * dm.hl, axis=0)
        delta = jnp.sum(do.astype(F32) * o, axis=1, keepdims=True)
        norms = jnp.concatenate([lse[k, here, :] for k in range(dm.hl)], axis=0)
        row, start = tile_rows(dm, t, tq, cuts)

        def chunk(kb, acc):
            there = pl.ds(mult(kb * tk, tk), tk)
            col = kb * tk + lax.broadcasted_iota(jnp.int32, (1, tk), 1)
            keys = packed[there, w : 2 * w]
            s = jnp.where((col <= row) & (col >= start), nt(q, keys), NEG)
            p = jnp.exp(s - norms)
            dp = nt(do, packed[there, 2 * w :])
            ds = (p * (dp - delta)).astype(BF16)
            dv[there, :] += tn(p.astype(BF16), do)
            dk[there, :] += tn(ds, q)
            return acc + nn(ds, keys)

        acc = lax.fori_loop(
            0, ((t + 1) * tq + tk - 1) // tk, chunk, jnp.zeros((dm.hl * tq, w), F32)
        )
        dq[here, :] = pick_heads(dm, acc) * scale
        return carry

    lax.fori_loop(0, dm.rows // tq, tile, 0)
    for at, src in enumerate((dq, dk, dv)):
        unsort_rows(dm, meta, src, blocks, at * w)


def attend_back_section(k, saved, grads, meta):
    dm = k.dm
    shape = (dm.nc, dm.t, 3 * dm.w)
    _, bufs = k.section(
        functools.partial(attend_back_body, dm),
        [(meta, "s")] + [(a, "v") for a in saved] + [(grads, "v")],
        [],
        [pltpu.VMEM(shape, BF16), pltpu.VMEM((dm.rows, dm.w), BF16)]
        + [pltpu.VMEM((dm.rows, dm.w), F32)] * 3,
        16 * dm.rows * dm.rows * dm.w,
    )
    blocks = send_blocks(dm, bufs[0], shape)
    k.start([blocks])
    return blocks


def top_body(dm, h, cot, small, result, dh, low, g_gain, g_shift):
    gain = small_vec(dm, small, "gf")
    v = h[...]
    result[...] = norm(v, gain, small_vec(dm, small, "sf")).astype(BF16)
    dv, g_gain[...], g_shift[...] = norm_back(v, gain, cot[...].astype(F32))
    dh[...] = dv
    low[...] = dv.astype(BF16)


def top_section(k, h, cot, small):
    dm = k.dm
    td, vec = (dm.t, dm.d), sds((1, dm.d), F32)
    return k.section(
        functools.partial(top_body, dm),
        [(h, "v"), (cot, "v"), (small, "v")],
        [sds(td, BF16), sds(td, F32), sds(td, BF16), vec, vec],
        [],
        20 * dm.t * dm.d,
    )[0]


def out_back_body(dm, layer, *refs):
    nc = dm.nc
    meta, gm, u, own = refs[:4]
    pieces = refs[4 : 4 + nc]
    du, sum_gm, sum_du = refs[4 + nc : 7 + nc]
    gr, own_buf, piece_buf, sems = refs[7 + nc :]
    c, f = lax.axis_index("ctx"), lax.axis_index("fsdp")
    weight = Pieces(dm, layer, own, pieces, own_buf, piece_buf, sems, None)
    weight.start()
    sum_gm[...] = col_sum(gm[...])
    for col in range(dm.ncs):
        at = mult((lax.rem(c, dm.ncs) ^ col) * dm.pc, dm.pc)
        gr[:, col * dm.pc : (col + 1) * dm.pc] = gm[:, pl.ds(at, dm.pc)]

    def finish(dact, at):
        at = pl.ds(mult(at, dm.pr), dm.pr)
        low = (dact * gelu_slope(u[:, at])).astype(BF16)
        du[:, at] = low
        sum_du[:, at] = col_sum(low)

    weight.wait_own()
    for g in range(nc // dm.ncs):
        finish(nt(gm[...], own_buf[g * dm.pr : (g + 1) * dm.pr, :]), f * dm.ffn + g * dm.pr)
    for g in range(nc // dm.ncs):
        for col in range(dm.ncs):
            weight.copies[g * dm.ncs + col].wait()
        for s in range(1, dm.nf):
            dact = None
            for col in range(dm.ncs):
                part = nt(gr[:, col * dm.pc : (col + 1) * dm.pc], piece_buf[g * dm.ncs + col, s - 1])
                dact = part if dact is None else dact + part
            finish(dact, ring(dm, f, s) * dm.ffn + ((c // dm.ncs) ^ g) * dm.pr)


def out_back_section(k, layer, gm, u, own, pieces, meta):
    dm = k.dm
    return k.section(
        functools.partial(out_back_body, dm, layer),
        [(meta, "s"), (gm, "v"), (u, "v"), (own, "a")] + [(p, "a") for p in pieces],
        [sds((dm.t, dm.ff), BF16), sds((1, dm.d), F32), sds((1, dm.ff), F32)],
        [("xr", pltpu.VMEM((dm.t, dm.d), BF16))] + piece_scratch(dm, (dm.ffn, dm.d)),
        2 * dm.t * dm.d * dm.ff,
    )[0]


def cols_back(dm, f, c, weight, dy, first, last, acc, out):
    weight.wait_own()
    acc[:, : dm.pr] = nt(dy[...], weight.own[...])
    acc[:, dm.pr :] = jnp.zeros((dm.t, dm.d - dm.pr), F32)
    for j in range(dm.nc):
        i = c ^ j

        def step():
            weight.copies[j].wait()
            at = pl.ds(mult((i - first) * dm.pc, dm.pc), dm.pc)
            acc[:, dm.pr :] += nt(dy[:, at], weight.flat(j))

        weight.each(j, step)
    for s in range(dm.nf):
        at = mult(ring(dm, f, s) * dm.pr, dm.pr)
        out[:, pl.ds(at, dm.pr)] = acc[:, s * dm.pr : (s + 1) * dm.pr].astype(out.dtype)


def fc_back_body(dm, layer, *refs):
    nc = dm.nc
    meta, du, dh, mid, small, own = refs[:6]
    pieces = refs[6 : 6 + nc]
    dmid, ga, sum_ga, g_gain, g_shift = refs[6 + nc : 11 + nc]
    acc, dn, own_buf, piece_buf, sems = refs[11 + nc :]
    c, f = lax.axis_index("ctx"), lax.axis_index("fsdp")
    weight = Pieces(dm, layer, own, pieces, own_buf, piece_buf, sems, None)
    weight.start()
    cols_back(dm, f, c, weight, du, 0, nc, acc, dn)
    dv, g_gain[...], g_shift[...] = norm_back(
        mid[...], small_vec(dm, small, "g2" + str(layer)), dn[...]
    )
    total = dh[...] + dv
    dmid[...] = total
    low = total.astype(BF16)
    ga[...] = low
    sum_ga[...] = col_sum(low)


def fc_back_section(k, layer, du, dh, mid, small, own, pieces, meta):
    dm = k.dm
    td, vec = (dm.t, dm.d), sds((1, dm.d), F32)
    return k.section(
        functools.partial(fc_back_body, dm, layer),
        [(meta, "s"), (du, "v"), (dh, "v"), (mid, "v"), (small, "v"), (own, "a")]
        + [(p, "a") for p in pieces],
        [sds(td, F32), sds(td, BF16), vec, vec, vec],
        [("acc", pltpu.VMEM(td, F32)), ("dn", pltpu.VMEM(td, F32))] + piece_scratch(dm, (dm.pr, dm.ff)),
        2 * dm.t * dm.d * dm.ff,
    )[0]


def proj_back_body(dm, layer, *refs):
    nc = dm.nc
    meta, ga, own = refs[:3]
    pieces = refs[3 : 3 + nc]
    acc, dob, blocks, own_buf, piece_buf, sems = refs[3 + nc :]
    c, f = lax.axis_index("ctx"), lax.axis_index("fsdp")
    weight = Pieces(dm, layer, own, pieces, own_buf, piece_buf, sems, lambda j: (c ^ j) >= dm.nq)
    weight.start()
    cols_back(dm, f, c, weight, ga, dm.nq, nc, acc, dob)
    for j in range(nc):
        blocks[j] = take_heads(dm, dob, 0, c ^ j)


def proj_back_section(k, layer, ga, own, pieces, meta):
    dm = k.dm
    td, shape = (dm.t, dm.d), (dm.nc, dm.t, dm.w)
    _, bufs = k.section(
        functools.partial(proj_back_body, dm, layer),
        [(meta, "s"), (ga, "v"), (own, "a")] + [(p, "a") for p in pieces],
        [],
        [("acc", pltpu.VMEM(td, F32)), pltpu.VMEM(td, BF16), pltpu.VMEM(shape, BF16)]
        + piece_scratch(dm, (dm.pr, dm.d)),
        2 * dm.t * dm.d * dm.d,
    )
    blocks = send_blocks(dm, bufs[2], shape)
    k.start([blocks])
    return blocks


def qkv_back_body(dm, layer, *refs):
    nc = dm.nc
    meta, dmid, h, small, own, blocks = refs[:6]
    pieces = refs[6 : 6 + nc]
    dh, low, dqkv, sum_dqkv, g_gain, g_shift = refs[6 + nc : 12 + nc]
    acc, dn, own_buf, piece_buf, sems = refs[12 + nc :]
    blocks = [blocks.at[j] for j in range(nc)]
    c, f = lax.axis_index("ctx"), lax.axis_index("fsdp")
    weight = Pieces(dm, layer, own, pieces, own_buf, piece_buf, sems, lambda j: (c ^ j) < dm.nq)
    weight.start()
    for third in range(3):
        put_heads(dm, dqkv, third * dm.d, blocks, third * dm.w, c)
    sum_dqkv[...] = col_sum(dqkv[...])
    cols_back(dm, f, c, weight, dqkv, 0, dm.nq, acc, dn)
    dv, g_gain[...], g_shift[...] = norm_back(
        h[...].astype(F32), small_vec(dm, small, "g1" + str(layer)), dn[...]
    )
    total = dmid[...] + dv
    dh[...] = total
    low[...] = total.astype(BF16)


def qkv_back_section(k, layer, dmid, h, small, own, blocks, pieces, meta):
    dm = k.dm
    td, vec = (dm.t, dm.d), sds((1, dm.d), F32)
    return k.section(
        functools.partial(qkv_back_body, dm, layer),
        [(meta, "s"), (dmid, "v"), (h, "v"), (small, "v"), (own, "a"), (blocks, "v")]
        + [(p, "a") for p in pieces],
        [sds(td, F32), sds(td, BF16), sds((dm.t, 3 * dm.d), BF16), sds((1, 3 * dm.d), F32), vec, vec],
        [("acc", pltpu.VMEM(td, F32)), ("dn", pltpu.VMEM(td, F32))] + piece_scratch(dm, (dm.pr, 3 * dm.d)),
        2 * dm.t * dm.d * 3 * dm.d,
    )[0]


def sum_body(indices, *refs):
    n = len(indices)
    out, bufs, sems = refs[n], refs[n + 1 : 2 * n + 1], refs[2 * n + 1]
    copies = [
        pltpu.make_async_copy(at_of(ref, index), buf, sems.at[at])
        for at, (ref, index, buf) in enumerate(zip(refs, indices, bufs))
    ]
    for copy in copies:
        copy.start()
    for copy in copies:
        copy.wait()
    total = bufs[0][...].astype(F32)
    for buf in bufs[1:]:
        total = total + buf[...].astype(F32)
    out[...] = total.astype(out.dtype)


def sum_section(k, terms, shape, dtype=BF16, parts=None):
    bufs = [
        ("sum" + str((at, shape, dtype)), pltpu.VMEM(shape, dtype)) for at in range(len(terms))
    ]
    return k.section(
        functools.partial(sum_body, [index for _, index in terms]),
        [(src, "a") for src, _ in terms],
        [sds(shape, dtype)],
        bufs + [("sum" + str(len(terms)), pltpu.SemaphoreType.DMA((len(terms),)))],
        0,
    )[0][0]


def small_body(dm, packed, others, out):
    f = lax.axis_index("fsdp")
    out[pl.ds(f, 1), :] = packed[...]
    for s in range(1, dm.nf):
        out[pl.ds(ring(dm, f, s), 1), :] = others[s - 1]


def collect_body(dm, *refs):
    names, (table, _) = vector_names(), small_offsets(dm)
    for name, ref in zip(names, refs):
        at, size = table[name]
        for g in range(dm.nf):
            refs[-1][g, :, at : at + size] = ref[:, g * size : (g + 1) * size]


def grad_body(dm, kind, *refs):
    c, f = lax.axis_index("ctx"), lax.axis_index("fsdp")
    out, xt = refs[-2:]
    pairs = [refs[n : n + 2] for n in range(0, len(refs) - 2, 2)]
    lefts = pairs[: len(pairs) // 2]
    for n, pair in enumerate(lefts):
        depth = pair[0].shape[1]
        for half, ref in enumerate(pair):
            xt[n * depth : (n + 1) * depth, half * dm.t : (half + 1) * dm.t] = ref[...].T
    rights = pairs[len(pairs) // 2 :]

    def fill(t, row_base, row_step, pair, col):
        cols = pl.ds(mult(col * dm.pc, dm.pc), dm.pc)
        dy = jnp.concatenate([pair[0][:, cols], pair[1][:, cols]], axis=0)
        for s in range(dm.nf):
            at = mult(row_base + ring(dm, f, s) * row_step, dm.pr)
            out[t, s] = nn(xt[pl.ds(at, dm.pr), :], dy).astype(BF16)

    for t in reversed(range(dm.nc // 2)):
        i = c ^ (2 * t)
        if kind == "attn":
            pl.when(i < dm.nq)(lambda: fill(t, 0, dm.pr, rights[0], i))
            pl.when(i >= dm.nq)(lambda: fill(t, dm.d, dm.pr, rights[1], i - dm.nq))
        elif kind == "fc":
            fill(t, 0, dm.pr, rights[0], i)
        else:
            fill(t, (i // dm.ncs) * dm.pr, dm.ffn, rights[0], lax.rem(i, dm.ncs))


def grad_section(k, kind, lefts, rights):
    dm = k.dm
    return k.section(
        functools.partial(grad_body, dm, kind),
        [(a, "v") for pair in lefts + rights for a in pair],
        [sds((dm.nc // 2, dm.nf, dm.pr, dm.pc), BF16)],
        [("xt", pltpu.VMEM((dm.ff, 2 * dm.t), BF16))],
        2 * dm.t * dm.d * dm.ff,
    )[0][0]


def place_body(dm, *refs):
    nc = dm.nc
    jobs = [(layer, kind) for kind in ("out", "fc", "attn") for layer in reversed(range(LAYERS))]
    pieces = {job: refs[n * nc : (n + 1) * nc] for n, job in enumerate(jobs)}
    vector = refs[len(jobs) * nc]
    qkv, proj, fc, out = refs[len(jobs) * nc + 1 : len(jobs) * nc + 5]
    small = refs[len(jobs) * nc + 5 : -5]
    loads, wide, tall, load_sems, sems = refs[-5:]
    c = lax.axis_index("ctx")

    def fetch(n):
        return [
            pltpu.make_async_copy(pieces[jobs[n]][j], loads.at[n % 2, j], load_sems.at[n % 2, j])
            for j in range(nc)
        ]

    def store(n):
        layer, kind = jobs[n]
        buf, sem = (tall if kind == "out" else wide).at[n % 2], sems.at[n % 2]
        if kind == "attn":
            return [
                pltpu.make_async_copy(buf.at[:, pl.ds(0, 3 * dm.d)], qkv.at[layer], sem.at[0]),
                pltpu.make_async_copy(buf.at[:, pl.ds(3 * dm.d, dm.d)], proj.at[layer], sem.at[1]),
            ]
        return [pltpu.make_async_copy(buf, (out if kind == "out" else fc).at[layer], sem.at[0])]

    for copy in fetch(0):
        copy.start()
    for n, name in enumerate(vector_names()):
        at, size = small_offsets(dm)[0][name]
        row, ref = (n // len(SMALL), small[n % len(SMALL)])
        if row == LAYERS:
            row, ref = 0, small[len(SMALL) + n % len(SMALL)]
        ref[row : row + 1, :] = vector[:, at : at + size]
    for n in range(len(jobs)):
        if n + 1 < len(jobs):
            for copy in fetch(n + 1):
                copy.start()
        if n >= 2:
            for copy in store(n - 2):
                copy.wait()
        for copy in fetch(n):
            copy.wait()
        for j in range(nc):
            i = c ^ j
            v = loads[n % 2, j].astype(F32)
            if jobs[n][1] == "out":
                rows = pl.ds(mult((i // dm.ncs) * dm.pr, dm.pr), dm.pr)
                tall[n % 2, rows, pl.ds(mult(lax.rem(i, dm.ncs) * dm.pc, dm.pc), dm.pc)] = v
            else:
                wide[n % 2, :, pl.ds(mult(i * dm.pc, dm.pc), dm.pc)] = v
        for copy in store(n):
            copy.start()
    for n in (len(jobs) - 2, len(jobs) - 1):
        for copy in store(n):
            copy.wait()


def place_call(dm, done, vector):
    names = [k + str(layer) for k in ("o", "c", "a") for layer in reversed(range(LAYERS))]
    pieces = [p for name in names for p in done[name]]
    shapes = [(dm.pr, 3 * dm.d), (dm.pr, dm.d), (dm.pr, dm.ff), (dm.ffn, dm.d)]
    table = small_offsets(dm)[0]
    vectors = [(LAYERS, table[name + "0"][1]) for name, _ in SMALL] + [(1, dm.pr)] * 2
    return pl.pallas_call(
        functools.partial(place_body, dm),
        out_shape=[sds((LAYERS,) + shape, F32) for shape in shapes] + [sds(v, F32) for v in vectors],
        in_specs=[pl.BlockSpec(memory_space=pl.ANY)] * len(pieces) + [pl.BlockSpec(memory_space=pltpu.VMEM)],
        out_specs=[pl.BlockSpec(memory_space=pl.ANY)] * len(shapes)
        + [pl.BlockSpec(memory_space=pltpu.VMEM)] * len(vectors),
        scratch_shapes=[
            pltpu.VMEM((2, dm.nc, dm.pr, dm.pc), BF16),
            pltpu.VMEM((2, dm.pr, dm.ff), F32),
            pltpu.VMEM((2, dm.ffn, dm.d), F32),
            pltpu.SemaphoreType.DMA((2, dm.nc)),
            pltpu.SemaphoreType.DMA((2, 2)),
        ],
        compiler_params=pltpu.CompilerParams(vmem_limit_bytes=VMEM_BYTES),
    )(*pieces, vector)


def plane_bits(nc):
    bits = []
    bit = 2
    while bit < nc:
        bits.append(bit)
        bit *= 2
    return bits


def moving(moves):
    return lambda k: k.start(moves)


def spread(dm, first):
    bits = plane_bits(dm.nc)
    held = {0: first}
    if len(bits) == 2:
        one, two = bits
        held.update({bit: whole(first, ("ctx", bit)) for bit in (one, two, 1)})
        yield moving([held[one], held[two], held[1]])
        lead = (slice(None),) * (len(first.shape) - 2)
        cut = first.shape[-2] // 2
        low, high = lead + (pl.ds(0, cut),), lead + (pl.ds(cut, cut),)
        far = Move(
            first.shape, first.dtype,
            [([(None, held[two], low)], ("ctx", one), low), ([(None, held[one], high)], ("ctx", two), high)],
        )
        held[one ^ two] = far
        held.update({bit ^ 1: whole(held[bit], ("ctx", 1)) for bit in bits})
        yield moving([far, held[one ^ 1], held[two ^ 1]])
        held[one ^ two ^ 1] = whole(far, ("ctx", 1))
        yield moving([held[one ^ two ^ 1]])
    else:
        for bit in bits + [1]:
            new = {j ^ bit: whole(v, ("ctx", bit)) for j, v in held.items()}
            yield moving(list(new.values()))
            held.update(new)
    return [held[j] for j in range(dm.nc)]


def gather(dm, source):
    others = Move(
        (dm.nf - 1, dm.pr, dm.pc), BF16,
        [(source, ("fsdp", s), (s - 1,)) for s in range(1, dm.nf)],
    )
    yield moving([others])
    return (yield from spread(dm, others))


def plane_sum(dm, terms):
    bits = plane_bits(dm.nc)
    if len(bits) == 2:
        one, two = bits
        cut = dm.pr // 2
        shape = (dm.nf, cut, dm.pc)

        def part(t, first):
            return (t, slice(None), pl.ds(first, cut))

        def send(t, first, bit):
            return Move(shape, BF16, [([(None, terms, part(t, first))], ("ctx", bit), None)])

        far_x, own_x = send(3, 0, one), send(1, 0, one)
        far_y, own_y = send(3, cut, two), send(2, cut, two)
        yield moving([far_x, far_y, own_x, own_y])
        near = []

        def second(k):
            x = sum_section(k, [(terms, part(1, cut)), (far_y, None)], shape)
            near.append(whole(x, ("ctx", one)))
            k.start(near[:1])
            y = sum_section(k, [(terms, part(2, 0)), (far_x, None)], shape)
            near.append(whole(y, ("ctx", two)))
            k.start(near[1:])

        yield second
        return [
            [(terms, part(0, 0)), (own_x, None), (near[1], None)],
            [(terms, part(0, cut)), (near[0], None), (own_y, None)],
        ]
    at, index = terms, ()
    count = dm.nc // 2
    for n, _ in enumerate(bits):
        count //= 2
        shape = (count, dm.nf, dm.pr, dm.pc)
        away = Move(shape, BF16, [([(None, at, (pl.ds(count, count),))], ("ctx", bits[-1 - n]), None)])
        yield moving([away])
        if count > 1:
            made = []

            def add(k):
                made.append(sum_section(k, [(at, (pl.ds(0, count),)), (away, None)], shape))

            yield add
            at = made[0]
    return [[(at, (0,)), (away, (0,))]]


def reduce(dm, terms):
    parts = yield from plane_sum(dm, terms)
    rows = dm.pr // len(parts)
    totals = []
    others = []

    def along(k):
        for n, part in enumerate(parts):
            totals.append(sum_section(k, part, (dm.nf, rows, dm.pc)))
            others.append(
                Move(
                    (dm.nf - 1, rows, dm.pc), BF16,
                    [
                        ([(None, totals[n], (s,))], ("fsdp", dm.nf - s), (s - 1,))
                        for s in range(1, dm.nf)
                    ],
                )
            )
            k.start(others[n:])

    yield along
    mine = []

    def join(k):
        def body(*refs):
            out = refs[-1]
            for n in range(len(parts)):
                out[n * rows : (n + 1) * rows, :] = refs[n][...]

        sums = [
            sum_section(
                k, [(totals[n], (0,))] + [(others[n], (s,)) for s in range(dm.nf - 1)], (rows, dm.pc)
            )
            for n in range(len(parts))
        ]
        mine.append(k.section(body, [(v, "v") for v in sums], [sds((dm.pr, dm.pc), BF16)], [], 0)[0][0])

    stages = spread_later(dm, mine, join)
    return (yield from stages)


def spread_later(dm, mine, join):
    inner = None

    def first(k):
        nonlocal inner
        join(k)
        inner = spread(dm, mine[0])
        next(inner)(k)

    yield first
    return (yield from inner)


def reduce_small(dm, total):
    n = total.shape[-1]
    row = lambda s: (lambda: (ring(dm, lax.axis_index("fsdp"), s),))
    bit = 1
    state = [total]
    while bit < dm.nc:

        def step(k):
            other = whole(state[-1], ("ctx", bit))
            k.start([other])
            state.append(other)

        def add(k):
            other = state.pop()
            state.append(sum_section(k, [(state[-1], None), (other, None)], total.shape, F32))

        yield step
        yield add
        bit *= 2
    total = state[-1]
    others = Move(
        (dm.nf - 1, 1, n), F32,
        [([(None, total, row(s))], ("fsdp", dm.nf - s), (s - 1,)) for s in range(1, dm.nf)],
    )
    yield moving([others])
    made = []

    def last(k):
        terms = [(total, row(0))] + [(others, (s,)) for s in range(dm.nf - 1)]
        made.append(sum_section(k, terms, (1, n), F32))

    yield last
    return made[0]


class Flow:
    def __init__(self, dm):
        self.dm, self.live, self.done = dm, {}, {}
        self.ids = itertools.count()

    def kernel(self, *names):
        k = Kernel(self.dm, self.ids)
        self.go(k, *names)
        return k

    def add(self, name, transfer):
        self.live[name] = transfer

    def go(self, k, *names):
        for name in names:
            if name in self.live:
                try:
                    next(self.live[name])(k)
                except StopIteration as stop:
                    self.done[name] = stop.value
                    del self.live[name]

    def finish(self, k, name):
        while name in self.live:
            self.go(k, name)
        return self.done[name]


def local(acts, cotangent, pair_slots, segments, *tensors):
    (
        attn_gain, attn_shift, qkv_weight, qkv_bias, proj_weight, proj_bias, mlp_gain, mlp_shift,
        fc_weight, fc_bias, out_weight, out_bias, final_gain, final_shift,
    ) = tensors
    nf, nc = lax.axis_size("fsdp"), lax.axis_size("ctx")
    dm = dims_of(acts, fc_weight, nf, nc)
    c, f = lax.axis_index("ctx"), lax.axis_index("fsdp")
    small_size = small_offsets(dm)[1]

    seg = segments[0]
    cut_one = jnp.sum((seg == 0).astype(jnp.int32))
    cut_two = cut_one + jnp.sum((seg == 1).astype(jnp.int32))
    index = jnp.arange(nc, dtype=jnp.int32)
    others = jnp.bitwise_xor(c, index)
    lows = jnp.sum(jnp.where(others[:, None] == index[None, :], pair_slots[None, :], 0), axis=1)
    slots = jnp.sum(jnp.where(lows[None, :] == index[:, None], index[None, :], 0), axis=1)
    meta = jnp.concatenate([jnp.stack([c, f, cut_one, cut_two]).astype(jnp.int32), lows, slots])

    def source(kind, layer):
        def cols(first, last):
            at = jnp.clip(lax.axis_index("ctx"), first, last - 1) - first
            return (layer, pl.ds(0, dm.pr), pl.ds(mult(at * dm.pc, dm.pc), dm.pc))

        def place():
            at = lax.axis_index("ctx")
            row, col = (at // dm.ncs) * dm.pr, lax.rem(at, dm.ncs) * dm.pc
            return (layer, pl.ds(mult(row, dm.pr), dm.pr), pl.ds(mult(col, dm.pc), dm.pc))

        if kind == "attn":
            return [
                (lambda: lax.axis_index("ctx") < dm.nq, qkv_weight, lambda: cols(0, dm.nq)),
                (lambda: lax.axis_index("ctx") >= dm.nq, proj_weight, lambda: cols(dm.nq, nc)),
            ]
        if kind == "fc":
            return [(None, fc_weight, lambda: cols(0, nc))]
        return [(None, out_weight, place)]

    per_layer = (attn_gain, attn_shift, qkv_bias, proj_bias, mlp_gain, mlp_shift, fc_bias, out_bias)
    parts = [p[layer] for layer in range(LAYERS) for p in per_layer] + [final_gain, final_shift]
    packed = jnp.concatenate(parts).reshape(1, small_size).astype(F32)
    small_move = Move(
        (nf - 1,) + packed.shape, F32,
        [([(None, packed, None)], ("fsdp", s), (s - 1,)) for s in range(1, nf)],
    )

    def other_core(v):
        return whole(v, ("ctx", 1))

    flow = Flow(dm)
    for layer in range(LAYERS):
        for kind, name in (("attn", "A"), ("fc", "C"), ("out", "O")):
            flow.add(name + str(layer), gather(dm, source(kind, layer)))

    k = flow.kernel()
    k.start([small_move])
    flow.go(k, "A0", "A0", "C0")
    (small,) = k.section(
        functools.partial(small_body, dm),
        [(packed, "v"), (small_move, "v")],
        [sds((nf, small_size), F32)],
        [],
        0,
    )[0]
    flow.go(k, "A0", "C0", "O0", "A0")
    h = acts[0]
    n1, blocks = qkv_section(k, 0, h, small, qkv_weight, flow.finish(k, "A0"), meta)
    flow.go(k, "C0", "O0", "A1")
    twin = [other_core(n1)]
    k.start(twin)
    vectors, kept = {}, []
    for layer in range(LAYERS):
        tag, nxt = str(layer), str(layer + 1)
        last = layer + 1 == LAYERS
        saved, heads = attend_section(k, blocks, meta)
        if last:
            flow.go(k, "C" + tag, "O" + tag)
        else:
            flow.go(k, "C" + tag, "O" + tag, "A" + nxt, "C" + nxt)
            k.run()
            k = flow.kernel("O" + tag, "A" + nxt)
        attn = flow.done["A" + tag]
        ob, mid, n2 = proj_section(k, layer, h, small, proj_weight, heads, attn, meta)
        if last:
            flow.go(k, "O" + tag)
        twin += [other_core(ob), other_core(n2)]
        k.start(twin[1:])
        u, act = fc_section(k, layer, n2, small, fc_weight, flow.finish(k, "C" + tag), meta)
        twin.append(other_core(act))
        k.start(twin[3:])
        if not last:
            flow.go(k, "C" + nxt, "A" + nxt, "O" + nxt)
        nxt_h = out_section(k, layer, mid, act, small, out_weight, flow.finish(k, "O" + tag), meta)
        kept.append((h, n1, saved, ob, mid, n2, u, act, twin))
        h = nxt_h
        if not last:
            n1, blocks = qkv_section(k, layer + 1, h, small, qkv_weight, flow.finish(k, "A" + nxt), meta)
            twin = [other_core(n1)]
            k.start(twin)
            flow.go(k, "C" + nxt, "O" + nxt)

    weights = flow.done
    result, dh, gm, vectors["gf"], vectors["sf"] = top_section(k, h, cotangent[0], small)

    for layer in reversed(range(LAYERS)):
        tag, nxt = str(layer), str(layer + 1)
        o_, a_, k_ = "o" + nxt, "a" + nxt, "c" + nxt
        o, a, ck = "o" + tag, "a" + tag, "c" + tag
        h, n1, saved, ob, mid, n2, u, act, (n1_, ob_, n2_, act_) = kept[layer]
        gm_ = other_core(gm)
        k.start([gm_])
        du, vectors["bo" + tag], vectors["bf" + tag] = out_back_section(
            k, layer, gm, u, out_weight, weights["O" + tag], meta
        )
        du_ = other_core(du)
        k.start([du_])
        flow.go(k, k_, k_)
        k.run()

        k = flow.kernel(a_)
        flow.add(o, reduce(dm, grad_section(k, "out", [(act, act_)], [(gm, gm_)])))
        flow.go(k, o)
        dmid, ga, vectors["bp" + tag], vectors["g2" + tag], vectors["s2" + tag] = fc_back_section(
            k, layer, du, dh, mid, small, fc_weight, weights["C" + tag], meta
        )
        ga_ = other_core(ga)
        k.start([ga_])
        grads = proj_back_section(k, layer, ga, proj_weight, weights["A" + tag], meta)
        flow.go(k, a_)
        flow.add(ck, reduce(dm, grad_section(k, "fc", [(n2, n2_)], [(du, du_)])))
        flow.go(k, ck, o)
        if dm.rows * dm.nc > 2048 * 8:
            k.run()
            k = flow.kernel()
        blocks = attend_back_section(k, saved, grads, meta)
        flow.go(k, o, ck, a_, a_, a_)
        k.run()

        k = flow.kernel(ck, o)
        dh, gm, dqkv, vectors["bq" + tag], vectors["g1" + tag], vectors["s1" + tag] = qkv_back_section(
            k, layer, dmid, h, small, qkv_weight, blocks, weights["A" + tag], meta
        )
        dqkv_ = other_core(dqkv)
        k.start([dqkv_])
        flow.go(k, o, o)
        if layer == 0:
            shape = (nf, 1, small_size)
            rows = k.section(
                functools.partial(collect_body, dm),
                [(vectors[name], "v") for name in vector_names()],
                [sds(shape, F32)],
                [],
                0,
            )[0][0]
            flow.add("small", reduce_small(dm, rows))
            flow.go(k, "small")
        flow.add(
            a,
            reduce(dm, grad_section(k, "attn", [(n1, n1_), (ob, ob_)], [(dqkv, dqkv_), (ga, ga_)])),
        )
        flow.go(k, a, ck)

    flow.go(k, "small", "small", "a0", "c0", "small", "small", "a0", "c0", "small", "small")
    for name in ("a1", "c1", "o1", "c0", "o0", "a0"):
        flow.finish(k, name)
    mine = flow.finish(k, "small")
    k.run()
    done = {name: [value(v) for v in flow.done[name]] for name in ("o0", "c0", "a0", "o1", "c1", "a1")}
    grads = place_call(dm, done, value(mine))
    qkv_grad, proj_grad, fc_grad, out_grad, g1, s1, bq, bp, g2, s2, bf, bo, gf, sf = grads
    return (
        value(result)[None], value(gm)[None], g1, s1, qkv_grad, bq, proj_grad, bp, g2, s2, fc_grad, bf,
        out_grad, bo, gf.reshape(-1), sf.reshape(-1),
    )


def solution(mesh):
    row = P("fsdp", "ctx", None)
    vec, mat = P(None, "fsdp"), P(None, "fsdp", None)
    tensors = (vec, vec, mat, vec, mat, vec, vec, vec, mat, vec, mat, vec, P("fsdp"), P("fsdp"))
    return jax.shard_map(
        local,
        mesh=mesh,
        in_specs=(row, row, P(), P("fsdp", None)) + tensors,
        out_specs=(row, row) + tensors,
        check_vma=False,
    )
```

```python
import collections
import functools
import itertools

import jax
import jax.numpy as jnp
from jax import lax
from jax.experimental import pallas as pl
from jax.experimental.pallas import tpu as pltpu
from jax.sharding import PartitionSpec as P

HEADS = 16
HEAD_DIM = 64
LAYERS = 2
EPS = 1e-05
NEG = -1e30
LOW = -1e29
F32 = jnp.float32
BF16 = jnp.bfloat16
VMEM_BYTES = 61 * 1024 * 1024

FIELDS = ("t", "d", "ff", "nf", "nc", "pr", "pc", "nq", "ncs", "ffn", "w", "hl", "rows", "half")
Dims = collections.namedtuple("Dims", FIELDS)


def dims_of(acts, fc_weight, nf, nc):
    t, d = acts.shape[1], acts.shape[2]
    ff = fc_weight.shape[2]
    pr, pc = d // nf, ff // nc
    return Dims(
        t=t, d=d, ff=ff, nf=nf, nc=nc, pr=pr, pc=pc, nq=3 * d // pc, ncs=d // pc, ffn=ff // nf,
        w=d // nc, hl=HEADS // nc, rows=t * nc, half=t // 2,
    )


SMALL = (("g1", 1), ("s1", 1), ("bq", 3), ("bp", 1), ("g2", 1), ("s2", 1), ("bf", 4), ("bo", 1))


def small_offsets(dm):
    table, at = {}, 0
    for layer in range(LAYERS):
        for name, _ in SMALL:
            size = {"bq": 3 * dm.pr, "bf": dm.ffn}.get(name, dm.pr)
            table[name + str(layer)] = (at, size)
            at += size
    for name in ("gf", "sf"):
        table[name] = (at, dm.pr)
        at += dm.pr
    return table, at


def send_blocks(dm, slot, shape):
    return Move(
        shape, BF16,
        [([(None, slot, (j,))], ("ctx", j) if j else None, (j,)) for j in range(dm.nc)],
    )


def vector_names():
    return [name + str(layer) for layer in range(LAYERS) for name, _ in SMALL] + ["gf", "sf"]


def mult(v, by):
    return pl.multiple_of(v, by)


def nn(a, b):
    return lax.dot_general(a, b, (((1,), (0,)), ((), ())), preferred_element_type=F32)


def nt(a, b):
    return lax.dot_general(a, b, (((1,), (1,)), ((), ())), preferred_element_type=F32)


def tn(a, b):
    return lax.dot_general(a, b, (((0,), (0,)), ((), ())), preferred_element_type=F32)


def col_sum(v):
    return jnp.sum(v.astype(F32), axis=0, keepdims=True)


def small_vec(dm, small_ref, name):
    at, size = small_offsets(dm)[0][name]
    return jnp.concatenate([small_ref[g : g + 1, at : at + size] for g in range(dm.nf)], axis=1)


def norm_parts(v):
    center = v - jnp.mean(v, axis=-1, keepdims=True)
    scale = lax.rsqrt(jnp.mean(center * center, axis=-1, keepdims=True) + EPS)
    return center * scale, scale


def norm(v, gain, shift):
    return norm_parts(v)[0] * gain + shift


def norm_back(v, gain, dy):
    xh, scale = norm_parts(v)
    e = dy * gain
    dv = scale * (
        e - jnp.mean(e, axis=-1, keepdims=True) - xh * jnp.mean(e * xh, axis=-1, keepdims=True)
    )
    return dv, col_sum(dy * xh), col_sum(dy)


K0 = 0.7978845608028654
K1 = 0.044715


def gelu(u):
    return 0.5 * u * (1.0 + jnp.tanh(K0 * (u + K1 * u * u * u)))


def gelu_slope(u):
    th = jnp.tanh(K0 * (u + K1 * u * u * u))
    return 0.5 * (1.0 + th) + 0.5 * u * (1.0 - th * th) * (K0 * (1.0 + 3.0 * K1 * u * u))


class Slot:
    def __init__(self, kind, at, like=None):
        self.kind, self.at, self.result = kind, at, None
        if like is not None:
            self.shape, self.dtype = like.shape, like.dtype


class Move:
    def __init__(self, shape, dtype, parts, base=None):
        self.shape, self.dtype, self.parts, self.base = shape, dtype, parts, base
        self.result = None


def whole(array, route):
    return Move(array.shape, array.dtype, [([(None, array, None)], route, None)])


def value(v):
    return v.result if isinstance(v, (Move, Slot)) else v


def at_of(ref, index):
    return ref if index is None else ref.at[index() if callable(index) else index]


class Kernel:
    def __init__(self, dm, ids=None):
        self.dm, self.ids = dm, ids
        self.arrays, self.in_specs, self.slots = [], [], {}
        self.outs, self.out_specs, self.out_slots = [], [], []
        self.scratch, self.keys, self.steps = [], {}, []
        self.moves, self.flops = [], 0

    def operand(self, a, place):
        if isinstance(a, (Slot, Move)) and a.result is None:
            return self.load(a) if isinstance(a, Move) and place == "v" else a
        a = value(a)
        key = (id(a), place)
        if key not in self.slots:
            spaces = {"v": pltpu.VMEM, "s": pltpu.SMEM, "a": pl.ANY}
            self.slots[key] = Slot("in", len(self.arrays))
            self.arrays.append(a)
            self.in_specs.append(pl.BlockSpec(memory_space=spaces[place]))
        return self.slots[key]

    def load(self, move):
        key = ("load", id(move))
        if key not in self.keys:
            self.load_all([(move, key)])
        return self.keys[key]

    def load_all(self, wanted):
        srcs, dsts = [], []
        for array, key in wanted:
            key = key if isinstance(key, tuple) else (key, array.shape)
            if key not in self.keys:
                self.keys[key] = Slot("scratch", len(self.scratch), array)
                self.scratch.append(pltpu.VMEM(array.shape, array.dtype))
            srcs.append(self.operand(array, "a"))
            dsts.append(self.keys[key])
        n = len(wanted)

        def body(*refs):
            copies = [pltpu.make_async_copy(refs[i], refs[n + i], refs[2 * n].at[i]) for i in range(n)]
            for copy in copies:
                copy.start()
            for copy in copies:
                copy.wait()

        sems = self.buffer(("load" + str(n), pltpu.SemaphoreType.DMA((n,))))
        self.steps.append(("body", body, srcs + dsts + [sems]))
        return dsts

    def output(self, out, space):
        slot = Slot("out", len(self.outs), out)
        self.outs.append(out)
        self.out_specs.append(pl.BlockSpec(memory_space=space))
        self.out_slots.append(slot)
        return slot

    def buffer(self, spec):
        key, spec = spec if isinstance(spec, tuple) else (None, spec)
        if key is None or key not in self.keys:
            slot = Slot("scratch", len(self.scratch))
            self.scratch.append(spec)
            if key is None:
                return slot
            self.keys[key] = slot
        return self.keys[key]

    def section(self, body, operands, outs, scratch, flops):
        refs = [self.operand(a, place) for a, place in operands]
        made = [self.output(o, pltpu.VMEM) for o in outs]
        bufs = [self.buffer(spec) for spec in scratch]
        self.steps.append(("body", body, refs + made + bufs))
        self.flops += flops
        return made, bufs

    def start(self, moves):
        for move in moves:
            parts = [
                ([(cond, self.operand(src, "a"), index) for cond, src, index in sources], route, place)
                for sources, route, place in move.parts
            ]
            if move.base is None:
                slot = self.output(sds(move.shape, move.dtype), pl.ANY)
            else:
                slot = next(made for m, _, made in self.moves if m is move.base)
            self.moves.append((move, parts, slot))
            self.steps.append(("start", len(self.moves) - 1, None))

    def run(self, local=None):
        dm, moves, steps = self.dm, self.moves, self.steps
        order = {id(m): n for n, (m, _, _) in enumerate(moves)}
        count = sum(len(parts) for _, parts, _ in moves)
        routes = sorted({route for _, parts, _ in moves for _, route, _ in parts if route is not None})
        n_in, n_out, n_scratch = len(self.arrays), len(self.outs), len(self.scratch)
        sems = [pltpu.SemaphoreType.DMA((count,))] * 2 if count else []

        def kernel(*refs):
            groups = {"in": refs[:n_in], "out": refs[n_in : n_in + n_out], "scratch": refs[n_in + n_out :]}
            if count:
                send_sems, recv_sems = refs[-2:]
            c, f = lax.axis_index("ctx"), lax.axis_index("fsdp")

            def device(route, back=False):
                axis, by = route
                if axis == "ctx":
                    return (c ^ by, f)
                return (c, lax.rem(f + (dm.nf - by if back else by), dm.nf))

            if routes:
                barrier = pltpu.get_barrier_semaphore()
                for route in routes:
                    pl.semaphore_signal(
                        barrier, inc=1, device_id=device(route, True), device_id_type=pl.DeviceIdType.MESH
                    )
                pl.semaphore_wait(barrier, len(routes))

            def ref_of(src):
                if isinstance(src, Move):
                    src = moves[order[id(src)]][2]
                return groups[src.kind][src.at]

            at, copies = 0, []
            for _, parts, slot in moves:
                rows = []
                for sources, route, place in parts:
                    choices = []
                    for cond, src, index in sources:
                        ends = at_of(ref_of(src), index), at_of(ref_of(slot), place)
                        if route is None:
                            copy = pltpu.make_async_copy(*ends, recv_sems.at[at])
                        else:
                            copy = pltpu.make_async_remote_copy(
                                *ends, send_sems.at[at], recv_sems.at[at],
                                device_id=device(route), device_id_type=pl.DeviceIdType.MESH,
                            )
                        choices.append((cond, copy))
                    rows.append((route, choices))
                    at += 1
                copies.append(rows)
            arrived = set()

            def wait(n):
                if n in arrived:
                    return
                arrived.add(n)
                for route, choices in copies[n]:
                    copy = choices[0][1]
                    copy.wait() if route is None else copy.wait_recv()

            def ready(src):
                if isinstance(src, Move):
                    wait(order[id(src)])

            for kind, what, used in steps:
                if kind == "body":
                    for slot in used:
                        ready(slot)
                        for n, (m, _, _) in enumerate(moves):
                            if m.base is slot:
                                wait(n)
                    what(*[ref_of(slot) for slot in used])
                    continue
                for sources, _, _ in moves[what][1]:
                    for _, src, _ in sources:
                        ready(src)
                for _, choices in copies[what]:
                    for cond, copy in choices:
                        if cond is None:
                            copy.start()
                        else:
                            pl.when(cond())(copy.start)
            for n in range(len(moves)):
                wait(n)
            for rows in copies:
                for route, choices in rows:
                    if route is not None:
                        choices[0][1].wait_send()

        params = {"collective_id": next(self.ids), "has_side_effects": True} if routes else {}
        moved = sum(a.size * a.dtype.itemsize for a in self.arrays + self.outs)
        results = pl.pallas_call(
            kernel,
            out_shape=self.outs,
            in_specs=self.in_specs,
            out_specs=self.out_specs,
            scratch_shapes=self.scratch + sems,
            compiler_params=pltpu.CompilerParams(vmem_limit_bytes=VMEM_BYTES, **params),
            cost_estimate=pl.CostEstimate(flops=self.flops, bytes_accessed=moved, transcendentals=0),
        )(*self.arrays)
        for slot, result in zip(self.out_slots, results):
            slot.result = result
        for move, _, slot in moves:
            move.result = slot.result


def sds(shape, dtype):
    return jax.ShapeDtypeStruct(shape, dtype)


class Pieces:
    def __init__(self, dm, layer, own, pieces, own_buf, piece_buf, sems, wanted):
        self.dm, self.wanted = dm, wanted
        self.own_copy = pltpu.make_async_copy(own.at[layer], own_buf, sems.at[dm.nc])
        self.copies = [
            pltpu.make_async_copy(pieces[j], piece_buf.at[j], sems.at[j]) for j in range(dm.nc)
        ]
        self.own, self.buf = own_buf, piece_buf

    def start(self):
        self.own_copy.start()
        for j in range(self.dm.nc):
            self.each(j, self.copies[j].start)

    def each(self, j, act):
        if self.wanted is None:
            act()
        else:
            pl.when(self.wanted(j))(act)

    def wait_own(self):
        self.own_copy.wait()

    def flat(self, j):
        return self.buf[j].reshape((self.dm.nf - 1) * self.dm.pr, self.dm.pc)


def piece_scratch(dm, own_shape):
    return [
        ("own" + str(own_shape), pltpu.VMEM(own_shape, BF16)),
        ("pieces", pltpu.VMEM((dm.nc, dm.nf - 1, dm.pr, dm.pc), BF16)),
        ("loads", pltpu.SemaphoreType.DMA((dm.nc + 1,))),
    ]


def ring(dm, f, s):
    return lax.rem(f + (dm.nf - s), dm.nf)


def relative(dm, f, src, dst):
    for s in range(dm.nf):
        at = mult(ring(dm, f, s) * dm.pr, dm.pr)
        dst[:, s * dm.pr : (s + 1) * dm.pr] = src[:, pl.ds(at, dm.pr)]


def take_heads(dm, ref, base, i):
    if dm.w % 128 == 0:
        return ref[:, pl.ds(mult(base + i * dm.w, 128), dm.w)]
    per = 128 // dm.w
    wide = ref[:, pl.ds(mult(base + (i // per) * 128, 128), 128)]
    part = wide[:, : dm.w]
    for at in range(1, per):
        part = jnp.where(lax.rem(i, per) == at, wide[:, at * dm.w : (at + 1) * dm.w], part)
    return part


def put_heads(dm, ref, base, blocks, at, c):
    if dm.w % 128 == 0:
        for j in range(dm.nc):
            ref[:, pl.ds(mult(base + (c ^ j) * dm.w, 128), dm.w)] = blocks[j][:, at : at + dm.w]
        return
    for j in range(0, dm.nc, 2):
        one, two = blocks[j][:, at : at + dm.w], blocks[j + 1][:, at : at + dm.w]
        even = lax.rem(c, 2) == 0
        pair = jnp.concatenate([jnp.where(even, one, two), jnp.where(even, two, one)], axis=1)
        ref[:, pl.ds(mult(base + ((c ^ j) // 2) * 128, 128), 128)] = pair


def qkv_body(dm, layer, *refs):
    nc = dm.nc
    meta, h, small, own = refs[:4]
    pieces = refs[4 : 4 + nc]
    n1, xr, y, bias, blocks, own_buf, piece_buf, sems = refs[4 + nc :]
    c, f = lax.axis_index("ctx"), lax.axis_index("fsdp")
    weight = Pieces(dm, layer, own, pieces, own_buf, piece_buf, sems, lambda j: (c ^ j) < dm.nq)
    weight.start()
    tag = str(layer)
    n1[...] = norm(
        h[...].astype(F32), small_vec(dm, small, "g1" + tag), small_vec(dm, small, "s1" + tag)
    ).astype(BF16)
    bias[...] = small_vec(dm, small, "bq" + tag)
    relative(dm, f, n1, xr)
    weight.wait_own()
    for j in range(nc):
        i = c ^ j

        @pl.when(i < dm.nq)
        def _():
            weight.copies[j].wait()
            at = pl.ds(mult(i * dm.pc, dm.pc), dm.pc)
            acc = nn(xr[:, dm.pr :], weight.flat(j)) + nn(xr[:, : dm.pr], own_buf[:, at])
            y[:, at] = (acc + bias[:, at]).astype(BF16)

    for j in range(nc):
        for third in range(3):
            blocks[j, :, third * dm.w : (third + 1) * dm.w] = take_heads(
                dm, y, third * dm.d, c ^ j
            )


def qkv_section(k, layer, h, small, own, pieces, meta):
    dm = k.dm
    shape = (dm.nc, dm.t, 3 * dm.w)
    (n1,), bufs = k.section(
        functools.partial(qkv_body, dm, layer),
        [(meta, "s"), (h, "v"), (small, "v"), (own, "a")] + [(p, "a") for p in pieces],
        [sds((dm.t, dm.d), BF16)],
        [
            ("xr", pltpu.VMEM((dm.t, dm.d), BF16)),
            pltpu.VMEM((dm.t, 3 * dm.d), BF16),
            pltpu.VMEM((1, 3 * dm.d), F32),
            pltpu.VMEM(shape, BF16),
        ]
        + piece_scratch(dm, (dm.pr, 3 * dm.d)),
        2 * dm.t * dm.d * 3 * dm.d,
    )
    blocks = send_blocks(dm, bufs[3], shape)
    k.start([blocks])
    return n1, blocks


def proj_body(dm, layer, *refs):
    nc = dm.nc
    meta, h, small, own, heads = refs[:5]
    pieces = refs[5 : 5 + nc]
    ob, mid, n2 = refs[5 + nc : 8 + nc]
    xr, bias, own_buf, piece_buf, sems = refs[8 + nc :]
    c, f = lax.axis_index("ctx"), lax.axis_index("fsdp")
    weight = Pieces(dm, layer, own, pieces, own_buf, piece_buf, sems, lambda j: (c ^ j) >= dm.nq)
    weight.start()
    tag = str(layer)
    bias[...] = small_vec(dm, small, "bp" + tag)
    put_heads(dm, ob, 0, [heads.at[j] for j in range(nc)], 0, c)
    relative(dm, f, ob, xr)
    weight.wait_own()
    for j in range(nc):
        i = c ^ j

        @pl.when(i >= dm.nq)
        def _():
            weight.copies[j].wait()
            at = pl.ds(mult((i - dm.nq) * dm.pc, dm.pc), dm.pc)
            acc = nn(xr[:, dm.pr :], weight.flat(j)) + nn(xr[:, : dm.pr], own_buf[:, at])
            mid[:, at] = h[:, at].astype(F32) + acc + bias[:, at]

    n2[...] = norm(
        mid[...], small_vec(dm, small, "g2" + tag), small_vec(dm, small, "s2" + tag)
    ).astype(BF16)


def proj_section(k, layer, h, small, own, heads, pieces, meta):
    dm = k.dm
    td = (dm.t, dm.d)
    return k.section(
        functools.partial(proj_body, dm, layer),
        [(meta, "s"), (h, "v"), (small, "v"), (own, "a"), (heads, "v")] + [(p, "a") for p in pieces],
        [sds(td, BF16), sds(td, F32), sds(td, BF16)],
        [("xr", pltpu.VMEM(td, BF16)), pltpu.VMEM((1, dm.d), F32)] + piece_scratch(dm, (dm.pr, dm.d)),
        2 * dm.t * dm.d * dm.d,
    )[0]


def fc_body(dm, layer, *refs):
    nc = dm.nc
    meta, n2, small, own = refs[:4]
    pieces = refs[4 : 4 + nc]
    u, act = refs[4 + nc : 6 + nc]
    xr, bias, own_buf, piece_buf, sems = refs[6 + nc :]
    c, f = lax.axis_index("ctx"), lax.axis_index("fsdp")
    weight = Pieces(dm, layer, own, pieces, own_buf, piece_buf, sems, None)
    weight.start()
    bias[...] = small_vec(dm, small, "bf" + str(layer))
    relative(dm, f, n2, xr)
    weight.wait_own()
    for j in range(nc):
        i = c ^ j
        weight.copies[j].wait()
        at = pl.ds(mult(i * dm.pc, dm.pc), dm.pc)
        acc = nn(xr[:, dm.pr :], weight.flat(j)) + nn(xr[:, : dm.pr], own_buf[:, at])
        acc = acc + bias[:, at]
        u[:, at] = acc
        act[:, at] = gelu(acc).astype(BF16)


def fc_section(k, layer, n2, small, own, pieces, meta):
    dm = k.dm
    return k.section(
        functools.partial(fc_body, dm, layer),
        [(meta, "s"), (n2, "v"), (small, "v"), (own, "a")] + [(p, "a") for p in pieces],
        [sds((dm.t, dm.ff), F32), sds((dm.t, dm.ff), BF16)],
        [("xr", pltpu.VMEM((dm.t, dm.d), BF16)), pltpu.VMEM((1, dm.ff), F32)]
        + piece_scratch(dm, (dm.pr, dm.ff)),
        2 * dm.t * dm.d * dm.ff,
    )[0]


def out_body(dm, layer, *refs):
    nc = dm.nc
    meta, mid, act, small, own = refs[:5]
    pieces = refs[5 : 5 + nc]
    h = refs[5 + nc]
    own_buf, piece_buf, sems = refs[6 + nc :]
    c, f = lax.axis_index("ctx"), lax.axis_index("fsdp")
    weight = Pieces(dm, layer, own, pieces, own_buf, piece_buf, sems, None)
    weight.start()
    weight.wait_own()
    mine = act[:, pl.ds(mult(f * dm.ffn, dm.ffn), dm.ffn)]
    h[...] = mid[...] + nn(mine, own_buf[...]) + small_vec(dm, small, "bo" + str(layer))
    for col in range(dm.ncs):
        acc = None
        for j in range(col, nc, dm.ncs):
            i = c ^ j
            weight.copies[j].wait()
            for s in range(1, dm.nf):
                at = mult(ring(dm, f, s) * dm.ffn + (i // dm.ncs) * dm.pr, dm.pr)
                part = nn(act[:, pl.ds(at, dm.pr)], piece_buf[j, s - 1])
                acc = part if acc is None else acc + part
        at = pl.ds(mult((lax.rem(c, dm.ncs) ^ col) * dm.pc, dm.pc), dm.pc)
        h[:, at] = h[:, at] + acc


def out_section(k, layer, mid, act, small, own, pieces, meta):
    dm = k.dm
    return k.section(
        functools.partial(out_body, dm, layer),
        [(meta, "s"), (mid, "v"), (act, "v"), (small, "v"), (own, "a")] + [(p, "a") for p in pieces],
        [sds((dm.t, dm.d), F32)],
        piece_scratch(dm, (dm.ffn, dm.d)),
        2 * dm.t * dm.d * dm.ff,
    )[0][0]


def chosen(dm, which, take):
    out = take(0).astype(F32)
    pick = jnp.full(out.shape, which, jnp.int32)
    for k in range(1, dm.nc):
        out = jnp.where(pick == k, take(k).astype(F32), out)
    return out.astype(BF16)


def sort_rows(dm, meta, blocks, dst):
    for piece in range(2 * dm.nc):
        slot = meta[4 + dm.nc + min(piece, 2 * dm.nc - 1 - piece)]
        half = 0 if piece < dm.nc else dm.half
        dst[piece * dm.half : (piece + 1) * dm.half, :] = chosen(
            dm, slot, lambda j: blocks[j, half : half + dm.half, :]
        )


def unsort_rows(dm, meta, src, blocks, at):
    cols = slice(at, at + src.shape[1])

    def rows(piece):
        return src[piece * dm.half : (piece + 1) * dm.half, :]

    for j in range(dm.nc):
        low = meta[4 + j]
        blocks[j, : dm.half, cols] = chosen(dm, low, rows)
        blocks[j, dm.half :, cols] = chosen(dm, low, lambda k: rows(2 * dm.nc - 1 - k))


def stack_heads(dm, v, scale=None):
    if scale is not None:
        v = v * scale
    if dm.hl == 1:
        return v
    lane = lax.broadcasted_iota(jnp.int32, v.shape, 1) // HEAD_DIM
    return jnp.concatenate([jnp.where(lane == k, v, 0.0).astype(v.dtype) for k in range(dm.hl)], axis=0)


def pick_heads(dm, v):
    if dm.hl == 1:
        return v
    rows = v.shape[0] // dm.hl
    lane = lax.broadcasted_iota(jnp.int32, (rows, v.shape[1]), 1) // HEAD_DIM
    out = v[:rows]
    for k in range(1, dm.hl):
        out = jnp.where(lane == k, v[k * rows : (k + 1) * rows], out)
    return out


def doc_start(first_cut, second_cut, row):
    return jnp.where(row < first_cut, 0, jnp.where(row < second_cut, first_cut, second_cut))


def tile_rows(dm, t, tq, cuts):
    row = t * tq + lax.rem(lax.broadcasted_iota(jnp.int32, (dm.hl * tq, 1), 0), tq)
    return row, doc_start(cuts[0], cuts[1], row)


TILE = 512


def attend_body(dm, *refs):
    nc, w = dm.nc, dm.w
    meta, blocks, packed, lse, mixed, heads = refs
    cuts = (meta[2], meta[3])
    tq = tk = min(TILE, dm.rows)
    sort_rows(dm, meta, blocks, packed)

    def tile(t, carry):
        here = pl.ds(mult(t * tq, tq), tq)
        q = stack_heads(dm, packed[here, :w], HEAD_DIM**-0.5)
        row, start = tile_rows(dm, t, tq, cuts)

        def chunk(kb, state, last=False):
            top, mass, acc = state
            there = pl.ds(mult(kb * tk, tk), tk)
            col = kb * tk + lax.broadcasted_iota(jnp.int32, (1, tk), 1)
            seen = (col <= row) & (col >= start) if last else col >= start
            s = jnp.where(seen, nt(q, packed[there, w : 2 * w]), NEG)
            new_top = jnp.maximum(top, jnp.max(s, axis=1, keepdims=True))
            p = jnp.exp(s - new_top)
            fade = jnp.exp(top - new_top)
            mass = mass * fade + jnp.sum(p, axis=1, keepdims=True)
            acc = acc * fade + nn(p.astype(BF16), packed[there, 2 * w :])
            return new_top, mass, acc

        initial = (
            jnp.full((dm.hl * tq, 1), LOW, F32),
            jnp.zeros((dm.hl * tq, 1), F32),
            jnp.zeros((dm.hl * tq, w), F32),
        )
        top, mass, acc = chunk(t, lax.fori_loop(0, t, chunk, initial), True)
        mixed[here, :] = pick_heads(dm, acc * (1.0 / mass))
        norms = top + jnp.log(mass)
        for k in range(dm.hl):
            lse[here, k : k + 1] = norms[k * tq : (k + 1) * tq]
        return carry

    lax.fori_loop(0, dm.rows // tq, tile, 0)
    unsort_rows(dm, meta, mixed, heads, 0)


def attend_section(k, blocks, meta):
    dm = k.dm
    shape = (dm.nc, dm.t, dm.w)
    saved, bufs = k.section(
        functools.partial(attend_body, dm),
        [(meta, "s"), (blocks, "v")],
        [sds((dm.rows, 3 * dm.w), BF16), sds((dm.rows, dm.hl), F32), sds((dm.rows, dm.w), F32)],
        [pltpu.VMEM(shape, BF16)],
        8 * dm.rows * dm.rows * dm.w,
    )
    heads = send_blocks(dm, bufs[0], shape)
    k.start([heads])
    return saved, heads


def attend_back_body(dm, *refs):
    nc, w = dm.nc, dm.w
    meta, packed, lse, mixed, grads, blocks, dmix, dq, dk, dv = refs
    cuts = (meta[2], meta[3])
    tq = tk = min(TILE, dm.rows)
    scale = HEAD_DIM**-0.5
    sort_rows(dm, meta, grads, dmix)
    dk[...] = jnp.zeros_like(dk)
    dv[...] = jnp.zeros_like(dv)

    def tile(t, carry):
        here = pl.ds(mult(t * tq, tq), tq)
        q = stack_heads(dm, packed[here, :w], scale)
        do = stack_heads(dm, dmix[here, :])
        o = jnp.concatenate([mixed[here, :]] * dm.hl, axis=0)
        delta = jnp.sum(do.astype(F32) * o, axis=1, keepdims=True)
        norms = jnp.concatenate([lse[here, k : k + 1] for k in range(dm.hl)], axis=0)
        row, start = tile_rows(dm, t, tq, cuts)

        def chunk(kb, acc, last=False):
            there = pl.ds(mult(kb * tk, tk), tk)
            col = kb * tk + lax.broadcasted_iota(jnp.int32, (1, tk), 1)
            keys = packed[there, w : 2 * w]
            seen = (col <= row) & (col >= start) if last else col >= start
            s = jnp.where(seen, nt(q, keys), NEG)
            p = jnp.exp(s - norms)
            dp = nt(do, packed[there, 2 * w :])
            ds = (p * (dp - delta)).astype(BF16)
            dv[there, :] += tn(p.astype(BF16), do)
            dk[there, :] += tn(ds, q)
            return acc + nn(ds, keys)

        acc = chunk(t, lax.fori_loop(0, t, chunk, jnp.zeros((dm.hl * tq, w), F32)), True)
        dq[here, :] = (pick_heads(dm, acc) * scale).astype(BF16)
        return carry

    lax.fori_loop(0, dm.rows // tq, tile, 0)
    for at, src in enumerate((dq, dk, dv)):
        unsort_rows(dm, meta, src, blocks, at * w)


def attend_back_section(k, saved, grads, meta):
    dm = k.dm
    shape = (dm.nc, dm.t, 3 * dm.w)
    _, bufs = k.section(
        functools.partial(attend_back_body, dm),
        [(meta, "s")] + [(a, "v") for a in saved] + [(grads, "v")],
        [],
        [pltpu.VMEM(shape, BF16)]
        + [pltpu.VMEM((dm.rows, dm.w), BF16)] * 2
        + [pltpu.VMEM((dm.rows, dm.w), F32)] * 2,
        16 * dm.rows * dm.rows * dm.w,
    )
    blocks = send_blocks(dm, bufs[0], shape)
    k.start([blocks])
    return blocks


def top_body(dm, h, cot, small, result, dh, low, g_gain, g_shift):
    gain = small_vec(dm, small, "gf")
    v = h[...]
    result[...] = norm(v, gain, small_vec(dm, small, "sf")).astype(BF16)
    dv, g_gain[...], g_shift[...] = norm_back(v, gain, cot[...].astype(F32))
    dh[...] = dv
    low[...] = dv.astype(BF16)


def top_section(k, h, cot, small):
    dm = k.dm
    td, vec = (dm.t, dm.d), sds((1, dm.d), F32)
    return k.section(
        functools.partial(top_body, dm),
        [(h, "v"), (cot, "v"), (small, "v")],
        [sds(td, BF16), sds(td, F32), sds(td, BF16), vec, vec],
        [],
        20 * dm.t * dm.d,
    )[0]


def out_back_body(dm, layer, *refs):
    nc = dm.nc
    meta, gm, u, own = refs[:4]
    pieces = refs[4 : 4 + nc]
    du, sum_gm, sum_du = refs[4 + nc : 7 + nc]
    gr, own_buf, piece_buf, sems = refs[7 + nc :]
    c, f = lax.axis_index("ctx"), lax.axis_index("fsdp")
    weight = Pieces(dm, layer, own, pieces, own_buf, piece_buf, sems, None)
    weight.start()
    sum_gm[...] = col_sum(gm[...])
    for col in range(dm.ncs):
        at = mult((lax.rem(c, dm.ncs) ^ col) * dm.pc, dm.pc)
        gr[:, col * dm.pc : (col + 1) * dm.pc] = gm[:, pl.ds(at, dm.pc)]

    def finish(dact, at):
        at = pl.ds(mult(at, dm.pr), dm.pr)
        low = (dact * gelu_slope(u[:, at])).astype(BF16)
        du[:, at] = low
        sum_du[:, at] = col_sum(low)

    weight.wait_own()
    for g in range(nc // dm.ncs):
        finish(nt(gm[...], own_buf[g * dm.pr : (g + 1) * dm.pr, :]), f * dm.ffn + g * dm.pr)
    for g in range(nc // dm.ncs):
        for col in range(dm.ncs):
            weight.copies[g * dm.ncs + col].wait()
        for s in range(1, dm.nf):
            dact = None
            for col in range(dm.ncs):
                part = nt(gr[:, col * dm.pc : (col + 1) * dm.pc], piece_buf[g * dm.ncs + col, s - 1])
                dact = part if dact is None else dact + part
            finish(dact, ring(dm, f, s) * dm.ffn + ((c // dm.ncs) ^ g) * dm.pr)


def out_back_section(k, layer, gm, u, own, pieces, meta):
    dm = k.dm
    return k.section(
        functools.partial(out_back_body, dm, layer),
        [(meta, "s"), (gm, "v"), (u, "v"), (own, "a")] + [(p, "a") for p in pieces],
        [sds((dm.t, dm.ff), BF16), sds((1, dm.d), F32), sds((1, dm.ff), F32)],
        [("xr", pltpu.VMEM((dm.t, dm.d), BF16))] + piece_scratch(dm, (dm.ffn, dm.d)),
        2 * dm.t * dm.d * dm.ff,
    )[0]


def cols_back(dm, f, c, weight, dy, first, last, acc, out):
    weight.wait_own()
    acc[:, : dm.pr] = nt(dy[...], weight.own[...])
    acc[:, dm.pr :] = jnp.zeros((dm.t, dm.d - dm.pr), F32)
    for j in range(dm.nc):
        i = c ^ j

        def step():
            weight.copies[j].wait()
            at = pl.ds(mult((i - first) * dm.pc, dm.pc), dm.pc)
            acc[:, dm.pr :] += nt(dy[:, at], weight.flat(j))

        weight.each(j, step)
    for s in range(dm.nf):
        at = mult(ring(dm, f, s) * dm.pr, dm.pr)
        out[:, pl.ds(at, dm.pr)] = acc[:, s * dm.pr : (s + 1) * dm.pr].astype(out.dtype)


def fc_back_body(dm, layer, *refs):
    nc = dm.nc
    meta, du, dh, mid, small, own = refs[:6]
    pieces = refs[6 : 6 + nc]
    dmid, ga, sum_ga, g_gain, g_shift = refs[6 + nc : 11 + nc]
    acc, dn, own_buf, piece_buf, sems = refs[11 + nc :]
    c, f = lax.axis_index("ctx"), lax.axis_index("fsdp")
    weight = Pieces(dm, layer, own, pieces, own_buf, piece_buf, sems, None)
    weight.start()
    cols_back(dm, f, c, weight, du, 0, nc, acc, dn)
    dv, g_gain[...], g_shift[...] = norm_back(
        mid[...], small_vec(dm, small, "g2" + str(layer)), dn[...]
    )
    total = dh[...] + dv
    dmid[...] = total
    low = total.astype(BF16)
    ga[...] = low
    sum_ga[...] = col_sum(low)


def fc_back_section(k, layer, du, dh, mid, small, own, pieces, meta):
    dm = k.dm
    td, vec = (dm.t, dm.d), sds((1, dm.d), F32)
    return k.section(
        functools.partial(fc_back_body, dm, layer),
        [(meta, "s"), (du, "v"), (dh, "v"), (mid, "v"), (small, "v"), (own, "a")]
        + [(p, "a") for p in pieces],
        [sds(td, F32), sds(td, BF16), vec, vec, vec],
        [("acc", pltpu.VMEM(td, F32)), ("dn", pltpu.VMEM(td, F32))] + piece_scratch(dm, (dm.pr, dm.ff)),
        2 * dm.t * dm.d * dm.ff,
    )[0]


def proj_back_body(dm, layer, *refs):
    nc = dm.nc
    meta, ga, own = refs[:3]
    pieces = refs[3 : 3 + nc]
    acc, dob, blocks, own_buf, piece_buf, sems = refs[3 + nc :]
    c, f = lax.axis_index("ctx"), lax.axis_index("fsdp")
    weight = Pieces(dm, layer, own, pieces, own_buf, piece_buf, sems, lambda j: (c ^ j) >= dm.nq)
    weight.start()
    cols_back(dm, f, c, weight, ga, dm.nq, nc, acc, dob)
    for j in range(nc):
        blocks[j] = take_heads(dm, dob, 0, c ^ j)


def proj_back_section(k, layer, ga, own, pieces, meta):
    dm = k.dm
    td, shape = (dm.t, dm.d), (dm.nc, dm.t, dm.w)
    _, bufs = k.section(
        functools.partial(proj_back_body, dm, layer),
        [(meta, "s"), (ga, "v"), (own, "a")] + [(p, "a") for p in pieces],
        [],
        [("acc", pltpu.VMEM(td, F32)), pltpu.VMEM(td, BF16), pltpu.VMEM(shape, BF16)]
        + piece_scratch(dm, (dm.pr, dm.d)),
        2 * dm.t * dm.d * dm.d,
    )
    blocks = send_blocks(dm, bufs[2], shape)
    k.start([blocks])
    return blocks


def qkv_back_body(dm, layer, *refs):
    nc = dm.nc
    meta, dmid, h, small, own, blocks = refs[:6]
    pieces = refs[6 : 6 + nc]
    dh, low, dqkv, sum_dqkv, g_gain, g_shift = refs[6 + nc : 12 + nc]
    acc, dn, own_buf, piece_buf, sems = refs[12 + nc :]
    blocks = [blocks.at[j] for j in range(nc)]
    c, f = lax.axis_index("ctx"), lax.axis_index("fsdp")
    weight = Pieces(dm, layer, own, pieces, own_buf, piece_buf, sems, lambda j: (c ^ j) < dm.nq)
    weight.start()
    for third in range(3):
        put_heads(dm, dqkv, third * dm.d, blocks, third * dm.w, c)
    sum_dqkv[...] = col_sum(dqkv[...])
    cols_back(dm, f, c, weight, dqkv, 0, dm.nq, acc, dn)
    dv, g_gain[...], g_shift[...] = norm_back(
        h[...].astype(F32), small_vec(dm, small, "g1" + str(layer)), dn[...]
    )
    total = dmid[...] + dv
    dh[...] = total
    low[...] = total.astype(BF16)


def qkv_back_section(k, layer, dmid, h, small, own, blocks, pieces, meta):
    dm = k.dm
    td, vec = (dm.t, dm.d), sds((1, dm.d), F32)
    return k.section(
        functools.partial(qkv_back_body, dm, layer),
        [(meta, "s"), (dmid, "v"), (h, "v"), (small, "v"), (own, "a"), (blocks, "v")]
        + [(p, "a") for p in pieces],
        [sds(td, F32), sds(td, BF16), sds((dm.t, 3 * dm.d), BF16), sds((1, 3 * dm.d), F32), vec, vec],
        [("acc", pltpu.VMEM(td, F32)), ("dn", pltpu.VMEM(td, F32))] + piece_scratch(dm, (dm.pr, 3 * dm.d)),
        2 * dm.t * dm.d * 3 * dm.d,
    )[0]


def sum_body(indices, *refs):
    n = len(indices)
    out, bufs, sems = refs[n], refs[n + 1 : 2 * n + 1], refs[2 * n + 1]
    copies = [
        pltpu.make_async_copy(at_of(ref, index), buf, sems.at[at])
        for at, (ref, index, buf) in enumerate(zip(refs, indices, bufs))
    ]
    for copy in copies:
        copy.start()
    for copy in copies:
        copy.wait()
    total = bufs[0][...].astype(F32)
    for buf in bufs[1:]:
        total = total + buf[...].astype(F32)
    out[...] = total.astype(out.dtype)


def sum_section(k, terms, shape, dtype=BF16, parts=None):
    bufs = [
        ("sum" + str((at, shape, dtype)), pltpu.VMEM(shape, dtype)) for at in range(len(terms))
    ]
    return k.section(
        functools.partial(sum_body, [index for _, index in terms]),
        [(src, "a") for src, _ in terms],
        [sds(shape, dtype)],
        bufs + [("sum" + str(len(terms)), pltpu.SemaphoreType.DMA((len(terms),)))],
        0,
    )[0][0]


def pack_body(dm, *refs):
    for n, name in enumerate(vector_names()):
        at, size = small_offsets(dm)[0][name]
        layer, which = n // len(SMALL), n % len(SMALL)
        if layer == LAYERS:
            layer, which = 0, len(SMALL) + which
        refs[-1][:, at : at + size] = refs[which][layer : layer + 1, :].astype(F32)


def small_body(dm, packed, others, out):
    f = lax.axis_index("fsdp")
    out[pl.ds(f, 1), :] = packed[...]
    for s in range(1, dm.nf):
        out[pl.ds(ring(dm, f, s), 1), :] = others[s - 1]


def collect_body(dm, *refs):
    names, (table, _) = vector_names(), small_offsets(dm)
    for name, ref in zip(names, refs):
        at, size = table[name]
        for g in range(dm.nf):
            refs[-1][g, :, at : at + size] = ref[:, g * size : (g + 1) * size]


def grad_body(dm, kind, *refs):
    c, f = lax.axis_index("ctx"), lax.axis_index("fsdp")
    out, xt = refs[-2:]
    pairs = [refs[n : n + 2] for n in range(0, len(refs) - 2, 2)]
    lefts = pairs[: len(pairs) // 2]
    for n, pair in enumerate(lefts):
        depth = pair[0].shape[1]
        for half, ref in enumerate(pair):
            for at in range(0, depth, dm.pc):
                xt[n * depth + at : n * depth + at + dm.pc, half * dm.t : (half + 1) * dm.t] = ref[
                    :, at : at + dm.pc
                ].T
    rights = pairs[len(pairs) // 2 :]

    def fill(t, row_base, row_step, pair, col):
        cols = pl.ds(mult(col * dm.pc, dm.pc), dm.pc)
        dy = jnp.concatenate([pair[0][:, cols], pair[1][:, cols]], axis=0)
        for s in range(dm.nf):
            at = mult(row_base + ring(dm, f, s) * row_step, dm.pr)
            out[t, s] = nn(xt[pl.ds(at, dm.pr), :], dy).astype(BF16)

    for t in reversed(range(dm.nc // 2)):
        i = c ^ (2 * t)
        if kind == "attn":
            pl.when(i < dm.nq)(lambda: fill(t, 0, dm.pr, rights[0], i))
            pl.when(i >= dm.nq)(lambda: fill(t, dm.d, dm.pr, rights[1], i - dm.nq))
        elif kind == "fc":
            fill(t, 0, dm.pr, rights[0], i)
        else:
            fill(t, (i // dm.ncs) * dm.pr, dm.ffn, rights[0], lax.rem(i, dm.ncs))


def grad_section(k, kind, lefts, rights):
    dm = k.dm
    if kind != "attn":
        pairs = [lefts[0], rights[0]]
        if kind == "out":
            made = k.load_all([(value(v), name) for pair in pairs for v, name in zip(pair, ("own", "twin"))])
            lefts, rights = [made[:2]], [made[2:]]
        else:
            made = k.load_all([(value(pair[1]), "twin") for pair in pairs])
            lefts, rights = [(pairs[0][0], made[0])], [(pairs[1][0], made[1])]
    return k.section(
        functools.partial(grad_body, dm, kind),
        [(a, "v") for pair in lefts + rights for a in pair],
        [sds((dm.nc // 2, dm.nf, dm.pr, dm.pc), BF16)],
        [("xt", pltpu.VMEM((dm.ff, 2 * dm.t), BF16))],
        2 * dm.t * dm.d * dm.ff,
    )[0][0]


def place_body(dm, *refs):
    nc = dm.nc
    jobs = [(layer, kind) for kind in ("out", "fc", "attn") for layer in reversed(range(LAYERS))]
    pieces = {job: refs[n * nc : (n + 1) * nc] for n, job in enumerate(jobs)}
    vector = refs[len(jobs) * nc]
    qkv, proj, fc, out = refs[len(jobs) * nc + 1 : len(jobs) * nc + 5]
    small = refs[len(jobs) * nc + 5 : -5]
    loads, wide, tall, load_sems, sems = refs[-5:]
    c = lax.axis_index("ctx")

    def fetch(n):
        return [
            pltpu.make_async_copy(pieces[jobs[n]][j], loads.at[n % 2, j], load_sems.at[n % 2, j])
            for j in range(nc)
        ]

    def store(n):
        layer, kind = jobs[n]
        buf, sem = (tall if kind == "out" else wide).at[n % 2], sems.at[n % 2]
        if kind == "attn":
            return [
                pltpu.make_async_copy(buf.at[:, pl.ds(0, 3 * dm.d)], qkv.at[layer], sem.at[0]),
                pltpu.make_async_copy(buf.at[:, pl.ds(3 * dm.d, dm.d)], proj.at[layer], sem.at[1]),
            ]
        return [pltpu.make_async_copy(buf, (out if kind == "out" else fc).at[layer], sem.at[0])]

    for copy in fetch(0):
        copy.start()
    for n, name in enumerate(vector_names()):
        at, size = small_offsets(dm)[0][name]
        row, ref = (n // len(SMALL), small[n % len(SMALL)])
        if row == LAYERS:
            row, ref = 0, small[len(SMALL) + n % len(SMALL)]
        ref[row : row + 1, :] = vector[:, at : at + size]
    for n in range(len(jobs)):
        if n + 1 < len(jobs):
            for copy in fetch(n + 1):
                copy.start()
        if n >= 2:
            for copy in store(n - 2):
                copy.wait()
        for copy in fetch(n):
            copy.wait()
        for j in range(nc):
            i = c ^ j
            v = loads[n % 2, j].astype(F32)
            if jobs[n][1] == "out":
                rows = pl.ds(mult((i // dm.ncs) * dm.pr, dm.pr), dm.pr)
                tall[n % 2, rows, pl.ds(mult(lax.rem(i, dm.ncs) * dm.pc, dm.pc), dm.pc)] = v
            else:
                wide[n % 2, :, pl.ds(mult(i * dm.pc, dm.pc), dm.pc)] = v
        for copy in store(n):
            copy.start()
    for n in (len(jobs) - 2, len(jobs) - 1):
        for copy in store(n):
            copy.wait()


def place_call(dm, done, vector):
    names = [k + str(layer) for k in ("o", "c", "a") for layer in reversed(range(LAYERS))]
    pieces = [p for name in names for p in done[name]]
    shapes = [(dm.pr, 3 * dm.d), (dm.pr, dm.d), (dm.pr, dm.ff), (dm.ffn, dm.d)]
    table = small_offsets(dm)[0]
    vectors = [(LAYERS, table[name + "0"][1]) for name, _ in SMALL] + [(1, dm.pr)] * 2
    return pl.pallas_call(
        functools.partial(place_body, dm),
        out_shape=[sds((LAYERS,) + shape, F32) for shape in shapes] + [sds(v, F32) for v in vectors],
        in_specs=[pl.BlockSpec(memory_space=pl.ANY)] * len(pieces) + [pl.BlockSpec(memory_space=pltpu.VMEM)],
        out_specs=[pl.BlockSpec(memory_space=pl.ANY)] * len(shapes)
        + [pl.BlockSpec(memory_space=pltpu.VMEM)] * len(vectors),
        scratch_shapes=[
            pltpu.VMEM((2, dm.nc, dm.pr, dm.pc), BF16),
            pltpu.VMEM((2, dm.pr, dm.ff), F32),
            pltpu.VMEM((2, dm.ffn, dm.d), F32),
            pltpu.SemaphoreType.DMA((2, dm.nc)),
            pltpu.SemaphoreType.DMA((2, 2)),
        ],
        compiler_params=pltpu.CompilerParams(vmem_limit_bytes=VMEM_BYTES),
    )(*pieces, vector)


def plane_bits(nc):
    bits = []
    bit = 2
    while bit < nc:
        bits.append(bit)
        bit *= 2
    return bits


def moving(moves):
    return lambda k: k.start(moves)


def spread(dm, first):
    bits = plane_bits(dm.nc)
    held = {0: first}
    if len(bits) == 2:
        one, two = bits
        held.update({bit: whole(first, ("ctx", bit)) for bit in (one, two, 1)})
        yield moving([held[one], held[two], held[1]])
        lead = (slice(None),) * (len(first.shape) - 2)
        cut = first.shape[-2] // 2
        low, high = lead + (pl.ds(0, cut),), lead + (pl.ds(cut, cut),)
        far = Move(
            first.shape, first.dtype,
            [([(None, held[two], low)], ("ctx", one), low), ([(None, held[one], high)], ("ctx", two), high)],
        )
        held[one ^ two] = far
        held.update({bit ^ 1: whole(held[bit], ("ctx", 1)) for bit in bits})
        yield moving([far, held[one ^ 1], held[two ^ 1]])
        held[one ^ two ^ 1] = whole(far, ("ctx", 1))
        yield moving([held[one ^ two ^ 1]])
    else:
        for bit in bits + [1]:
            new = {j ^ bit: whole(v, ("ctx", bit)) for j, v in held.items()}
            yield moving(list(new.values()))
            held.update(new)
    return [held[j] for j in range(dm.nc)]


def gather(dm, source):
    others = Move(
        (dm.nf - 1, dm.pr, dm.pc), BF16,
        [(source, ("fsdp", s), (s - 1,)) for s in range(1, dm.nf)],
    )
    yield moving([others])
    return (yield from spread(dm, others))


def shift_order(dm):
    return sorted(range(1, dm.nf), key=lambda s: min(s, dm.nf - s))


def gather_split(dm, source):
    bits = plane_bits(dm.nc)
    if len(bits) != 2:
        return (yield from gather(dm, source))
    order = shift_order(dm)
    one, two = bits

    def line(parts):
        made = {}
        for s in order:
            base = made[order[0]] if made else None
            made[s] = Move((dm.nf - 1, dm.pr, dm.pc), BF16, parts(s), base)
        return made

    def along(prev, route):
        return line(lambda s: [([(None, prev[s], (s - 1,))], route, (s - 1,))])

    z = line(lambda s: [(source, ("fsdp", s), (s - 1,))])
    yield moving([z[s] for s in order])
    x, y, core = along(z, ("ctx", one)), along(z, ("ctx", two)), along(z, ("ctx", 1))
    for s in order:
        yield moving([x[s], y[s], core[s]])
    cut = dm.pr // 2

    def corner(s):
        low, high = (s - 1, pl.ds(0, cut)), (s - 1, pl.ds(cut, cut))
        return [([(None, y[s], low)], ("ctx", one), low), ([(None, x[s], high)], ("ctx", two), high)]

    far = line(corner)
    x_, y_ = along(x, ("ctx", 1)), along(y, ("ctx", 1))
    for s in order:
        yield moving([far[s], x_[s], y_[s]])
    far_ = along(far, ("ctx", 1))
    yield moving([far_[s] for s in order])
    held = {0: z, 1: core, one: x, one ^ 1: x_, two: y, two ^ 1: y_, one ^ two: far, one ^ two ^ 1: far_}
    return [held[j][order[0]] for j in range(dm.nc)]


def plane_sum(dm, terms, first_shard, shards):
    bits = plane_bits(dm.nc)
    if len(bits) == 2:
        one, two = bits
        cut = dm.pr // 2
        shape = (shards, cut, dm.pc)

        def part(t, first):
            return (t, pl.ds(first_shard, shards), pl.ds(first, cut))

        def send(t, first, bit):
            return Move(shape, BF16, [([(None, terms, part(t, first))], ("ctx", bit), None)])

        far_x, own_x = send(3, 0, one), send(1, 0, one)
        far_y, own_y = send(3, cut, two), send(2, cut, two)
        yield moving([far_x, far_y, own_x, own_y])
        near = []

        def second(k):
            x = sum_section(k, [(terms, part(1, cut)), (far_y, None)], shape)
            near.append(whole(x, ("ctx", one)))
            k.start(near[:1])
            y = sum_section(k, [(terms, part(2, 0)), (far_x, None)], shape)
            near.append(whole(y, ("ctx", two)))
            k.start(near[1:])

        yield second
        return [
            [(terms, part(0, 0)), (own_x, None), (near[1], None)],
            [(terms, part(0, cut)), (near[0], None), (own_y, None)],
        ]
    at, index = terms, ()
    count = dm.nc // 2
    for n, _ in enumerate(bits):
        count //= 2
        shape = (count, dm.nf, dm.pr, dm.pc)
        away = Move(shape, BF16, [([(None, at, (pl.ds(count, count),))], ("ctx", bits[-1 - n]), None)])
        yield moving([away])
        if count > 1:
            made = []

            def add(k):
                made.append(sum_section(k, [(at, (pl.ds(0, count),)), (away, None)], shape))

            yield add
            at = made[0]
    return [[(at, (0,)), (away, (0,))]]


def reduce(dm, terms, split=False):
    split = split and len(plane_bits(dm.nc)) == 2
    groups = [(s, 1) for s in shift_order(dm) + [0]] if split else [(0, dm.nf)]
    sums = [plane_sum(dm, terms, *group) for group in groups]
    parts = [None] * len(groups)

    def stage(n):
        try:
            return next(sums[n])
        except StopIteration as stop:
            parts[n] = stop.value
            return None

    own, others = {}, []

    def along(n):
        first, count = groups[n]

        def put(k):
            rows = dm.pr // len(parts[n])
            for at, part in enumerate(parts[n]):
                total = sum_section(k, part, (count, rows, dm.pc))
                sent = [s for s in range(first, first + count) if s > 0]
                if first == 0:
                    own[at] = total
                if sent:
                    move = Move(
                        (len(sent), rows, dm.pc), BF16,
                        [
                            ([(None, total, (s - first,))], ("fsdp", dm.nf - s), (m,))
                            for m, s in enumerate(sent)
                        ],
                    )
                    others.append((at, move, len(sent)))
                    k.start([move])

        return put

    for n in range(len(groups)):
        yield stage(n)
    if split:
        for n in range(len(groups) + 1):
            if n < len(groups):
                yield stage(n)
            if n > 0:
                stage(n - 1)
                yield along(n - 1)
    else:
        more = stage(0)
        while more is not None:
            yield more
            more = stage(0)
        yield along(0)
    mine = []

    def join(k):
        rows = dm.pr // len(own)

        def body(*refs):
            for n in range(len(own)):
                refs[-1][n * rows : (n + 1) * rows, :] = refs[n][...]

        sums = [
            sum_section(
                k,
                [(own[at], (0,))] + [(m, (i,)) for to, m, size in others if to == at for i in range(size)],
                (rows, dm.pc),
            )
            for at in range(len(own))
        ]
        mine.append(k.section(body, [(v, "v") for v in sums], [sds((dm.pr, dm.pc), BF16)], [], 0)[0][0])

    return (yield from spread_later(dm, mine, join))


def spread_later(dm, mine, join):
    inner = None

    def first(k):
        nonlocal inner
        join(k)
        inner = spread(dm, mine[0])
        next(inner)(k)

    yield first
    return (yield from inner)


def reduce_small(dm, total):
    n = total.shape[-1]
    row = lambda s: (lambda: (ring(dm, lax.axis_index("fsdp"), s),))
    bit = 1
    state = [total]
    while bit < dm.nc:

        def step(k):
            other = whole(state[-1], ("ctx", bit))
            k.start([other])
            state.append(other)

        def add(k):
            other = state.pop()
            state.append(sum_section(k, [(state[-1], None), (other, None)], total.shape, F32))

        yield step
        yield add
        bit *= 2
    total = state[-1]
    others = Move(
        (dm.nf - 1, 1, n), F32,
        [([(None, total, row(s))], ("fsdp", dm.nf - s), (s - 1,)) for s in range(1, dm.nf)],
    )
    yield moving([others])
    made = []

    def last(k):
        terms = [(total, row(0))] + [(others, (s,)) for s in range(dm.nf - 1)]
        made.append(sum_section(k, terms, (1, n), F32))

    yield last
    return made[0]


class Flow:
    def __init__(self, dm):
        self.dm, self.live, self.done = dm, {}, {}
        self.ids = itertools.count()

    def kernel(self, *names):
        k = Kernel(self.dm, self.ids)
        self.go(k, *names)
        return k

    def add(self, name, transfer):
        self.live[name] = transfer

    def go(self, k, *names):
        for name in names:
            if name in self.live:
                try:
                    next(self.live[name])(k)
                except StopIteration as stop:
                    self.done[name] = stop.value
                    del self.live[name]

    def finish(self, k, name):
        while name in self.live:
            self.go(k, name)
        return self.done[name]


def local(acts, cotangent, pair_slots, segments, *tensors):
    (
        attn_gain, attn_shift, qkv_weight, qkv_bias, proj_weight, proj_bias, mlp_gain, mlp_shift,
        fc_weight, fc_bias, out_weight, out_bias, final_gain, final_shift,
    ) = tensors
    nf, nc = lax.axis_size("fsdp"), lax.axis_size("ctx")
    dm = dims_of(acts, fc_weight, nf, nc)
    c, f = lax.axis_index("ctx"), lax.axis_index("fsdp")
    small_size = small_offsets(dm)[1]

    seg = segments[0]
    cut_one = jnp.sum((seg == 0).astype(jnp.int32))
    cut_two = cut_one + jnp.sum((seg == 1).astype(jnp.int32))
    index = jnp.arange(nc, dtype=jnp.int32)
    others = jnp.bitwise_xor(c, index)
    lows = jnp.sum(jnp.where(others[:, None] == index[None, :], pair_slots[None, :], 0), axis=1)
    slots = jnp.sum(jnp.where(lows[None, :] == index[:, None], index[None, :], 0), axis=1)
    meta = jnp.concatenate([jnp.stack([c, f, cut_one, cut_two]).astype(jnp.int32), lows, slots])

    def source(kind, layer):
        def cols(first, last):
            at = jnp.clip(lax.axis_index("ctx"), first, last - 1) - first
            return (layer, pl.ds(0, dm.pr), pl.ds(mult(at * dm.pc, dm.pc), dm.pc))

        def place():
            at = lax.axis_index("ctx")
            row, col = (at // dm.ncs) * dm.pr, lax.rem(at, dm.ncs) * dm.pc
            return (layer, pl.ds(mult(row, dm.pr), dm.pr), pl.ds(mult(col, dm.pc), dm.pc))

        if kind == "attn":
            return [
                (lambda: lax.axis_index("ctx") < dm.nq, qkv_weight, lambda: cols(0, dm.nq)),
                (lambda: lax.axis_index("ctx") >= dm.nq, proj_weight, lambda: cols(dm.nq, nc)),
            ]
        if kind == "fc":
            return [(None, fc_weight, lambda: cols(0, nc))]
        return [(None, out_weight, place)]

    def other_core(v):
        return whole(v, ("ctx", 1))

    flow = Flow(dm)
    for layer in range(LAYERS):
        for kind, name in (("attn", "A"), ("fc", "C"), ("out", "O")):
            how = gather_split if layer == 0 and name == "A" else gather
            flow.add(name + str(layer), how(dm, source(kind, layer)))

    k = flow.kernel()
    flow.go(k, "A0")
    per_layer = (attn_gain, attn_shift, qkv_bias, proj_bias, mlp_gain, mlp_shift, fc_bias, out_bias)
    _, (packed,) = k.section(
        functools.partial(pack_body, dm),
        [(v, "v") for v in per_layer] + [(v.reshape(1, -1), "v") for v in (final_gain, final_shift)],
        [],
        [pltpu.VMEM((1, small_size), F32)],
        0,
    )
    small_move = Move(
        (nf - 1, 1, small_size), F32,
        [([(None, packed, None)], ("fsdp", s), (s - 1,)) for s in range(1, nf)],
    )
    k.start([small_move])
    flow.go(k, "A0", "A0", "A0", "C0", "A0", "A0", "A0")
    (small,) = k.section(
        functools.partial(small_body, dm),
        [(packed, "v"), (small_move, "v")],
        [sds((nf, small_size), F32)],
        [],
        0,
    )[0]
    h = acts[0]
    first = flow.finish(k, "A0")
    flow.go(k, "O0")
    n1, blocks = qkv_section(k, 0, h, small, qkv_weight, first, meta)
    flow.go(k, "A1")
    twin = [other_core(n1)]
    k.start(twin)
    k.load(blocks)
    flow.go(k, "C0", "O0")
    vectors, kept = {}, []
    for layer in range(LAYERS):
        tag, nxt = str(layer), str(layer + 1)
        last = layer + 1 == LAYERS
        saved, heads = attend_section(k, blocks, meta)
        if last:
            flow.go(k, "C" + tag, "O" + tag)
        else:
            flow.go(k, "C" + tag, "O" + tag, "C" + tag)
            k.run()
            k = flow.kernel("A" + nxt, "O" + tag, "C" + nxt)
        attn = flow.done["A" + tag]
        ob, mid, n2 = proj_section(k, layer, h, small, proj_weight, heads, attn, meta)
        if last:
            flow.go(k, "O" + tag)
        twin += [other_core(ob), other_core(n2)]
        k.start(twin[1:])
        u, act = fc_section(k, layer, n2, small, fc_weight, flow.finish(k, "C" + tag), meta)
        twin.append(other_core(act))
        k.start(twin[3:])
        if not last:
            flow.go(k, "A" + nxt, "O" + nxt, "C" + nxt)
        nxt_h = out_section(k, layer, mid, act, small, out_weight, flow.finish(k, "O" + tag), meta)
        kept.append((h, n1, saved, ob, mid, n2, u, act, twin))
        h = nxt_h
        if not last:
            n1, blocks = qkv_section(k, layer + 1, h, small, qkv_weight, flow.finish(k, "A" + nxt), meta)
            twin = [other_core(n1)]
            k.start(twin)
            flow.go(k, "C" + nxt, "O" + nxt)

    weights = flow.done
    result, dh, gm, vectors["gf"], vectors["sf"] = top_section(k, h, cotangent[0], small)

    for layer in reversed(range(LAYERS)):
        tag, nxt = str(layer), str(layer + 1)
        o_, a_, k_ = "o" + nxt, "a" + nxt, "c" + nxt
        o, a, ck = "o" + tag, "a" + tag, "c" + tag
        h, n1, saved, ob, mid, n2, u, act, (n1_, ob_, n2_, act_) = kept[layer]
        gm_ = other_core(gm)
        k.start([gm_])
        du, vectors["bo" + tag], vectors["bf" + tag] = out_back_section(
            k, layer, gm, u, out_weight, weights["O" + tag], meta
        )
        du_ = other_core(du)
        k.start([du_])
        flow.go(k, o_)
        k.run()

        k = flow.kernel(a_, k_, o_)
        flow.add(o, reduce(dm, grad_section(k, "out", [(act, act_)], [(gm, gm_)])))
        flow.go(k, o)
        dmid, ga, vectors["bp" + tag], vectors["g2" + tag], vectors["s2" + tag] = fc_back_section(
            k, layer, du, dh, mid, small, fc_weight, weights["C" + tag], meta
        )
        ga_ = other_core(ga)
        k.start([ga_])
        grads = proj_back_section(k, layer, ga, proj_weight, weights["A" + tag], meta)
        flow.go(k, a_, k_, o_)
        flow.add(ck, reduce(dm, grad_section(k, "fc", [(n2, n2_)], [(du, du_)])))
        flow.go(k, ck, o)
        if dm.rows * dm.nc > 2048 * 8:
            k.run()
            k = flow.kernel()
        blocks = attend_back_section(k, saved, grads, meta)
        flow.go(k, a_, a_, a_, k_)
        k.run()

        k = flow.kernel(ck, o)
        dh, gm, dqkv, vectors["bq" + tag], vectors["g1" + tag], vectors["s1" + tag] = qkv_back_section(
            k, layer, dmid, h, small, qkv_weight, blocks, weights["A" + tag], meta
        )
        dqkv_ = other_core(dqkv)
        k.start([dqkv_])
        flow.go(k, ck)
        if layer == 0:
            shape = (nf, 1, small_size)
            rows = k.section(
                functools.partial(collect_body, dm),
                [(vectors[name], "v") for name in vector_names()],
                [sds(shape, F32)],
                [],
                0,
            )[0][0]
            flow.add("small", reduce_small(dm, rows))
            flow.go(k, "small")
        flow.add(
            a,
            reduce(
                dm, grad_section(k, "attn", [(n1, n1_), (ob, ob_)], [(dqkv, dqkv_), (ga, ga_)]), layer == 0
            ),
        )
        flow.go(k, a, *([a] * 3 if layer == 0 else []))

    flow.go(k, "o0", "a0", "small", "small", "a0", "o0", "a0", "c0", "small", "small", "a0", "o0", "a0", "c0")
    flow.go(k, "small", "a0", "a0", "c0", "a0", "small", "small")
    for name in ("a1", "c1", "o1", "c0", "o0", "a0"):
        flow.finish(k, name)
    mine = flow.finish(k, "small")
    k.run()
    done = {name: [value(v) for v in flow.done[name]] for name in ("o0", "c0", "a0", "o1", "c1", "a1")}
    grads = place_call(dm, done, value(mine))
    qkv_grad, proj_grad, fc_grad, out_grad, g1, s1, bq, bp, g2, s2, bf, bo, gf, sf = grads
    return (
        value(result)[None], value(gm)[None], g1, s1, qkv_grad, bq, proj_grad, bp, g2, s2, fc_grad, bf,
        out_grad, bo, gf.reshape(-1), sf.reshape(-1),
    )


def solution(mesh):
    row = P("fsdp", "ctx", None)
    vec, mat = P(None, "fsdp"), P(None, "fsdp", None)
    tensors = (vec, vec, mat, vec, mat, vec, vec, vec, mat, vec, mat, vec, P("fsdp"), P("fsdp"))
    return jax.shard_map(
        local,
        mesh=mesh,
        in_specs=(row, row, P(), P("fsdp", None)) + tensors,
        out_specs=(row, row) + tensors,
        check_vma=False,
    )
```

```python
import collections
import functools
import itertools

import jax
import jax.numpy as jnp
from jax import lax
from jax.experimental import pallas as pl
from jax.experimental.pallas import tpu as pltpu
from jax.sharding import PartitionSpec as P

HEADS = 16
HEAD_DIM = 64
LAYERS = 2
EPS = 1e-05
NEG = -1e30
LOW = -1e29
F32 = jnp.float32
BF16 = jnp.bfloat16
VMEM_BYTES = 61 * 1024 * 1024

FIELDS = ("t", "d", "ff", "nf", "nc", "pr", "pc", "nq", "ncs", "ffn", "w", "hl", "rows", "half")
Dims = collections.namedtuple("Dims", FIELDS)


def dims_of(acts, fc_weight, nf, nc):
    t, d = acts.shape[1], acts.shape[2]
    ff = fc_weight.shape[2]
    pr, pc = d // nf, ff // nc
    return Dims(
        t=t, d=d, ff=ff, nf=nf, nc=nc, pr=pr, pc=pc, nq=3 * d // pc, ncs=d // pc, ffn=ff // nf,
        w=d // nc, hl=HEADS // nc, rows=t * nc, half=t // 2,
    )


SMALL = (("g1", 1), ("s1", 1), ("bq", 3), ("bp", 1), ("g2", 1), ("s2", 1), ("bf", 4), ("bo", 1))


def small_offsets(dm):
    table, at = {}, 0
    for layer in range(LAYERS):
        for name, _ in SMALL:
            size = {"bq": 3 * dm.pr, "bf": dm.ffn}.get(name, dm.pr)
            table[name + str(layer)] = (at, size)
            at += size
    for name in ("gf", "sf"):
        table[name] = (at, dm.pr)
        at += dm.pr
    return table, at


def send_blocks(dm, slot, shape):
    return Move(
        shape, BF16,
        [([(None, slot, (j,))], ("ctx", j) if j else None, (j,)) for j in range(dm.nc)],
    )


def vector_names():
    return [name + str(layer) for layer in range(LAYERS) for name, _ in SMALL] + ["gf", "sf"]


def mult(v, by):
    return pl.multiple_of(v, by)


def nn(a, b):
    return lax.dot_general(a, b, (((1,), (0,)), ((), ())), preferred_element_type=F32)


def nt(a, b):
    return lax.dot_general(a, b, (((1,), (1,)), ((), ())), preferred_element_type=F32)


def tn(a, b):
    return lax.dot_general(a, b, (((0,), (0,)), ((), ())), preferred_element_type=F32)


def col_sum(v):
    return jnp.sum(v.astype(F32), axis=0, keepdims=True)


def small_vec(dm, small_ref, name):
    at, size = small_offsets(dm)[0][name]
    return jnp.concatenate([small_ref[g : g + 1, at : at + size] for g in range(dm.nf)], axis=1)


def norm_parts(v):
    center = v - jnp.mean(v, axis=-1, keepdims=True)
    scale = lax.rsqrt(jnp.mean(center * center, axis=-1, keepdims=True) + EPS)
    return center * scale, scale


def norm(v, gain, shift):
    return norm_parts(v)[0] * gain + shift


def norm_back(v, gain, dy):
    xh, scale = norm_parts(v)
    e = dy * gain
    dv = scale * (
        e - jnp.mean(e, axis=-1, keepdims=True) - xh * jnp.mean(e * xh, axis=-1, keepdims=True)
    )
    return dv, col_sum(dy * xh), col_sum(dy)


K0 = 0.7978845608028654
K1 = 0.044715


def gelu(u):
    return 0.5 * u * (1.0 + jnp.tanh(K0 * (u + K1 * u * u * u)))


def gelu_slope(u):
    th = jnp.tanh(K0 * (u + K1 * u * u * u))
    return 0.5 * (1.0 + th) + 0.5 * u * (1.0 - th * th) * (K0 * (1.0 + 3.0 * K1 * u * u))


class Slot:
    def __init__(self, kind, at, like=None):
        self.kind, self.at, self.result = kind, at, None
        if like is not None:
            self.shape, self.dtype = like.shape, like.dtype


class Move:
    def __init__(self, shape, dtype, parts, base=None):
        self.shape, self.dtype, self.parts, self.base = shape, dtype, parts, base
        self.result = None


def whole(array, route):
    return Move(array.shape, array.dtype, [([(None, array, None)], route, None)])


def value(v):
    return v.result if isinstance(v, (Move, Slot)) else v


def at_of(ref, index):
    return ref if index is None else ref.at[index() if callable(index) else index]


class Kernel:
    def __init__(self, dm, ids=None):
        self.dm, self.ids = dm, ids
        self.arrays, self.in_specs, self.slots = [], [], {}
        self.outs, self.out_specs, self.out_slots = [], [], []
        self.scratch, self.keys, self.steps = [], {}, []
        self.moves, self.flops = [], 0

    def operand(self, a, place):
        if isinstance(a, (Slot, Move)) and a.result is None:
            return self.load(a) if isinstance(a, Move) and place == "v" else a
        a = value(a)
        key = (id(a), place)
        if key not in self.slots:
            spaces = {"v": pltpu.VMEM, "s": pltpu.SMEM, "a": pl.ANY}
            self.slots[key] = Slot("in", len(self.arrays))
            self.arrays.append(a)
            self.in_specs.append(pl.BlockSpec(memory_space=spaces[place]))
        return self.slots[key]

    def load(self, move):
        key = ("load", id(move))
        if key not in self.keys:
            self.load_all([(move, key)])
        return self.keys[key]

    def load_all(self, wanted):
        srcs, dsts = [], []
        for array, key in wanted:
            key = key if isinstance(key, tuple) else (key, array.shape)
            if key not in self.keys:
                self.keys[key] = Slot("scratch", len(self.scratch), array)
                self.scratch.append(pltpu.VMEM(array.shape, array.dtype))
            srcs.append(self.operand(array, "a"))
            dsts.append(self.keys[key])
        n = len(wanted)

        def body(*refs):
            copies = [pltpu.make_async_copy(refs[i], refs[n + i], refs[2 * n].at[i]) for i in range(n)]
            for copy in copies:
                copy.start()
            for copy in copies:
                copy.wait()

        sems = self.buffer(("load" + str(n), pltpu.SemaphoreType.DMA((n,))))
        self.steps.append(("body", body, srcs + dsts + [sems]))
        return dsts

    def output(self, out, space):
        slot = Slot("out", len(self.outs), out)
        self.outs.append(out)
        self.out_specs.append(pl.BlockSpec(memory_space=space))
        self.out_slots.append(slot)
        return slot

    def buffer(self, spec):
        key, spec = spec if isinstance(spec, tuple) else (None, spec)
        if key is None or key not in self.keys:
            slot = Slot("scratch", len(self.scratch))
            self.scratch.append(spec)
            if key is None:
                return slot
            self.keys[key] = slot
        return self.keys[key]

    def section(self, body, operands, outs, scratch, flops):
        refs = [self.operand(a, place) for a, place in operands]
        made = [self.output(o, pltpu.VMEM) for o in outs]
        bufs = [self.buffer(spec) for spec in scratch]
        self.steps.append(("body", body, refs + made + bufs))
        self.flops += flops
        return made, bufs

    def start(self, moves):
        for move in moves:
            parts = [
                ([(cond, self.operand(src, "a"), index) for cond, src, index in sources], route, place)
                for sources, route, place in move.parts
            ]
            if move.base is None:
                slot = self.output(sds(move.shape, move.dtype), pl.ANY)
            else:
                slot = next(made for m, _, made in self.moves if m is move.base)
            self.moves.append((move, parts, slot))
            self.steps.append(("start", len(self.moves) - 1, None))

    def run(self, local=None):
        dm, moves, steps = self.dm, self.moves, self.steps
        order = {id(m): n for n, (m, _, _) in enumerate(moves)}
        count = sum(len(parts) for _, parts, _ in moves)
        routes = sorted({route for _, parts, _ in moves for _, route, _ in parts if route is not None})
        n_in, n_out, n_scratch = len(self.arrays), len(self.outs), len(self.scratch)
        sems = [pltpu.SemaphoreType.DMA((count,))] * 2 if count else []

        def kernel(*refs):
            groups = {"in": refs[:n_in], "out": refs[n_in : n_in + n_out], "scratch": refs[n_in + n_out :]}
            if count:
                send_sems, recv_sems = refs[-2:]
            c, f = lax.axis_index("ctx"), lax.axis_index("fsdp")

            def device(route, back=False):
                axis, by = route
                if axis == "ctx":
                    return (c ^ by, f)
                return (c, lax.rem(f + (dm.nf - by if back else by), dm.nf))

            if routes:
                barrier = pltpu.get_barrier_semaphore()
                for route in routes:
                    pl.semaphore_signal(
                        barrier, inc=1, device_id=device(route, True), device_id_type=pl.DeviceIdType.MESH
                    )
                pl.semaphore_wait(barrier, len(routes))

            def ref_of(src):
                if isinstance(src, Move):
                    src = moves[order[id(src)]][2]
                return groups[src.kind][src.at]

            at, copies = 0, []
            for _, parts, slot in moves:
                rows = []
                for sources, route, place in parts:
                    choices = []
                    for cond, src, index in sources:
                        ends = at_of(ref_of(src), index), at_of(ref_of(slot), place)
                        if route is None:
                            copy = pltpu.make_async_copy(*ends, recv_sems.at[at])
                        else:
                            copy = pltpu.make_async_remote_copy(
                                *ends, send_sems.at[at], recv_sems.at[at],
                                device_id=device(route), device_id_type=pl.DeviceIdType.MESH,
                            )
                        choices.append((cond, copy))
                    rows.append((route, choices))
                    at += 1
                copies.append(rows)
            arrived = set()

            def wait(n):
                if n in arrived:
                    return
                arrived.add(n)
                for route, choices in copies[n]:
                    copy = choices[0][1]
                    copy.wait() if route is None else copy.wait_recv()

            def ready(src):
                if isinstance(src, Move):
                    wait(order[id(src)])

            for kind, what, used in steps:
                if kind == "body":
                    for slot in used:
                        ready(slot)
                        for n, (m, _, _) in enumerate(moves):
                            if m.base is slot:
                                wait(n)
                    what(*[ref_of(slot) for slot in used])
                    continue
                for sources, _, _ in moves[what][1]:
                    for _, src, _ in sources:
                        ready(src)
                for _, choices in copies[what]:
                    for cond, copy in choices:
                        if cond is None:
                            copy.start()
                        else:
                            pl.when(cond())(copy.start)
            for n in range(len(moves)):
                wait(n)
            for rows in copies:
                for route, choices in rows:
                    if route is not None:
                        choices[0][1].wait_send()

        params = {"collective_id": next(self.ids), "has_side_effects": True} if routes else {}
        moved = sum(a.size * a.dtype.itemsize for a in self.arrays + self.outs)
        results = pl.pallas_call(
            kernel,
            out_shape=self.outs,
            in_specs=self.in_specs,
            out_specs=self.out_specs,
            scratch_shapes=self.scratch + sems,
            compiler_params=pltpu.CompilerParams(vmem_limit_bytes=VMEM_BYTES, **params),
            cost_estimate=pl.CostEstimate(flops=self.flops, bytes_accessed=moved, transcendentals=0),
        )(*self.arrays)
        for slot, result in zip(self.out_slots, results):
            slot.result = result
        for move, _, slot in moves:
            move.result = slot.result


def sds(shape, dtype):
    return jax.ShapeDtypeStruct(shape, dtype)


class Pieces:
    def __init__(self, dm, layer, own, pieces, own_buf, piece_buf, sems, wanted):
        self.dm, self.wanted = dm, wanted
        self.own_copy = pltpu.make_async_copy(own.at[layer], own_buf, sems.at[dm.nc])
        self.copies = [
            pltpu.make_async_copy(pieces[j], piece_buf.at[j], sems.at[j]) for j in range(dm.nc)
        ]
        self.own, self.buf = own_buf, piece_buf

    def start(self):
        self.own_copy.start()
        for j in range(self.dm.nc):
            self.each(j, self.copies[j].start)

    def each(self, j, act):
        if self.wanted is None:
            act()
        else:
            pl.when(self.wanted(j))(act)

    def wait_own(self):
        self.own_copy.wait()

    def flat(self, j):
        return self.buf[j].reshape((self.dm.nf - 1) * self.dm.pr, self.dm.pc)


def piece_scratch(dm, own_shape):
    return [
        ("own" + str(own_shape), pltpu.VMEM(own_shape, BF16)),
        ("pieces", pltpu.VMEM((dm.nc, dm.nf - 1, dm.pr, dm.pc), BF16)),
        ("loads", pltpu.SemaphoreType.DMA((dm.nc + 1,))),
    ]


def ring(dm, f, s):
    return lax.rem(f + (dm.nf - s), dm.nf)


def relative(dm, f, src, dst):
    for s in range(dm.nf):
        at = mult(ring(dm, f, s) * dm.pr, dm.pr)
        dst[:, s * dm.pr : (s + 1) * dm.pr] = src[:, pl.ds(at, dm.pr)]


def take_heads(dm, ref, base, i):
    if dm.w % 128 == 0:
        return ref[:, pl.ds(mult(base + i * dm.w, 128), dm.w)]
    per = 128 // dm.w
    wide = ref[:, pl.ds(mult(base + (i // per) * 128, 128), 128)]
    part = wide[:, : dm.w]
    for at in range(1, per):
        part = jnp.where(lax.rem(i, per) == at, wide[:, at * dm.w : (at + 1) * dm.w], part)
    return part


def put_heads(dm, ref, base, blocks, at, c):
    if dm.w % 128 == 0:
        for j in range(dm.nc):
            ref[:, pl.ds(mult(base + (c ^ j) * dm.w, 128), dm.w)] = blocks[j][:, at : at + dm.w]
        return
    for j in range(0, dm.nc, 2):
        one, two = blocks[j][:, at : at + dm.w], blocks[j + 1][:, at : at + dm.w]
        even = lax.rem(c, 2) == 0
        pair = jnp.concatenate([jnp.where(even, one, two), jnp.where(even, two, one)], axis=1)
        ref[:, pl.ds(mult(base + ((c ^ j) // 2) * 128, 128), 128)] = pair


def qkv_body(dm, layer, *refs):
    nc = dm.nc
    meta, h, small, own = refs[:4]
    pieces = refs[4 : 4 + nc]
    n1, xr, y, bias, blocks, own_buf, piece_buf, sems = refs[4 + nc :]
    c, f = lax.axis_index("ctx"), lax.axis_index("fsdp")
    weight = Pieces(dm, layer, own, pieces, own_buf, piece_buf, sems, lambda j: (c ^ j) < dm.nq)
    weight.start()
    tag = str(layer)
    n1[...] = norm(
        h[...].astype(F32), small_vec(dm, small, "g1" + tag), small_vec(dm, small, "s1" + tag)
    ).astype(BF16)
    bias[...] = small_vec(dm, small, "bq" + tag)
    relative(dm, f, n1, xr)
    weight.wait_own()
    for j in range(nc):
        i = c ^ j

        @pl.when(i < dm.nq)
        def _():
            weight.copies[j].wait()
            at = pl.ds(mult(i * dm.pc, dm.pc), dm.pc)
            acc = nn(xr[:, dm.pr :], weight.flat(j)) + nn(xr[:, : dm.pr], own_buf[:, at])
            y[:, at] = (acc + bias[:, at]).astype(BF16)

    for j in range(nc):
        for third in range(3):
            blocks[j, :, third * dm.w : (third + 1) * dm.w] = take_heads(
                dm, y, third * dm.d, c ^ j
            )


def qkv_section(k, layer, h, small, own, pieces, meta):
    dm = k.dm
    shape = (dm.nc, dm.t, 3 * dm.w)
    (n1,), bufs = k.section(
        functools.partial(qkv_body, dm, layer),
        [(meta, "s"), (h, "v"), (small, "v"), (own, "a")] + [(p, "a") for p in pieces],
        [sds((dm.t, dm.d), BF16)],
        [
            ("xr", pltpu.VMEM((dm.t, dm.d), BF16)),
            pltpu.VMEM((dm.t, 3 * dm.d), BF16),
            pltpu.VMEM((1, 3 * dm.d), F32),
            pltpu.VMEM(shape, BF16),
        ]
        + piece_scratch(dm, (dm.pr, 3 * dm.d)),
        2 * dm.t * dm.d * 3 * dm.d,
    )
    blocks = send_blocks(dm, bufs[3], shape)
    k.start([blocks])
    return n1, blocks


def proj_body(dm, layer, *refs):
    nc = dm.nc
    meta, h, small, own, heads = refs[:5]
    pieces = refs[5 : 5 + nc]
    ob, mid, n2 = refs[5 + nc : 8 + nc]
    xr, bias, own_buf, piece_buf, sems = refs[8 + nc :]
    c, f = lax.axis_index("ctx"), lax.axis_index("fsdp")
    weight = Pieces(dm, layer, own, pieces, own_buf, piece_buf, sems, lambda j: (c ^ j) >= dm.nq)
    weight.start()
    tag = str(layer)
    bias[...] = small_vec(dm, small, "bp" + tag)
    put_heads(dm, ob, 0, [heads.at[j] for j in range(nc)], 0, c)
    relative(dm, f, ob, xr)
    weight.wait_own()
    for j in range(nc):
        i = c ^ j

        @pl.when(i >= dm.nq)
        def _():
            weight.copies[j].wait()
            at = pl.ds(mult((i - dm.nq) * dm.pc, dm.pc), dm.pc)
            acc = nn(xr[:, dm.pr :], weight.flat(j)) + nn(xr[:, : dm.pr], own_buf[:, at])
            mid[:, at] = h[:, at].astype(F32) + acc + bias[:, at]

    n2[...] = norm(
        mid[...], small_vec(dm, small, "g2" + tag), small_vec(dm, small, "s2" + tag)
    ).astype(BF16)


def proj_section(k, layer, h, small, own, heads, pieces, meta):
    dm = k.dm
    td = (dm.t, dm.d)
    return k.section(
        functools.partial(proj_body, dm, layer),
        [(meta, "s"), (h, "v"), (small, "v"), (own, "a"), (heads, "v")] + [(p, "a") for p in pieces],
        [sds(td, BF16), sds(td, F32), sds(td, BF16)],
        [("xr", pltpu.VMEM(td, BF16)), pltpu.VMEM((1, dm.d), F32)] + piece_scratch(dm, (dm.pr, dm.d)),
        2 * dm.t * dm.d * dm.d,
    )[0]


def fc_body(dm, layer, *refs):
    nc = dm.nc
    meta, n2, small, own = refs[:4]
    pieces = refs[4 : 4 + nc]
    u, act = refs[4 + nc : 6 + nc]
    xr, bias, own_buf, piece_buf, sems = refs[6 + nc :]
    c, f = lax.axis_index("ctx"), lax.axis_index("fsdp")
    weight = Pieces(dm, layer, own, pieces, own_buf, piece_buf, sems, None)
    weight.start()
    bias[...] = small_vec(dm, small, "bf" + str(layer))
    relative(dm, f, n2, xr)
    weight.wait_own()
    for j in range(nc):
        i = c ^ j
        weight.copies[j].wait()
        at = pl.ds(mult(i * dm.pc, dm.pc), dm.pc)
        acc = nn(xr[:, dm.pr :], weight.flat(j)) + nn(xr[:, : dm.pr], own_buf[:, at])
        acc = acc + bias[:, at]
        u[:, at] = acc
        act[:, at] = gelu(acc).astype(BF16)


def fc_section(k, layer, n2, small, own, pieces, meta):
    dm = k.dm
    return k.section(
        functools.partial(fc_body, dm, layer),
        [(meta, "s"), (n2, "v"), (small, "v"), (own, "a")] + [(p, "a") for p in pieces],
        [sds((dm.t, dm.ff), F32), sds((dm.t, dm.ff), BF16)],
        [("xr", pltpu.VMEM((dm.t, dm.d), BF16)), pltpu.VMEM((1, dm.ff), F32)]
        + piece_scratch(dm, (dm.pr, dm.ff)),
        2 * dm.t * dm.d * dm.ff,
    )[0]


def out_body(dm, layer, *refs):
    nc = dm.nc
    meta, mid, act, small, own = refs[:5]
    pieces = refs[5 : 5 + nc]
    h = refs[5 + nc]
    own_buf, piece_buf, sems = refs[6 + nc :]
    c, f = lax.axis_index("ctx"), lax.axis_index("fsdp")
    weight = Pieces(dm, layer, own, pieces, own_buf, piece_buf, sems, None)
    weight.start()
    weight.wait_own()
    mine = act[:, pl.ds(mult(f * dm.ffn, dm.ffn), dm.ffn)]
    h[...] = mid[...] + nn(mine, own_buf[...]) + small_vec(dm, small, "bo" + str(layer))
    for col in range(dm.ncs):
        acc = None
        for j in range(col, nc, dm.ncs):
            i = c ^ j
            weight.copies[j].wait()
            for s in range(1, dm.nf):
                at = mult(ring(dm, f, s) * dm.ffn + (i // dm.ncs) * dm.pr, dm.pr)
                part = nn(act[:, pl.ds(at, dm.pr)], piece_buf[j, s - 1])
                acc = part if acc is None else acc + part
        at = pl.ds(mult((lax.rem(c, dm.ncs) ^ col) * dm.pc, dm.pc), dm.pc)
        h[:, at] = h[:, at] + acc


def out_section(k, layer, mid, act, small, own, pieces, meta):
    dm = k.dm
    return k.section(
        functools.partial(out_body, dm, layer),
        [(meta, "s"), (mid, "v"), (act, "v"), (small, "v"), (own, "a")] + [(p, "a") for p in pieces],
        [sds((dm.t, dm.d), F32)],
        piece_scratch(dm, (dm.ffn, dm.d)),
        2 * dm.t * dm.d * dm.ff,
    )[0][0]


def chosen(dm, which, take):
    out = take(0).astype(F32)
    pick = jnp.full(out.shape, which, jnp.int32)
    for k in range(1, dm.nc):
        out = jnp.where(pick == k, take(k).astype(F32), out)
    return out.astype(BF16)


def sort_rows(dm, meta, blocks, dst):
    for piece in range(2 * dm.nc):
        slot = meta[4 + dm.nc + min(piece, 2 * dm.nc - 1 - piece)]
        half = 0 if piece < dm.nc else dm.half
        dst[piece * dm.half : (piece + 1) * dm.half, :] = chosen(
            dm, slot, lambda j: blocks[j, half : half + dm.half, :]
        )


def unsort_rows(dm, meta, src, blocks, at):
    cols = slice(at, at + src.shape[1])

    def rows(piece):
        return src[piece * dm.half : (piece + 1) * dm.half, :]

    for j in range(dm.nc):
        low = meta[4 + j]
        blocks[j, : dm.half, cols] = chosen(dm, low, rows)
        blocks[j, dm.half :, cols] = chosen(dm, low, lambda k: rows(2 * dm.nc - 1 - k))


def stack_heads(dm, v, scale=None):
    if scale is not None:
        v = v * scale
    if dm.hl == 1:
        return v
    lane = lax.broadcasted_iota(jnp.int32, v.shape, 1) // HEAD_DIM
    return jnp.concatenate([jnp.where(lane == k, v, 0.0).astype(v.dtype) for k in range(dm.hl)], axis=0)


def pick_heads(dm, v):
    if dm.hl == 1:
        return v
    rows = v.shape[0] // dm.hl
    lane = lax.broadcasted_iota(jnp.int32, (rows, v.shape[1]), 1) // HEAD_DIM
    out = v[:rows]
    for k in range(1, dm.hl):
        out = jnp.where(lane == k, v[k * rows : (k + 1) * rows], out)
    return out


def doc_start(first_cut, second_cut, row):
    return jnp.where(row < first_cut, 0, jnp.where(row < second_cut, first_cut, second_cut))


def tile_rows(dm, t, tq, cuts):
    row = t * tq + lax.rem(lax.broadcasted_iota(jnp.int32, (dm.hl * tq, 1), 0), tq)
    return row, doc_start(cuts[0], cuts[1], row)


TILE = 512


def attend_body(dm, *refs):
    nc, w = dm.nc, dm.w
    meta, blocks, packed, lse, mixed, heads = refs
    cuts = (meta[2], meta[3])
    tq = tk = min(TILE, dm.rows)
    sort_rows(dm, meta, blocks, packed)

    def tile(t, carry):
        here = pl.ds(mult(t * tq, tq), tq)
        q = stack_heads(dm, packed[here, :w], HEAD_DIM**-0.5)
        row, start = tile_rows(dm, t, tq, cuts)

        def chunk(kb, state, last=False):
            top, mass, acc = state
            there = pl.ds(mult(kb * tk, tk), tk)
            col = kb * tk + lax.broadcasted_iota(jnp.int32, (1, tk), 1)
            seen = (col <= row) & (col >= start) if last else col >= start
            s = jnp.where(seen, nt(q, packed[there, w : 2 * w]), NEG)
            new_top = jnp.maximum(top, jnp.max(s, axis=1, keepdims=True))
            p = jnp.exp(s - new_top)
            fade = jnp.exp(top - new_top)
            mass = mass * fade + jnp.sum(p, axis=1, keepdims=True)
            acc = acc * fade + nn(p.astype(BF16), packed[there, 2 * w :])
            return new_top, mass, acc

        initial = (
            jnp.full((dm.hl * tq, 1), LOW, F32),
            jnp.zeros((dm.hl * tq, 1), F32),
            jnp.zeros((dm.hl * tq, w), F32),
        )
        top, mass, acc = chunk(t, lax.fori_loop(0, t, chunk, initial), True)
        mixed[here, :] = pick_heads(dm, acc * (1.0 / mass))
        norms = top + jnp.log(mass)
        for k in range(dm.hl):
            lse[here, k : k + 1] = norms[k * tq : (k + 1) * tq]
        return carry

    lax.fori_loop(0, dm.rows // tq, tile, 0)
    unsort_rows(dm, meta, mixed, heads, 0)


def attend_section(k, blocks, meta):
    dm = k.dm
    shape = (dm.nc, dm.t, dm.w)
    saved, bufs = k.section(
        functools.partial(attend_body, dm),
        [(meta, "s"), (blocks, "v")],
        [sds((dm.rows, 3 * dm.w), BF16), sds((dm.rows, dm.hl), F32), sds((dm.rows, dm.w), F32)],
        [pltpu.VMEM(shape, BF16)],
        8 * dm.rows * dm.rows * dm.w,
    )
    heads = send_blocks(dm, bufs[0], shape)
    k.start([heads])
    return saved, heads


def attend_back_body(dm, *refs):
    nc, w = dm.nc, dm.w
    meta, packed, lse, mixed, grads, blocks, dmix, dq, dk, dv = refs
    cuts = (meta[2], meta[3])
    tq = tk = min(TILE, dm.rows)
    scale = HEAD_DIM**-0.5
    sort_rows(dm, meta, grads, dmix)
    dk[...] = jnp.zeros_like(dk)
    dv[...] = jnp.zeros_like(dv)

    def tile(t, carry):
        here = pl.ds(mult(t * tq, tq), tq)
        q = stack_heads(dm, packed[here, :w], scale)
        do = stack_heads(dm, dmix[here, :])
        o = jnp.concatenate([mixed[here, :]] * dm.hl, axis=0)
        delta = jnp.sum(do.astype(F32) * o, axis=1, keepdims=True)
        norms = jnp.concatenate([lse[here, k : k + 1] for k in range(dm.hl)], axis=0)
        row, start = tile_rows(dm, t, tq, cuts)

        def chunk(kb, acc, last=False):
            there = pl.ds(mult(kb * tk, tk), tk)
            col = kb * tk + lax.broadcasted_iota(jnp.int32, (1, tk), 1)
            keys = packed[there, w : 2 * w]
            seen = (col <= row) & (col >= start) if last else col >= start
            s = jnp.where(seen, nt(q, keys), NEG)
            p = jnp.exp(s - norms)
            dp = nt(do, packed[there, 2 * w :])
            ds = (p * (dp - delta)).astype(BF16)
            dv[there, :] += tn(p.astype(BF16), do)
            dk[there, :] += tn(ds, q)
            return acc + nn(ds, keys)

        acc = chunk(t, lax.fori_loop(0, t, chunk, jnp.zeros((dm.hl * tq, w), F32)), True)
        dq[here, :] = (pick_heads(dm, acc) * scale).astype(BF16)
        return carry

    lax.fori_loop(0, dm.rows // tq, tile, 0)
    for at, src in enumerate((dq, dk, dv)):
        unsort_rows(dm, meta, src, blocks, at * w)


def attend_back_section(k, saved, grads, meta):
    dm = k.dm
    shape = (dm.nc, dm.t, 3 * dm.w)
    _, bufs = k.section(
        functools.partial(attend_back_body, dm),
        [(meta, "s")] + [(a, "v") for a in saved] + [(grads, "v")],
        [],
        [pltpu.VMEM(shape, BF16)]
        + [pltpu.VMEM((dm.rows, dm.w), BF16)] * 2
        + [pltpu.VMEM((dm.rows, dm.w), F32)] * 2,
        16 * dm.rows * dm.rows * dm.w,
    )
    blocks = send_blocks(dm, bufs[0], shape)
    k.start([blocks])
    return blocks


def top_body(dm, h, cot, small, result, dh, low, g_gain, g_shift):
    gain = small_vec(dm, small, "gf")
    v = h[...]
    result[...] = norm(v, gain, small_vec(dm, small, "sf")).astype(BF16)
    dv, g_gain[...], g_shift[...] = norm_back(v, gain, cot[...].astype(F32))
    dh[...] = dv
    low[...] = dv.astype(BF16)


def top_section(k, h, cot, small):
    dm = k.dm
    td, vec = (dm.t, dm.d), sds((1, dm.d), F32)
    return k.section(
        functools.partial(top_body, dm),
        [(h, "v"), (cot, "v"), (small, "v")],
        [sds(td, BF16), sds(td, F32), sds(td, BF16), vec, vec],
        [],
        20 * dm.t * dm.d,
    )[0]


def out_back_body(dm, layer, *refs):
    nc = dm.nc
    meta, gm, u, own = refs[:4]
    pieces = refs[4 : 4 + nc]
    du, sum_gm, sum_du = refs[4 + nc : 7 + nc]
    gr, own_buf, piece_buf, sems = refs[7 + nc :]
    c, f = lax.axis_index("ctx"), lax.axis_index("fsdp")
    weight = Pieces(dm, layer, own, pieces, own_buf, piece_buf, sems, None)
    weight.start()
    sum_gm[...] = col_sum(gm[...])
    for col in range(dm.ncs):
        at = mult((lax.rem(c, dm.ncs) ^ col) * dm.pc, dm.pc)
        gr[:, col * dm.pc : (col + 1) * dm.pc] = gm[:, pl.ds(at, dm.pc)]

    def finish(dact, at):
        at = pl.ds(mult(at, dm.pr), dm.pr)
        low = (dact * gelu_slope(u[:, at])).astype(BF16)
        du[:, at] = low
        sum_du[:, at] = col_sum(low)

    weight.wait_own()
    for g in range(nc // dm.ncs):
        finish(nt(gm[...], own_buf[g * dm.pr : (g + 1) * dm.pr, :]), f * dm.ffn + g * dm.pr)
    for g in range(nc // dm.ncs):
        for col in range(dm.ncs):
            weight.copies[g * dm.ncs + col].wait()
        for s in range(1, dm.nf):
            dact = None
            for col in range(dm.ncs):
                part = nt(gr[:, col * dm.pc : (col + 1) * dm.pc], piece_buf[g * dm.ncs + col, s - 1])
                dact = part if dact is None else dact + part
            finish(dact, ring(dm, f, s) * dm.ffn + ((c // dm.ncs) ^ g) * dm.pr)


def out_back_section(k, layer, gm, u, own, pieces, meta):
    dm = k.dm
    return k.section(
        functools.partial(out_back_body, dm, layer),
        [(meta, "s"), (gm, "v"), (u, "v"), (own, "a")] + [(p, "a") for p in pieces],
        [sds((dm.t, dm.ff), BF16), sds((1, dm.d), F32), sds((1, dm.ff), F32)],
        [("xr", pltpu.VMEM((dm.t, dm.d), BF16))] + piece_scratch(dm, (dm.ffn, dm.d)),
        2 * dm.t * dm.d * dm.ff,
    )[0]


def cols_back(dm, f, c, weight, dy, first, last, acc, out):
    weight.wait_own()
    acc[:, : dm.pr] = nt(dy[...], weight.own[...])
    acc[:, dm.pr :] = jnp.zeros((dm.t, dm.d - dm.pr), F32)
    for j in range(dm.nc):
        i = c ^ j

        def step():
            weight.copies[j].wait()
            at = pl.ds(mult((i - first) * dm.pc, dm.pc), dm.pc)
            acc[:, dm.pr :] += nt(dy[:, at], weight.flat(j))

        weight.each(j, step)
    for s in range(dm.nf):
        at = mult(ring(dm, f, s) * dm.pr, dm.pr)
        out[:, pl.ds(at, dm.pr)] = acc[:, s * dm.pr : (s + 1) * dm.pr].astype(out.dtype)


def fc_back_body(dm, layer, *refs):
    nc = dm.nc
    meta, du, dh, mid, small, own = refs[:6]
    pieces = refs[6 : 6 + nc]
    dmid, ga, sum_ga, g_gain, g_shift = refs[6 + nc : 11 + nc]
    acc, dn, own_buf, piece_buf, sems = refs[11 + nc :]
    c, f = lax.axis_index("ctx"), lax.axis_index("fsdp")
    weight = Pieces(dm, layer, own, pieces, own_buf, piece_buf, sems, None)
    weight.start()
    cols_back(dm, f, c, weight, du, 0, nc, acc, dn)
    dv, g_gain[...], g_shift[...] = norm_back(
        mid[...], small_vec(dm, small, "g2" + str(layer)), dn[...]
    )
    total = dh[...] + dv
    dmid[...] = total
    low = total.astype(BF16)
    ga[...] = low
    sum_ga[...] = col_sum(low)


def fc_back_section(k, layer, du, dh, mid, small, own, pieces, meta):
    dm = k.dm
    td, vec = (dm.t, dm.d), sds((1, dm.d), F32)
    return k.section(
        functools.partial(fc_back_body, dm, layer),
        [(meta, "s"), (du, "v"), (dh, "v"), (mid, "v"), (small, "v"), (own, "a")]
        + [(p, "a") for p in pieces],
        [sds(td, F32), sds(td, BF16), vec, vec, vec],
        [("acc", pltpu.VMEM(td, F32)), ("dn", pltpu.VMEM(td, F32))] + piece_scratch(dm, (dm.pr, dm.ff)),
        2 * dm.t * dm.d * dm.ff,
    )[0]


def proj_back_body(dm, layer, *refs):
    nc = dm.nc
    meta, ga, own = refs[:3]
    pieces = refs[3 : 3 + nc]
    acc, dob, blocks, own_buf, piece_buf, sems = refs[3 + nc :]
    c, f = lax.axis_index("ctx"), lax.axis_index("fsdp")
    weight = Pieces(dm, layer, own, pieces, own_buf, piece_buf, sems, lambda j: (c ^ j) >= dm.nq)
    weight.start()
    cols_back(dm, f, c, weight, ga, dm.nq, nc, acc, dob)
    for j in range(nc):
        blocks[j] = take_heads(dm, dob, 0, c ^ j)


def proj_back_section(k, layer, ga, own, pieces, meta):
    dm = k.dm
    td, shape = (dm.t, dm.d), (dm.nc, dm.t, dm.w)
    _, bufs = k.section(
        functools.partial(proj_back_body, dm, layer),
        [(meta, "s"), (ga, "v"), (own, "a")] + [(p, "a") for p in pieces],
        [],
        [("acc", pltpu.VMEM(td, F32)), pltpu.VMEM(td, BF16), pltpu.VMEM(shape, BF16)]
        + piece_scratch(dm, (dm.pr, dm.d)),
        2 * dm.t * dm.d * dm.d,
    )
    blocks = send_blocks(dm, bufs[2], shape)
    k.start([blocks])
    return blocks


def qkv_back_body(dm, layer, *refs):
    nc = dm.nc
    meta, dmid, h, small, own, blocks = refs[:6]
    pieces = refs[6 : 6 + nc]
    dh, low, dqkv, sum_dqkv, g_gain, g_shift = refs[6 + nc : 12 + nc]
    acc, dn, own_buf, piece_buf, sems = refs[12 + nc :]
    blocks = [blocks.at[j] for j in range(nc)]
    c, f = lax.axis_index("ctx"), lax.axis_index("fsdp")
    weight = Pieces(dm, layer, own, pieces, own_buf, piece_buf, sems, lambda j: (c ^ j) < dm.nq)
    weight.start()
    for third in range(3):
        put_heads(dm, dqkv, third * dm.d, blocks, third * dm.w, c)
    sum_dqkv[...] = col_sum(dqkv[...])
    cols_back(dm, f, c, weight, dqkv, 0, dm.nq, acc, dn)
    dv, g_gain[...], g_shift[...] = norm_back(
        h[...].astype(F32), small_vec(dm, small, "g1" + str(layer)), dn[...]
    )
    total = dmid[...] + dv
    dh[...] = total
    low[...] = total.astype(BF16)


def qkv_back_section(k, layer, dmid, h, small, own, blocks, pieces, meta):
    dm = k.dm
    td, vec = (dm.t, dm.d), sds((1, dm.d), F32)
    return k.section(
        functools.partial(qkv_back_body, dm, layer),
        [(meta, "s"), (dmid, "v"), (h, "v"), (small, "v"), (own, "a"), (blocks, "v")]
        + [(p, "a") for p in pieces],
        [sds(td, F32), sds(td, BF16), sds((dm.t, 3 * dm.d), BF16), sds((1, 3 * dm.d), F32), vec, vec],
        [("acc", pltpu.VMEM(td, F32)), ("dn", pltpu.VMEM(td, F32))] + piece_scratch(dm, (dm.pr, 3 * dm.d)),
        2 * dm.t * dm.d * 3 * dm.d,
    )[0]


def sum_body(indices, *refs):
    n = len(indices)
    out, bufs, sems = refs[n], refs[n + 1 : 2 * n + 1], refs[2 * n + 1]
    copies = [
        pltpu.make_async_copy(at_of(ref, index), buf, sems.at[at])
        for at, (ref, index, buf) in enumerate(zip(refs, indices, bufs))
    ]
    for copy in copies:
        copy.start()
    for copy in copies:
        copy.wait()
    total = bufs[0][...].astype(F32)
    for buf in bufs[1:]:
        total = total + buf[...].astype(F32)
    out[...] = total.astype(out.dtype)


def sum_section(k, terms, shape, dtype=BF16, parts=None):
    bufs = [
        ("sum" + str((at, shape, dtype)), pltpu.VMEM(shape, dtype)) for at in range(len(terms))
    ]
    return k.section(
        functools.partial(sum_body, [index for _, index in terms]),
        [(src, "a") for src, _ in terms],
        [sds(shape, dtype)],
        bufs + [("sum" + str(len(terms)), pltpu.SemaphoreType.DMA((len(terms),)))],
        0,
    )[0][0]


def pack_body(dm, *refs):
    for n, name in enumerate(vector_names()):
        at, size = small_offsets(dm)[0][name]
        layer, which = n // len(SMALL), n % len(SMALL)
        if layer == LAYERS:
            layer, which = 0, len(SMALL) + which
        refs[-1][:, at : at + size] = refs[which][layer : layer + 1, :].astype(F32)


def small_body(dm, packed, others, out):
    f = lax.axis_index("fsdp")
    out[pl.ds(f, 1), :] = packed[...]
    for s in range(1, dm.nf):
        out[pl.ds(ring(dm, f, s), 1), :] = others[s - 1]


def collect_body(dm, *refs):
    names, (table, _) = vector_names(), small_offsets(dm)
    for name, ref in zip(names, refs):
        at, size = table[name]
        for g in range(dm.nf):
            refs[-1][g, :, at : at + size] = ref[:, g * size : (g + 1) * size]


def grad_body(dm, kind, shards, more, *refs):
    c, f = lax.axis_index("ctx"), lax.axis_index("fsdp")
    out, xt = refs[-2:]
    pairs = [refs[n : n + 2] for n in range(0, len(refs) - 2, 2)]
    lefts = pairs[: len(pairs) // 2]
    for n, pair in enumerate([] if more else lefts):
        depth = pair[0].shape[1]
        for half, ref in enumerate(pair):
            for at in range(0, depth, dm.pc):
                xt[n * depth + at : n * depth + at + dm.pc, half * dm.t : (half + 1) * dm.t] = ref[
                    :, at : at + dm.pc
                ].T
    rights = pairs[len(pairs) // 2 :]

    def fill(t, row_base, row_step, pair, col):
        cols = pl.ds(mult(col * dm.pc, dm.pc), dm.pc)
        dy = jnp.concatenate([pair[0][:, cols], pair[1][:, cols]], axis=0)
        for s in shards:
            at = mult(row_base + ring(dm, f, s) * row_step, dm.pr)
            out[t, s] = nn(xt[pl.ds(at, dm.pr), :], dy).astype(BF16)

    for t in reversed(range(dm.nc // 2)):
        i = c ^ (2 * t)
        if kind == "attn":
            pl.when(i < dm.nq)(lambda: fill(t, 0, dm.pr, rights[0], i))
            pl.when(i >= dm.nq)(lambda: fill(t, dm.d, dm.pr, rights[1], i - dm.nq))
        elif kind == "fc":
            fill(t, 0, dm.pr, rights[0], i)
        else:
            fill(t, (i // dm.ncs) * dm.pr, dm.ffn, rights[0], lax.rem(i, dm.ncs))


def grad_section(k, kind, lefts, rights, shards=None, out=None):
    dm = k.dm
    if kind != "attn":
        pairs = [lefts[0], rights[0]]
        if kind == "out":
            made = k.load_all([(value(v), name) for pair in pairs for v, name in zip(pair, ("own", "twin"))])
            lefts, rights = [made[:2]], [made[2:]]
        else:
            made = k.load_all([(value(pair[1]), "twin") for pair in pairs])
            lefts, rights = [(pairs[0][0], made[0])], [(pairs[1][0], made[1])]
    made = k.section(
        functools.partial(grad_body, dm, kind, shards or range(dm.nf), out is not None),
        [(a, "v") for pair in lefts + rights for a in pair] + ([(out, "v")] if out is not None else []),
        [] if out is not None else [sds((dm.nc // 2, dm.nf, dm.pr, dm.pc), BF16)],
        [("xt", pltpu.VMEM((dm.ff, 2 * dm.t), BF16))],
        2 * dm.t * dm.d * dm.ff,
    )[0]
    return out if out is not None else made[0]


def place_body(dm, *refs):
    nc = dm.nc
    jobs = [(layer, kind) for kind in ("out", "fc", "attn") for layer in reversed(range(LAYERS))]
    pieces = {job: refs[n * nc : (n + 1) * nc] for n, job in enumerate(jobs)}
    vector = refs[len(jobs) * nc]
    qkv, proj, fc, out = refs[len(jobs) * nc + 1 : len(jobs) * nc + 5]
    small = refs[len(jobs) * nc + 5 : -5]
    loads, wide, tall, load_sems, sems = refs[-5:]
    c = lax.axis_index("ctx")

    def fetch(n):
        return [
            pltpu.make_async_copy(pieces[jobs[n]][j], loads.at[n % 2, j], load_sems.at[n % 2, j])
            for j in range(nc)
        ]

    def store(n):
        layer, kind = jobs[n]
        buf, sem = (tall if kind == "out" else wide).at[n % 2], sems.at[n % 2]
        if kind == "attn":
            return [
                pltpu.make_async_copy(buf.at[:, pl.ds(0, 3 * dm.d)], qkv.at[layer], sem.at[0]),
                pltpu.make_async_copy(buf.at[:, pl.ds(3 * dm.d, dm.d)], proj.at[layer], sem.at[1]),
            ]
        return [pltpu.make_async_copy(buf, (out if kind == "out" else fc).at[layer], sem.at[0])]

    for copy in fetch(0):
        copy.start()
    for n, name in enumerate(vector_names()):
        at, size = small_offsets(dm)[0][name]
        row, ref = (n // len(SMALL), small[n % len(SMALL)])
        if row == LAYERS:
            row, ref = 0, small[len(SMALL) + n % len(SMALL)]
        ref[row : row + 1, :] = vector[:, at : at + size]
    for n in range(len(jobs)):
        if n + 1 < len(jobs):
            for copy in fetch(n + 1):
                copy.start()
        if n >= 2:
            for copy in store(n - 2):
                copy.wait()
        for copy in fetch(n):
            copy.wait()
        for j in range(nc):
            i = c ^ j
            v = loads[n % 2, j].astype(F32)
            if jobs[n][1] == "out":
                rows = pl.ds(mult((i // dm.ncs) * dm.pr, dm.pr), dm.pr)
                tall[n % 2, rows, pl.ds(mult(lax.rem(i, dm.ncs) * dm.pc, dm.pc), dm.pc)] = v
            else:
                wide[n % 2, :, pl.ds(mult(i * dm.pc, dm.pc), dm.pc)] = v
        for copy in store(n):
            copy.start()
    for n in (len(jobs) - 2, len(jobs) - 1):
        for copy in store(n):
            copy.wait()


def place_call(dm, done, vector):
    names = [k + str(layer) for k in ("o", "c", "a") for layer in reversed(range(LAYERS))]
    pieces = [p for name in names for p in done[name]]
    shapes = [(dm.pr, 3 * dm.d), (dm.pr, dm.d), (dm.pr, dm.ff), (dm.ffn, dm.d)]
    table = small_offsets(dm)[0]
    vectors = [(LAYERS, table[name + "0"][1]) for name, _ in SMALL] + [(1, dm.pr)] * 2
    return pl.pallas_call(
        functools.partial(place_body, dm),
        out_shape=[sds((LAYERS,) + shape, F32) for shape in shapes] + [sds(v, F32) for v in vectors],
        in_specs=[pl.BlockSpec(memory_space=pl.ANY)] * len(pieces) + [pl.BlockSpec(memory_space=pltpu.VMEM)],
        out_specs=[pl.BlockSpec(memory_space=pl.ANY)] * len(shapes)
        + [pl.BlockSpec(memory_space=pltpu.VMEM)] * len(vectors),
        scratch_shapes=[
            pltpu.VMEM((2, dm.nc, dm.pr, dm.pc), BF16),
            pltpu.VMEM((2, dm.pr, dm.ff), F32),
            pltpu.VMEM((2, dm.ffn, dm.d), F32),
            pltpu.SemaphoreType.DMA((2, dm.nc)),
            pltpu.SemaphoreType.DMA((2, 2)),
        ],
        compiler_params=pltpu.CompilerParams(vmem_limit_bytes=VMEM_BYTES),
    )(*pieces, vector)


def plane_bits(nc):
    bits = []
    bit = 2
    while bit < nc:
        bits.append(bit)
        bit *= 2
    return bits


def moving(moves):
    return lambda k: k.start(moves)


def spread(dm, first):
    bits = plane_bits(dm.nc)
    held = {0: first}
    if len(bits) == 2:
        one, two = bits
        held.update({bit: whole(first, ("ctx", bit)) for bit in (one, two, 1)})
        yield moving([held[one], held[two], held[1]])
        lead = (slice(None),) * (len(first.shape) - 2)
        cut = first.shape[-2] // 2
        low, high = lead + (pl.ds(0, cut),), lead + (pl.ds(cut, cut),)
        far = Move(
            first.shape, first.dtype,
            [([(None, held[two], low)], ("ctx", one), low), ([(None, held[one], high)], ("ctx", two), high)],
        )
        held[one ^ two] = far
        held.update({bit ^ 1: whole(held[bit], ("ctx", 1)) for bit in bits})
        yield moving([far, held[one ^ 1], held[two ^ 1]])
        held[one ^ two ^ 1] = whole(far, ("ctx", 1))
        yield moving([held[one ^ two ^ 1]])
    else:
        for bit in bits + [1]:
            new = {j ^ bit: whole(v, ("ctx", bit)) for j, v in held.items()}
            yield moving(list(new.values()))
            held.update(new)
    return [held[j] for j in range(dm.nc)]


def gather(dm, source):
    others = Move(
        (dm.nf - 1, dm.pr, dm.pc), BF16,
        [(source, ("fsdp", s), (s - 1,)) for s in range(1, dm.nf)],
    )
    yield moving([others])
    return (yield from spread(dm, others))


def shift_order(dm):
    return sorted(range(1, dm.nf), key=lambda s: min(s, dm.nf - s))


def gather_split(dm, source):
    bits = plane_bits(dm.nc)
    if len(bits) != 2:
        return (yield from gather(dm, source))
    order = shift_order(dm)
    one, two = bits

    def line(parts):
        made = {}
        for s in order:
            base = made[order[0]] if made else None
            made[s] = Move((dm.nf - 1, dm.pr, dm.pc), BF16, parts(s), base)
        return made

    def along(prev, route):
        return line(lambda s: [([(None, prev[s], (s - 1,))], route, (s - 1,))])

    z = line(lambda s: [(source, ("fsdp", s), (s - 1,))])
    yield moving([z[s] for s in order])
    x, y, core = along(z, ("ctx", one)), along(z, ("ctx", two)), along(z, ("ctx", 1))
    for s in order:
        yield moving([x[s], y[s], core[s]])
    cut = dm.pr // 2

    def corner(s):
        low, high = (s - 1, pl.ds(0, cut)), (s - 1, pl.ds(cut, cut))
        return [([(None, y[s], low)], ("ctx", one), low), ([(None, x[s], high)], ("ctx", two), high)]

    far = line(corner)
    x_, y_ = along(x, ("ctx", 1)), along(y, ("ctx", 1))
    for s in order:
        yield moving([far[s], x_[s], y_[s]])
    far_ = along(far, ("ctx", 1))
    yield moving([far_[s] for s in order])
    held = {0: z, 1: core, one: x, one ^ 1: x_, two: y, two ^ 1: y_, one ^ two: far, one ^ two ^ 1: far_}
    return [held[j][order[0]] for j in range(dm.nc)]


def plane_sum(dm, terms, first_shard, shards):
    bits = plane_bits(dm.nc)
    if len(bits) == 2:
        one, two = bits
        cut = dm.pr // 2
        shape = (shards, cut, dm.pc)

        def part(t, first):
            return (t, pl.ds(first_shard, shards), pl.ds(first, cut))

        def send(t, first, bit):
            return Move(shape, BF16, [([(None, terms, part(t, first))], ("ctx", bit), None)])

        far_x, own_x = send(3, 0, one), send(1, 0, one)
        far_y, own_y = send(3, cut, two), send(2, cut, two)
        yield moving([far_x, far_y, own_x, own_y])
        near = []

        def second(k):
            x = sum_section(k, [(terms, part(1, cut)), (far_y, None)], shape)
            near.append(whole(x, ("ctx", one)))
            k.start(near[:1])
            y = sum_section(k, [(terms, part(2, 0)), (far_x, None)], shape)
            near.append(whole(y, ("ctx", two)))
            k.start(near[1:])

        yield second
        return [
            [(terms, part(0, 0)), (own_x, None), (near[1], None)],
            [(terms, part(0, cut)), (near[0], None), (own_y, None)],
        ]
    at, index = terms, ()
    count = dm.nc // 2
    for n, _ in enumerate(bits):
        count //= 2
        shape = (count, dm.nf, dm.pr, dm.pc)
        away = Move(shape, BF16, [([(None, at, (pl.ds(count, count),))], ("ctx", bits[-1 - n]), None)])
        yield moving([away])
        if count > 1:
            made = []

            def add(k):
                made.append(sum_section(k, [(at, (pl.ds(0, count),)), (away, None)], shape))

            yield add
            at = made[0]
    return [[(at, (0,)), (away, (0,))]]


def reduce(dm, terms, split=False):
    split = split and len(plane_bits(dm.nc)) == 2
    groups = [(s, 1) for s in shift_order(dm) + [0]] if split else [(0, dm.nf)]
    sums = [plane_sum(dm, terms, *group) for group in groups]
    parts = [None] * len(groups)

    def stage(n):
        try:
            return next(sums[n])
        except StopIteration as stop:
            parts[n] = stop.value
            return None

    own, others = {}, []

    def along(n):
        first, count = groups[n]

        def put(k):
            rows = dm.pr // len(parts[n])
            for at, part in enumerate(parts[n]):
                total = sum_section(k, part, (count, rows, dm.pc))
                sent = [s for s in range(first, first + count) if s > 0]
                if first == 0:
                    own[at] = total
                if sent:
                    move = Move(
                        (len(sent), rows, dm.pc), BF16,
                        [
                            ([(None, total, (s - first,))], ("fsdp", dm.nf - s), (m,))
                            for m, s in enumerate(sent)
                        ],
                    )
                    others.append((at, move, len(sent)))
                    k.start([move])

        return put

    for n in range(len(groups)):
        yield stage(n)
    if split:
        for n in range(len(groups) + 1):
            if n < len(groups):
                yield stage(n)
            if n > 0:
                stage(n - 1)
                yield along(n - 1)
    else:
        more = stage(0)
        while more is not None:
            yield more
            more = stage(0)
        yield along(0)
    mine = []

    def join(k):
        rows = dm.pr // len(own)

        def body(*refs):
            for n in range(len(own)):
                refs[-1][n * rows : (n + 1) * rows, :] = refs[n][...]

        sums = [
            sum_section(
                k,
                [(own[at], (0,))] + [(m, (i,)) for to, m, size in others if to == at for i in range(size)],
                (rows, dm.pc),
            )
            for at in range(len(own))
        ]
        mine.append(k.section(body, [(v, "v") for v in sums], [sds((dm.pr, dm.pc), BF16)], [], 0)[0][0])

    return (yield from spread_later(dm, mine, join))


def spread_later(dm, mine, join):
    inner = None

    def first(k):
        nonlocal inner
        join(k)
        inner = spread(dm, mine[0])
        next(inner)(k)

    yield first
    return (yield from inner)


def reduce_small(dm, total):
    n = total.shape[-1]
    row = lambda s: (lambda: (ring(dm, lax.axis_index("fsdp"), s),))
    bit = 1
    state = [total]
    while bit < dm.nc:

        def step(k):
            other = whole(state[-1], ("ctx", bit))
            k.start([other])
            state.append(other)

        def add(k):
            other = state.pop()
            state.append(sum_section(k, [(state[-1], None), (other, None)], total.shape, F32))

        yield step
        yield add
        bit *= 2
    total = state[-1]
    others = Move(
        (dm.nf - 1, 1, n), F32,
        [([(None, total, row(s))], ("fsdp", dm.nf - s), (s - 1,)) for s in range(1, dm.nf)],
    )
    yield moving([others])
    made = []

    def last(k):
        terms = [(total, row(0))] + [(others, (s,)) for s in range(dm.nf - 1)]
        made.append(sum_section(k, terms, (1, n), F32))

    yield last
    return made[0]


class Flow:
    def __init__(self, dm):
        self.dm, self.live, self.done = dm, {}, {}
        self.ids = itertools.count()

    def kernel(self, *names):
        k = Kernel(self.dm, self.ids)
        self.go(k, *names)
        return k

    def add(self, name, transfer):
        self.live[name] = transfer

    def go(self, k, *names):
        for name in names:
            if name in self.live:
                try:
                    next(self.live[name])(k)
                except StopIteration as stop:
                    self.done[name] = stop.value
                    del self.live[name]

    def finish(self, k, name):
        while name in self.live:
            self.go(k, name)
        return self.done[name]


def local(acts, cotangent, pair_slots, segments, *tensors):
    (
        attn_gain, attn_shift, qkv_weight, qkv_bias, proj_weight, proj_bias, mlp_gain, mlp_shift,
        fc_weight, fc_bias, out_weight, out_bias, final_gain, final_shift,
    ) = tensors
    nf, nc = lax.axis_size("fsdp"), lax.axis_size("ctx")
    dm = dims_of(acts, fc_weight, nf, nc)
    c, f = lax.axis_index("ctx"), lax.axis_index("fsdp")
    small_size = small_offsets(dm)[1]

    seg = segments[0]
    cut_one = jnp.sum((seg == 0).astype(jnp.int32))
    cut_two = cut_one + jnp.sum((seg == 1).astype(jnp.int32))
    index = jnp.arange(nc, dtype=jnp.int32)
    others = jnp.bitwise_xor(c, index)
    lows = jnp.sum(jnp.where(others[:, None] == index[None, :], pair_slots[None, :], 0), axis=1)
    slots = jnp.sum(jnp.where(lows[None, :] == index[:, None], index[None, :], 0), axis=1)
    meta = jnp.concatenate([jnp.stack([c, f, cut_one, cut_two]).astype(jnp.int32), lows, slots])

    def source(kind, layer):
        def cols(first, last):
            at = jnp.clip(lax.axis_index("ctx"), first, last - 1) - first
            return (layer, pl.ds(0, dm.pr), pl.ds(mult(at * dm.pc, dm.pc), dm.pc))

        def place():
            at = lax.axis_index("ctx")
            row, col = (at // dm.ncs) * dm.pr, lax.rem(at, dm.ncs) * dm.pc
            return (layer, pl.ds(mult(row, dm.pr), dm.pr), pl.ds(mult(col, dm.pc), dm.pc))

        if kind == "attn":
            return [
                (lambda: lax.axis_index("ctx") < dm.nq, qkv_weight, lambda: cols(0, dm.nq)),
                (lambda: lax.axis_index("ctx") >= dm.nq, proj_weight, lambda: cols(dm.nq, nc)),
            ]
        if kind == "fc":
            return [(None, fc_weight, lambda: cols(0, nc))]
        return [(None, out_weight, place)]

    def other_core(v):
        return whole(v, ("ctx", 1))

    flow = Flow(dm)
    for layer in range(LAYERS):
        for kind, name in (("attn", "A"), ("fc", "C"), ("out", "O")):
            how = gather_split if layer == 0 and name == "A" else gather
            flow.add(name + str(layer), how(dm, source(kind, layer)))

    k = flow.kernel()
    flow.go(k, "A0")
    per_layer = (attn_gain, attn_shift, qkv_bias, proj_bias, mlp_gain, mlp_shift, fc_bias, out_bias)
    _, (packed,) = k.section(
        functools.partial(pack_body, dm),
        [(v, "v") for v in per_layer] + [(v.reshape(1, -1), "v") for v in (final_gain, final_shift)],
        [],
        [pltpu.VMEM((1, small_size), F32)],
        0,
    )
    small_move = Move(
        (nf - 1, 1, small_size), F32,
        [([(None, packed, None)], ("fsdp", s), (s - 1,)) for s in range(1, nf)],
    )
    k.start([small_move])
    flow.go(k, "A0", "A0", "A0", "C0", "A0", "A0", "A0")
    (small,) = k.section(
        functools.partial(small_body, dm),
        [(packed, "v"), (small_move, "v")],
        [sds((nf, small_size), F32)],
        [],
        0,
    )[0]
    h = acts[0]
    first = flow.finish(k, "A0")
    flow.go(k, "O0")
    n1, blocks = qkv_section(k, 0, h, small, qkv_weight, first, meta)
    flow.go(k, "A1")
    twin = [other_core(n1)]
    k.start(twin)
    k.load(blocks)
    flow.go(k, "C0", "O0")
    vectors, kept = {}, []
    for layer in range(LAYERS):
        tag, nxt = str(layer), str(layer + 1)
        last = layer + 1 == LAYERS
        saved, heads = attend_section(k, blocks, meta)
        if last:
            flow.go(k, "C" + tag, "O" + tag)
        else:
            flow.go(k, "C" + tag, "O" + tag, "C" + tag)
            k.run()
            k = flow.kernel("A" + nxt, "O" + tag, "C" + nxt)
        attn = flow.done["A" + tag]
        ob, mid, n2 = proj_section(k, layer, h, small, proj_weight, heads, attn, meta)
        if last:
            flow.go(k, "O" + tag)
        twin += [other_core(ob), other_core(n2)]
        k.start(twin[1:])
        u, act = fc_section(k, layer, n2, small, fc_weight, flow.finish(k, "C" + tag), meta)
        twin.append(other_core(act))
        k.start(twin[3:])
        if not last:
            flow.go(k, "A" + nxt, "O" + nxt)
        nxt_h = out_section(k, layer, mid, act, small, out_weight, flow.finish(k, "O" + tag), meta)
        kept.append((h, n1, saved, ob, mid, n2, u, act, twin))
        h = nxt_h
        if not last:
            flow.go(k, "C" + nxt)
            n1, blocks = qkv_section(k, layer + 1, h, small, qkv_weight, flow.finish(k, "A" + nxt), meta)
            twin = [other_core(n1)]
            k.start(twin)
            flow.go(k, "C" + nxt, "O" + nxt)

    weights = flow.done
    result, dh, gm, vectors["gf"], vectors["sf"] = top_section(k, h, cotangent[0], small)

    for layer in reversed(range(LAYERS)):
        tag, nxt = str(layer), str(layer + 1)
        o_, a_, k_ = "o" + nxt, "a" + nxt, "c" + nxt
        o, a, ck = "o" + tag, "a" + tag, "c" + tag
        h, n1, saved, ob, mid, n2, u, act, (n1_, ob_, n2_, act_) = kept[layer]
        gm_ = other_core(gm)
        k.start([gm_])
        du, vectors["bo" + tag], vectors["bf" + tag] = out_back_section(
            k, layer, gm, u, out_weight, weights["O" + tag], meta
        )
        du_ = other_core(du)
        k.start([du_])
        flow.go(k, o_)
        k.run()

        k = flow.kernel(a_)
        flow.add(o, reduce(dm, grad_section(k, "out", [(act, act_)], [(gm, gm_)])))
        flow.go(k, o, k_, o_)
        dmid, ga, vectors["bp" + tag], vectors["g2" + tag], vectors["s2" + tag] = fc_back_section(
            k, layer, du, dh, mid, small, fc_weight, weights["C" + tag], meta
        )
        ga_ = other_core(ga)
        k.start([ga_])
        grads = proj_back_section(k, layer, ga, proj_weight, weights["A" + tag], meta)
        flow.go(k, a_, k_, o_)
        flow.add(ck, reduce(dm, grad_section(k, "fc", [(n2, n2_)], [(du, du_)])))
        flow.go(k, ck, o)
        if dm.rows * dm.nc > 2048 * 8:
            k.run()
            k = flow.kernel()
        blocks = attend_back_section(k, saved, grads, meta)
        flow.go(k, a_, k_)
        k.run()

        k = flow.kernel(a_)
        dh, gm, dqkv, vectors["bq" + tag], vectors["g1" + tag], vectors["s1" + tag] = qkv_back_section(
            k, layer, dmid, h, small, qkv_weight, blocks, weights["A" + tag], meta
        )
        dqkv_ = other_core(dqkv)
        k.start([dqkv_])
        flow.go(k, a_, k_, ck, o)
        if layer == 0:
            shape = (nf, 1, small_size)
            rows = k.section(
                functools.partial(collect_body, dm),
                [(vectors[name], "v") for name in vector_names()],
                [sds(shape, F32)],
                [],
                0,
            )[0][0]
            flow.add("small", reduce_small(dm, rows))
            flow.go(k, "small")
        pairs = [(n1, n1_), (ob, ob_)], [(dqkv, dqkv_), (ga, ga_)]
        if layer == 0 and len(plane_bits(nc)) == 2:
            order = shift_order(dm) + [0]
            terms = grad_section(k, "attn", *pairs, order[:1])
            flow.add(a, reduce(dm, terms, True))
            flow.go(k, a)
            for s in order[1:]:
                grad_section(k, "attn", *pairs, [s], terms)
                flow.go(k, a)
            flow.go(k, ck)
        else:
            flow.add(a, reduce(dm, grad_section(k, "attn", *pairs)))
            flow.go(k, a)

    flow.go(k, "o0", "a0", "small", "small", "a0", "o0", "a0", "c0", "small", "small", "a0", "o0", "a0", "c0")
    flow.go(k, "small", "a0", "a0", "c0", "a0", "small", "small")
    for name in ("a1", "c1", "o1", "c0", "o0", "a0"):
        flow.finish(k, name)
    mine = flow.finish(k, "small")
    k.run()
    done = {name: [value(v) for v in flow.done[name]] for name in ("o0", "c0", "a0", "o1", "c1", "a1")}
    grads = place_call(dm, done, value(mine))
    qkv_grad, proj_grad, fc_grad, out_grad, g1, s1, bq, bp, g2, s2, bf, bo, gf, sf = grads
    return (
        value(result)[None], value(gm)[None], g1, s1, qkv_grad, bq, proj_grad, bp, g2, s2, fc_grad, bf,
        out_grad, bo, gf.reshape(-1), sf.reshape(-1),
    )


def solution(mesh):
    row = P("fsdp", "ctx", None)
    vec, mat = P(None, "fsdp"), P(None, "fsdp", None)
    tensors = (vec, vec, mat, vec, mat, vec, vec, vec, mat, vec, mat, vec, P("fsdp"), P("fsdp"))
    return jax.shard_map(
        local,
        mesh=mesh,
        in_specs=(row, row, P(), P("fsdp", None)) + tensors,
        out_specs=(row, row) + tensors,
        check_vma=False,
    )
```
